32 devices in a mesh: replica: 2 (over x), fsdp: 16 (over z, y, core).
Axes of the slice: x: 2, y: 2, z: 4, core: 2. Of those that a mesh axis runs over, the one named last changes fastest.
Arguments:
- tokens: bfloat16 [32768, 768], P(('replica', 'fsdp')), may hold values from -6 to 6
- lengths: int32 [64, 8], P(('replica', 'fsdp')), may hold values from 1 to 128, 512 in all within a row
- w_qkv: bfloat16 [768, 2304], P('fsdp'), may hold values from -0.21875 to 0.21875
- bias_qv: bfloat16 [1536], P('fsdp'), may hold values from -1.75 to 1.75
- w_out: bfloat16 [768, 768], P('fsdp'), may hold values from -0.875 to 0.875
- bias_out: bfloat16 [768], P('fsdp'), may hold values from -1.75 to 1.75
- gain_one: bfloat16 [768], P('fsdp'), may hold values from 0.5 to 1.5
- shift_one: bfloat16 [768], P('fsdp'), may hold values from -1.75 to 1.75
- w_up: bfloat16 [768, 3072], P('fsdp'), may hold values from -0.21875 to 0.21875
- bias_up: bfloat16 [3072], P('fsdp'), may hold values from -1.75 to 1.75
- w_down: bfloat16 [3072, 768], P('fsdp'), may hold values from -0.15625 to 0.15625
- bias_down: bfloat16 [768], P('fsdp'), may hold values from -1.75 to 1.75
- gain_two: bfloat16 [768], P('fsdp'), may hold values from 0.5 to 1.5
- shift_two: bfloat16 [768], P('fsdp'), may hold values from -1.75 to 1.75
- cotangent: bfloat16 [32768, 768], P(('replica', 'fsdp')), may hold values from -6 to 6
Outputs:
- layer_out: bfloat16 [32768, 768], P(('replica', 'fsdp'))
- input_grad: float32 [32768, 768], P(('replica', 'fsdp'))
- pooled: float32 [64, 8, 768], replicated
- grad_w_qkv: float32 [768, 2304], P('fsdp')
- grad_bias_qv: float32 [1536], P('fsdp')
- grad_w_out: float32 [768, 768], P('fsdp')
- grad_bias_out: float32 [768], P('fsdp')
- grad_gain_one: float32 [768], P('fsdp')
- grad_shift_one: float32 [768], P('fsdp')
- grad_w_up: float32 [768, 3072], P('fsdp')
- grad_bias_up: float32 [3072], P('fsdp')
- grad_w_down: float32 [3072, 768], P('fsdp')
- grad_bias_down: float32 [768], P('fsdp')
- grad_gain_two: float32 [768], P('fsdp')
- grad_shift_two: float32 [768], P('fsdp')
The draws below stay inside these ranges and needn't reach their ends.
Inputs may be any that keep to these rules, and one draw needn't show every extreme that they name: The sentence lengths of each row sum to 512, and each row has a sentence of exactly 128 tokens.
All inputs are finite; a program needn't handle non-finite values.
Results may differ from the reference program's by a relative error of at most 0.015.
Values may be sent and summed in bfloat16 or wider, within the bound.
No kernel may reach another device: no remote copies, remote signals or barrier semaphores. Data moves between devices by JAX's collectives and lax.ppermute only.
A program may use at most 192 MiB of HBM per device.

```python
import math
import jax
import jax.numpy as jnp
import numpy as np
from jax import lax

D = 768
H = 12
HD = 64
FF = 3072
SEQ = 512
SEGS = 8
MOST_LEN = 128
ROWS = 64
TOKENS = 32768


def level_of(rng, shape, cuts, low, high):
    def one(dim, blocks):
        steps = jax.random.uniform(jax.random.fold_in(jax.random.fold_in(rng, 6), dim), (blocks,), jnp.float32, low / len(cuts), high / len(cuts))
        return jnp.repeat(jnp.exp(steps), shape[dim] // blocks).reshape((-1,) + (1,) * (len(shape) - dim - 1))

    factor_of = one(*cuts[0])
    for cut in cuts[1:]:
        factor_of = factor_of * one(*cut)
    return factor_of


def profile(amount, total, reach, slope):
    loads = [(1 << 20) // math.isqrt(grade ** slope) + 1 for grade in range(2, amount + 1)]
    spare, holding = total - reach - (amount - 1), [1] * (amount - 1)
    while spare > 0:
        free = [i for i in range(amount - 1) if holding[i] < reach]
        mass, left = sum([loads[i] for i in free]), spare
        for i in free:
            extra = min(reach - holding[i], max(1, left * loads[i] // mass), spare)
            holding[i] = holding[i] + extra
            spare = spare - extra
    return np.array([reach] + holding)


def ragged(rng, amount, total, most, lean):
    if amount == 2:
        one = jax.random.randint(rng, (), max(1, total - most), min(most, total - 1) + 1)
        return jnp.stack([one, total - one])
    sizes = jnp.asarray(profile(amount, total, most, lean), jnp.int32)
    pairs = (amount - 1) // 2
    donor, sink = sizes[1:1 + 2 * pairs:2], sizes[2:2 + 2 * pairs:2]
    margin = jnp.minimum(donor - 1, most - sink)
    passed = jax.random.randint(jax.random.fold_in(rng, 1), (pairs,), 0, 1 << 20) % (margin + 1)
    sizes = sizes.at[1:1 + 2 * pairs:2].set(donor - passed).at[2:2 + 2 * pairs:2].set(sink + passed)
    return sizes[jax.random.permutation(jax.random.fold_in(rng, 2), amount)]


def gaussian(rng, shape, spread, limit, shards=(), kind=jnp.bfloat16):
    factor_of = level_of(rng, shape, shards, -0.22, 0.18) if shards else 1.0
    values = jax.random.normal(rng, shape, jnp.float32) * spread * factor_of
    return jnp.minimum(jnp.maximum(values, -limit), limit).astype(kind)


def setup_inputs(seed: int = 0) -> dict:
    streams_of = jax.random.split(jax.random.key(seed), 16)
    return {
        "tokens": gaussian(streams_of[0], (TOKENS, D), 1.0, 6.0, ((0, 32),)),
        "lengths": jax.vmap(lambda own: ragged(own, SEGS, SEQ, MOST_LEN, 1))(jax.random.split(streams_of[1], ROWS)).reshape((ROWS, SEGS)).astype(jnp.int32),
        "w_qkv": gaussian(streams_of[2], (D, 3 * D), D ** -0.5, 0.21875, ((0, 16),)),
        "bias_qv": gaussian(streams_of[3], (2 * D,), 0.3, 1.75, ((0, 16),)),
        "w_out": gaussian(streams_of[4], (D, D), (D // 16) ** -0.5, 0.875, ((0, 16),)),
        "bias_out": gaussian(streams_of[5], (D,), 0.3, 1.75, ((0, 16),)),
        "gain_one": jnp.clip(1.0 + 0.1 * jax.random.normal(streams_of[6], (D,), jnp.float32), 0.5, 1.5).astype(jnp.bfloat16),
        "shift_one": gaussian(streams_of[7], (D,), 0.3, 1.75, ((0, 16),)),
        "w_up": gaussian(streams_of[8], (D, FF), D ** -0.5, 0.21875, ((0, 16),)),
        "bias_up": gaussian(streams_of[9], (FF,), 0.3, 1.75, ((0, 16),)),
        "w_down": gaussian(streams_of[10], (FF, D), (FF // 2) ** -0.5, 0.15625, ((0, 16),)),
        "bias_down": gaussian(streams_of[11], (D,), 0.3, 1.75, ((0, 16),)),
        "gain_two": jnp.clip(1.0 + 0.1 * jax.random.normal(streams_of[12], (D,), jnp.float32), 0.5, 1.5).astype(jnp.bfloat16),
        "shift_two": gaussian(streams_of[13], (D,), 0.3, 1.75, ((0, 16),)),
        "cotangent": gaussian(streams_of[14], (TOKENS, D), 1.0, 6.0, ((0, 32),)),
    }


@jax.custom_vjp
def low(v):
    return lax.optimization_barrier(v.astype(jnp.bfloat16)).astype(jnp.float32)

@jax.custom_vjp
def low_back(v):
    return v

def low_keep(v):
    return (low(v), None)

def low_pass(kept, grad):
    return (grad,)

def back_keep(v):
    return (v, None)

def back_low(kept, grad):
    return (low(grad),)
low.defvjp(low_keep, low_pass)
low_back.defvjp(back_keep, back_low)
highest = lax.Precision.HIGHEST
epsilon = 1e-12
root_half = 0.7071067811865476
masked_score = -1e+30

def layer_norm(values, gain, shift):
    centered = values - lax.optimization_barrier(jnp.mean(values, axis=-1, keepdims=True))
    variance = lax.optimization_barrier(jnp.mean(centered * centered, axis=-1, keepdims=True))
    return centered * lax.rsqrt(variance + epsilon) * gain + shift

def gelu(values):
    return 0.5 * values * (1.0 + lax.erf(values * root_half))

def segment_ids(lengths):
    segment_ends = jnp.cumsum(lengths, axis=1)
    places = jnp.arange(SEQ, dtype=jnp.int32)
    return lax.optimization_barrier(jnp.sum((places[None, :, None] >= segment_ends[:, None, :]).astype(jnp.int32), axis=2))

def attend_row(inputs):
    row_block, segment = inputs
    queries = row_block[:, :D].reshape(SEQ, H, HD)
    key_rows = row_block[:, D:2 * D].reshape(SEQ, H, HD)
    value_rows = row_block[:, 2 * D:].reshape(SEQ, H, HD)
    scores = low_back(jnp.einsum('qhd,khd->hqk', queries, key_rows, precision=highest) * HD ** (-0.5))
    same_segment = segment[:, None] == segment[None, :]
    scores = jnp.where(same_segment[None], scores, masked_score)
    highest_score = lax.optimization_barrier(jnp.max(scores, axis=-1, keepdims=True))
    weights = jnp.exp(scores - highest_score)
    probabilities = weights / lax.optimization_barrier(jnp.sum(weights, axis=-1, keepdims=True))
    mixed = jnp.einsum('hqk,khd->qhd', low(probabilities), value_rows, precision=highest)
    return mixed.reshape(SEQ, D)

def forward_rows(inputs, segment_rows, params):
    w_qkv, bias_qv, w_out, bias_out, gain_one, shift_one, w_up, bias_up, w_down, bias_down, gain_two, shift_two = params
    row_count = inputs.shape[0] // SEQ
    bias_full = jnp.concatenate([bias_qv[:D], jnp.zeros((D,), jnp.float32), bias_qv[D:]])
    projected = low_back(low(jnp.dot(inputs, w_qkv, precision=highest) + bias_full))
    mixed = lax.map(jax.checkpoint(attend_row), (projected.reshape(row_count, SEQ, 3 * D), segment_rows))
    mixed = low_back(low(mixed.reshape(row_count * SEQ, D)))
    attended = low_back(jnp.dot(mixed, w_out, precision=highest) + bias_out)
    normed = layer_norm(inputs + attended, gain_one, shift_one)
    upper = low_back(jnp.dot(low(normed), w_up, precision=highest) + bias_up)
    active = low(gelu(upper))
    down = low_back(jnp.dot(active, w_down, precision=highest) + bias_down)
    return layer_norm(normed + down, gain_two, shift_two)

def reference(tokens, lengths, w_qkv, bias_qv, w_out, bias_out, gain_one, shift_one, w_up, bias_up, w_down, bias_down, gain_two, shift_two, cotangent):
    params = tuple((item.astype(jnp.float32) for item in (w_qkv, bias_qv, w_out, bias_out, gain_one, shift_one, w_up, bias_up, w_down, bias_down, gain_two, shift_two)))
    segments = segment_ids(lengths)
    group_rows = math.gcd(ROWS, max(1, 4096 // SEQ))
    group_count = ROWS // group_rows
    token_groups = tokens.astype(jnp.float32).reshape(group_count, group_rows * SEQ, D)
    cotangent_groups = cotangent.astype(jnp.float32).reshape(group_count, group_rows * SEQ, D)
    segment_groups = segments.reshape(group_count, group_rows, SEQ)

    def group_step(totals, slices):
        inputs, segment_rows, cotangent_rows = slices

        def run_rows(inputs_now, params_now):
            return forward_rows(inputs_now, segment_rows, params_now)
        result, pullback = jax.vjp(run_rows, inputs, params)
        grad_inputs, grad_params = pullback(cotangent_rows)
        totals = tuple((before + added for before, added in zip(totals, grad_params)))
        return (totals, (result.astype(jnp.bfloat16), grad_inputs))
    zeros_start = tuple((jnp.zeros(item.shape, jnp.float32) for item in params))
    totals, (outputs, input_grads) = lax.scan(group_step, zeros_start, (token_groups, segment_groups, cotangent_groups))
    layer_out = outputs.reshape(TOKENS, D)
    input_grad = input_grads.reshape(TOKENS, D)
    sentence_ids = (jnp.arange(ROWS, dtype=jnp.int32)[:, None] * SEGS + segments).reshape(TOKENS)
    sentence_sums = jax.ops.segment_sum(layer_out.astype(jnp.float32), sentence_ids, num_segments=ROWS * SEGS)
    pooled = sentence_sums.reshape(ROWS, SEGS, D) / lengths.astype(jnp.float32)[:, :, None]
    return (layer_out, input_grad, pooled, totals[0], totals[1], totals[2], totals[3], totals[4], totals[5], totals[6], totals[7], totals[8], totals[9], totals[10], totals[11])
```

```python
import functools

import jax
import jax.numpy as jnp
from jax import lax
from jax.experimental import pallas as pl
from jax.experimental.pallas import tpu as pltpu
from jax.sharding import PartitionSpec as P

D = 768
H = 12
HD = 64
FF = 3072
SEQ = 512
SEGS = 8
GROUPS = 3
GW = D // GROUPS
PAIRS = GW // 128
BLOCK = 128
BLOCKS = SEQ // BLOCK
WIDE = 3 * BLOCK

epsilon = 1e-12
root_half = 0.7071067811865476
masked_score = -1e30
pdf_scale = 0.3989422804014327

BF = jnp.bfloat16
F32 = jnp.float32
VMEM_LIMIT = 56 * 2**20


def dot(a, b):
    return jnp.dot(a, b, preferred_element_type=F32)


def dot_t(a, b):
    return lax.dot_general(a, b, (((1,), (1,)), ((), ())), preferred_element_type=F32)


def t_dot(a, b):
    return lax.dot_general(a, b, (((0,), (0,)), ((), ())), preferred_element_type=F32)


def window(qb):
    return max(0, (qb - 1) * BLOCK), min(SEQ, (qb + 2) * BLOCK)


def call(kernel, grid, in_specs, out_specs, out_shape, flops, nbytes, scratch=(), prefetch=0):
    return pl.pallas_call(
        kernel,
        grid_spec=pltpu.PrefetchScalarGridSpec(
            num_scalar_prefetch=prefetch,
            grid=grid,
            in_specs=in_specs,
            out_specs=out_specs,
            scratch_shapes=list(scratch),
        ),
        out_shape=out_shape,
        compiler_params=pltpu.CompilerParams(vmem_limit_bytes=VMEM_LIMIT),
        cost_estimate=pl.CostEstimate(flops=flops, bytes_accessed=nbytes, transcendentals=0),
    )


def shaped(shape, dtype):
    return jax.ShapeDtypeStruct(shape, dtype)


def whole(shape):
    return pl.BlockSpec(shape, lambda *_: (0,) * len(shape), pipeline_mode=pl.Buffered(1))


def segment_of(places, lengths_ref, row):
    total = jnp.int32(0)
    segment = jnp.zeros(places.shape, jnp.int32)
    for s in range(SEGS):
        total = total + lengths_ref[row, s]
        segment = segment + (places >= total).astype(jnp.int32)
    return segment


def attend_forward_kernel(
    lengths_ref, tok_ref, wq_ref, wk_ref, wv_ref, bias_ref, q_ref, k_ref, v_ref, p_ref, m_ref
):
    row = pl.program_id(0)
    tok = tok_ref[...]
    q_ref[...] = (dot(tok, wq_ref[...]) + bias_ref[0:1, :]).astype(BF) * jnp.asarray(0.125, BF)
    k_ref[...] = dot(tok, wk_ref[...]).astype(BF)
    v_ref[...] = (dot(tok, wv_ref[...]) + bias_ref[1:2, :]).astype(BF)
    low = lax.broadcasted_iota(jnp.int32, (1, 128), 1) < HD
    for qb in range(BLOCKS):
        lo, hi = window(qb)
        width = hi - lo
        rows = slice(qb * BLOCK, (qb + 1) * BLOCK)
        seg_q = segment_of(
            lax.broadcasted_iota(jnp.int32, (BLOCK, 1), 0) + qb * BLOCK, lengths_ref, row
        )
        seg_k = segment_of(
            lax.broadcasted_iota(jnp.int32, (1, width), 1) + lo, lengths_ref, row
        )
        mask = jnp.where(seg_q == seg_k, 0.0, masked_score)
        for pair in range(PAIRS):
            lanes = slice(pair * 128, (pair + 1) * 128)
            q2 = q_ref[rows, lanes]
            k2 = k_ref[lo:hi, lanes]
            v2 = v_ref[lo:hi, lanes]
            mixed = []
            for h in range(2):
                qh = jnp.where(low if h == 0 else ~low, q2, jnp.zeros_like(q2))
                s = dot_t(qh, k2) + mask
                w = jnp.exp(s - jnp.max(s, axis=-1, keepdims=True))
                p = (w * (1.0 / jnp.sum(w, axis=-1, keepdims=True))).astype(BF)
                p_ref[pair, qb, h * BLOCK : (h + 1) * BLOCK, :width] = p
                mixed.append(dot(p, v2))
            m_ref[rows, lanes] = jnp.where(low, mixed[0], mixed[1]).astype(BF)


def attend_forward(lengths, tokens, wq, wk, wv, bias):
    t = tokens.shape[0]
    rows = t // SEQ
    row_spec = pl.BlockSpec((SEQ, GW), lambda r, *_: (r, 0))
    p_shape = (rows * PAIRS, BLOCKS, 2 * BLOCK, WIDE)
    return call(
        attend_forward_kernel,
        (rows,),
        [
            pl.BlockSpec((SEQ, D), lambda r, *_: (r, 0)),
            whole((D, GW)),
            whole((D, GW)),
            whole((D, GW)),
            whole((2, GW)),
        ],
        [row_spec] * 3
        + [pl.BlockSpec((PAIRS,) + p_shape[1:], lambda r, *_: (r, 0, 0, 0)), row_spec],
        [shaped((t, GW), BF)] * 3 + [shaped(p_shape, BF), shaped((t, GW), BF)],
        flops=t * D * D * 2 * 4,
        nbytes=8 * 2**20,
        prefetch=1,
    )(lengths, tokens, wq, wk, wv, bias)


def attend_backward_kernel(
    datt_ref, wo_ref, q_ref, k_ref, v_ref, p_ref, m_ref, dp_ref, sums_ref, dk_acc, dv_acc
):
    low = lax.broadcasted_iota(jnp.int32, (1, 128), 1) < HD
    dmix = dot_t(datt_ref[...], wo_ref[...]).astype(BF)
    dk_acc[...] = jnp.zeros_like(dk_acc)
    dv_acc[...] = jnp.zeros_like(dv_acc)
    for qb in range(BLOCKS):
        lo, hi = window(qb)
        width = hi - lo
        rows = slice(qb * BLOCK, (qb + 1) * BLOCK)
        for pair in range(PAIRS):
            lanes = slice(pair * 128, (pair + 1) * 128)
            q2 = q_ref[rows, lanes]
            k2 = k_ref[lo:hi, lanes]
            v2 = v_ref[lo:hi, lanes]
            do2 = dmix[rows, lanes]
            prod = do2.astype(F32) * m_ref[rows, lanes].astype(F32)
            dqs, scores, qs, dos = [], [], [], []
            for h in range(2):
                pick = low if h == 0 else ~low
                doh = jnp.where(pick, do2, jnp.zeros_like(do2))
                delta = jnp.sum(jnp.where(pick, prod, 0.0), axis=-1, keepdims=True)
                p = p_ref[pair, qb, h * BLOCK : (h + 1) * BLOCK, :width]
                ds = (p.astype(F32) * (dot_t(doh, v2) - delta)).astype(BF)
                dqs.append(dot(ds, k2))
                scores.append(ds)
                qs.append(jnp.where(pick, q2, jnp.zeros_like(q2)))
                dos.append(doh)
            dp_ref[rows, pair * 128 : (pair + 1) * 128] = (
                jnp.where(low, dqs[0], dqs[1]) * 0.125
            ).astype(BF)
            ds_both = jnp.concatenate(scores, axis=0)
            p_both = p_ref[pair, qb, :, :width]
            dk_acc[lo:hi, lanes] += t_dot(ds_both, jnp.concatenate(qs, axis=0))
            dv_acc[lo:hi, lanes] += t_dot(p_both, jnp.concatenate(dos, axis=0))
    dp_ref[:, GW : 2 * GW] = dk_acc[...].astype(BF)
    dp_ref[:, 2 * GW :] = dv_acc[...].astype(BF)
    sums = jnp.concatenate(
        [
            jnp.sum(dp_ref[:, :GW].astype(F32), axis=0, keepdims=True),
            jnp.sum(dp_ref[:, 2 * GW :].astype(F32), axis=0, keepdims=True),
        ],
        axis=0,
    )

    @pl.when(pl.program_id(0) == 0)
    def _():
        sums_ref[...] = sums

    @pl.when(pl.program_id(0) > 0)
    def _():
        sums_ref[...] += sums


def attend_backward(datt, w_out, group, kept):
    q, k, v, p, mixed = kept
    t = datt.shape[0]
    rows = t // SEQ
    row_spec = pl.BlockSpec((SEQ, GW), lambda r: (r, 0))
    return call(
        attend_backward_kernel,
        (rows,),
        [
            pl.BlockSpec((SEQ, D), lambda r: (r, 0)),
            pl.BlockSpec((GW, D), lambda r: (group, 0), pipeline_mode=pl.Buffered(1)),
            row_spec,
            row_spec,
            row_spec,
            pl.BlockSpec((PAIRS,) + p.shape[1:], lambda r: (r, 0, 0, 0)),
            row_spec,
        ],
        [pl.BlockSpec((SEQ, 3 * GW), lambda r: (r, 0)), pl.BlockSpec((2, GW), lambda r: (0, 0))],
        [shaped((t, 3 * GW), BF), shaped((2, GW), F32)],
        flops=t * D * D * 2 * 4,
        nbytes=8 * 2**20,
        scratch=[pltpu.VMEM((SEQ, GW), F32), pltpu.VMEM((SEQ, GW), F32)],
    )(datt, w_out, q, k, v, p, mixed)


TB = 256
CH = 768


def normalize(values):
    centered = values - jnp.mean(values, axis=-1, keepdims=True)
    variance = jnp.mean(centered * centered, axis=-1, keepdims=True)
    inverse = lax.rsqrt(variance + epsilon)
    return centered * inverse, inverse


def normalize_back(grad, xhat, inverse):
    mean = jnp.mean(grad, axis=-1, keepdims=True)
    along = jnp.mean(grad * xhat, axis=-1, keepdims=True)
    return (grad - mean - xhat * along) * inverse


def add_rows(ref, rows):
    stacked = jnp.concatenate([jnp.sum(r, axis=0, keepdims=True) for r in rows], axis=0)

    @pl.when(pl.program_id(0) == 0)
    def _():
        ref[...] = stacked

    @pl.when(pl.program_id(0) > 0)
    def _():
        ref[...] += stacked


def up_kernel(
    tok_ref, m0, m1, m2, wo_ref, vec_ref, wu_ref, bu_ref, xhat_ref, inv_ref, nl_ref, act_ref, gp_ref
):
    att = vec_ref[0:1, :]
    for g, m in enumerate((m0, m1, m2)):
        att = att + dot(m[...], wo_ref[g * GW : (g + 1) * GW, :])
    xhat, inverse = normalize(tok_ref[...].astype(F32) + att)
    xhat_ref[...] = xhat
    inv_ref[...] = inverse
    nl = (xhat * vec_ref[1:2, :] + vec_ref[2:3, :]).astype(BF)
    nl_ref[...] = nl
    for c in range(0, FF, CH):
        u = dot(nl, wu_ref[:, c : c + CH]) + bu_ref[:, c : c + CH]
        cdf = 0.5 * (1.0 + lax.erf(u * root_half))
        act_ref[:, c : c + CH] = (u * cdf).astype(BF)
        gp_ref[:, c : c + CH] = (cdf + u * (jnp.exp(u * u * -0.5) * pdf_scale)).astype(BF)


def up(tokens, mixed, w_out, vec, w_up, bias_up):
    t = tokens.shape[0]
    tok = lambda n: pl.BlockSpec((TB, n), lambda i: (i, 0))
    return call(
        up_kernel,
        (t // TB,),
        [tok(D), tok(GW), tok(GW), tok(GW), whole((D, D)), whole((3, D)), whole((D, FF)), whole((1, FF))],
        [tok(D), tok(1), tok(D), tok(FF), tok(FF)],
        [shaped((t, D), F32), shaped((t, 1), F32), shaped((t, D), BF), shaped((t, FF), BF), shaped((t, FF), BF)],
        flops=2 * t * D * (D + FF) * 2,
        nbytes=24 * 2**20,
    )(tokens, *mixed, w_out, vec, w_up, bias_up)


def down_kernel(
    lengths_ref, act_ref, xhat_ref, wd_ref, vec_ref, cot_ref, out_ref, ds_ref, dd_ref, sums_ref, pool_ref
):
    i = pl.program_id(0)
    normed = xhat_ref[...] * vec_ref[0:1, :] + vec_ref[1:2, :]
    second = normed + (dot(act_ref[...], wd_ref[...]) + vec_ref[2:3, :])
    xhat, inverse = normalize(second)
    out = (xhat * vec_ref[3:4, :] + vec_ref[4:5, :]).astype(BF)
    out_ref[...] = out
    cot = cot_ref[...].astype(F32)
    d_second = normalize_back(cot * vec_ref[3:4, :], xhat, inverse)
    ds_ref[...] = d_second
    d_down = d_second.astype(BF)
    dd_ref[...] = d_down
    add_rows(sums_ref, (cot * xhat, cot, d_down.astype(F32)))
    per_row = SEQ // TB
    row = i // per_row
    places = lax.broadcasted_iota(jnp.int32, (1, TB), 1) + (i % per_row) * TB
    segment = segment_of(places, lengths_ref, row)
    ids = lax.broadcasted_iota(jnp.int32, (SEGS, TB), 0)
    member = jnp.where(segment == ids, 1.0, 0.0).astype(BF)
    sums = dot(member, out)

    @pl.when(i % per_row == 0)
    def _():
        pool_ref[0] = sums

    @pl.when(i % per_row > 0)
    def _():
        pool_ref[0] += sums


def down(lengths, active, xhat, w_down, vec, cot):
    t = cot.shape[0]
    tok = lambda n: pl.BlockSpec((TB, n), lambda i, *_: (i, 0))
    return call(
        down_kernel,
        (t // TB,),
        [tok(FF), tok(D), whole((FF, D)), whole((5, D)), tok(D)],
        [
            tok(D),
            tok(D),
            tok(D),
            pl.BlockSpec((3, D), lambda i, *_: (0, 0)),
            pl.BlockSpec((1, SEGS, D), lambda i, *_: (i // (SEQ // TB), 0, 0)),
        ],
        [
            shaped((t, D), BF),
            shaped((t, D), F32),
            shaped((t, D), BF),
            shaped((3, D), F32),
            shaped((t // SEQ, SEGS, D), F32),
        ],
        flops=2 * t * D * FF,
        nbytes=24 * 2**20,
        prefetch=1,
    )(lengths, active, xhat, w_down, vec, cot)


def back_kernel(
    dd_ref, gp_ref, ds_ref, xhat_ref, inv_ref, wd_ref, wu_ref, gain_ref, du_ref, df_ref, da_ref, sums_ref, su_ref
):
    i = pl.program_id(0)
    dd = dd_ref[...]
    d_normed = ds_ref[...]
    for c in range(0, FF, CH):
        du = (dot_t(dd, wd_ref[c : c + CH, :]) * gp_ref[:, c : c + CH].astype(F32)).astype(BF)
        du_ref[:, c : c + CH] = du
        d_normed = d_normed + dot_t(du, wu_ref[:, c : c + CH])
        partial = jnp.sum(du.astype(F32), axis=0, keepdims=True)
        su_ref[:, c : c + CH] = jnp.where(i == 0, partial, su_ref[:, c : c + CH] + partial)
    xhat = xhat_ref[...]
    d_first = normalize_back(d_normed * gain_ref[...], xhat, inv_ref[...])
    df_ref[...] = d_first
    d_att = d_first.astype(BF)
    da_ref[...] = d_att
    add_rows(sums_ref, (d_normed * xhat, d_normed, d_att.astype(F32)))


def back(d_down, gp, d_second, xhat, inverse, w_down, w_up, gain):
    t = d_down.shape[0]
    tok = lambda n: pl.BlockSpec((TB, n), lambda i: (i, 0))
    return call(
        back_kernel,
        (t // TB,),
        [tok(D), tok(FF), tok(D), tok(D), tok(1), whole((FF, D)), whole((D, FF)), whole((1, D))],
        [tok(FF), tok(D), tok(D), pl.BlockSpec((3, D), lambda i: (0, 0)), pl.BlockSpec((1, FF), lambda i: (0, 0))],
        [shaped((t, FF), BF), shaped((t, D), F32), shaped((t, D), BF), shaped((3, D), F32), shaped((1, FF), F32)],
        flops=4 * t * D * FF,
        nbytes=32 * 2**20,
    )(d_down, gp, d_second, xhat, inverse, w_down, w_up, gain)


def input_kernel(df_ref, p0, p1, p2, wqkv_ref, out_ref):
    total = df_ref[...]
    for g, p in enumerate((p0, p1, p2)):
        for part in range(3):
            start = part * D + g * GW
            total = total + dot_t(p[:, part * GW : (part + 1) * GW], wqkv_ref[:, start : start + GW])
    out_ref[...] = total


def input_gradient(d_first, d_projected, w_qkv):
    t = d_first.shape[0]
    tok = lambda n: pl.BlockSpec((TB, n), lambda i: (i, 0))
    return call(
        input_kernel,
        (t // TB,),
        [tok(D), tok(D), tok(D), tok(D), whole((D, 3 * D))],
        tok(D),
        shaped((t, D), F32),
        flops=2 * t * D * 3 * D,
        nbytes=16 * 2**20,
    )(d_first, *d_projected, w_qkv)


def weight_kernel(ranks, half, me_ref, a_ref, b_ref, *refs):
    outs, (acc, sems) = refs[:-2], refs[-2:]
    me = me_ref[0]
    replica = me_ref[1]
    step = pl.program_id(0)
    columns = acc.shape[1]
    acc[...] = t_dot(a_ref[...], b_ref[...]).astype(BF)
    rows = acc.shape[0] // ranks
    copies = []
    for j in range(ranks):
        owner = me ^ j
        source = acc.at[pl.ds(pl.multiple_of(owner * rows, rows), rows)]
        copies.append(pltpu.make_async_copy(source, outs[j % 2].at[j // 2], sems.at[j]))
    for copy in copies:
        copy.start()
    for copy in copies:
        copy.wait()


def weight_gradient(where, a, b, ranks):
    t, m = a.shape
    n = b.shape[1]
    rows = m // ranks
    half = shaped((ranks // 2, rows, n), BF)
    return call(
        functools.partial(weight_kernel, ranks, False),
        (1,),
        [pl.BlockSpec((t, m), lambda i, *_: (0, 0)), pl.BlockSpec((t, n), lambda i, *_: (0, 0))],
        [pl.BlockSpec(memory_space=pl.ANY)] * 2,
        [half, half],
        flops=2 * t * m * n,
        nbytes=2 * (t * m + t * n + m * n),
        scratch=[pltpu.VMEM((m, n), BF), pltpu.SemaphoreType.DMA((ranks,))],
        prefetch=1,
    )(where, a, b)


def swap(x, mask, ranks):
    return lax.ppermute(x, "fsdp", [(i, i ^ mask) for i in range(ranks)])


def swap_replica(x):
    return lax.ppermute(x, "replica", [(0, 1), (1, 0)])


def bf_sum(*terms):
    total = terms[0].astype(F32)
    for term in terms[1:]:
        total = total + term.astype(F32)
    return total.astype(BF)


def gather_pieces(w, ranks):
    z = jnp.stack([w] + [swap(w, m, ranks) for m in (4, 8, 12)])
    y = swap(z, 2, ranks)
    return (z, y, swap(z, 1, ranks), swap(y, 1, ranks))


def assemble_kernel(me_ref, p0, p1, p2, p3, out_ref, sems):
    me = me_ref[0]
    rows = p0.shape[1]
    copies = []
    for index, piece in enumerate((p0, p1, p2, p3)):
        mask = (index % 2) * 2 + index // 2
        for k in range(4):
            owner = me ^ (4 * k + mask)
            target = out_ref.at[pl.ds(pl.multiple_of(owner * rows, rows), rows)]
            copies.append(pltpu.make_async_copy(piece.at[k], target, sems.at[index * 4 + k]))
    for copy in copies:
        copy.start()
    for copy in copies:
        copy.wait()


def assemble(where, pieces):
    _, rows, columns = pieces[0].shape
    return call(
        assemble_kernel,
        (1,),
        [pl.BlockSpec(memory_space=pl.ANY)] * 4,
        pl.BlockSpec(memory_space=pl.ANY),
        shaped((16 * rows, columns), BF),
        flops=0,
        nbytes=4 * 16 * rows * columns,
        scratch=[pltpu.SemaphoreType.DMA((16,))],
        prefetch=1,
    )(where, *pieces)


def gather_small(x, ranks, me):
    z = jnp.stack([x] + [swap(x, m, ranks) for m in (4, 8, 12)])
    y = swap(z, 2, ranks)
    zy = jnp.stack([z, y], axis=1)
    c = swap(zy, 1, ranks)
    relative = jnp.stack([zy, c], axis=2).reshape(ranks, -1)
    return relative[me ^ jnp.arange(ranks)]


def scatter_pieces(keep, send, ranks):
    _, rows, columns = keep.shape
    received = swap(send, 1, ranks)
    keep = keep.reshape(4, 2, rows, columns)
    received = received.reshape(4, 2, rows, columns)
    away = bf_sum(keep[:, 1], received[:, 1])
    stay = bf_sum(keep[:, 0], received[:, 0])
    back_y = swap(away, 2, ranks)
    parts = [bf_sum(stay[k], back_y[k]) for k in range(4)]
    total = bf_sum(parts[0], *[swap(parts[k], 4 * k, ranks) for k in (1, 2, 3)])
    return total.astype(F32) + swap_replica(total).astype(F32)


def scatter_small(x, ranks, me):
    relative = x[me ^ jnp.arange(ranks)].reshape(4, 2, 2, -1)
    relative = relative[:, :, 0] + swap(relative[:, :, 1], 1, ranks)
    relative = relative[:, 0] + swap(relative[:, 1], 2, ranks)
    total = relative[0] + sum(swap(relative[k], 4 * k, ranks) for k in (1, 2, 3))
    return total + swap_replica(total)


def gather_pooled(pooled, ranks, me, replica):
    z = jnp.stack([pooled] + [swap(pooled, m, ranks) for m in (4, 8, 12)])
    y = swap(z, 2, ranks)
    zy = jnp.stack([z, y], axis=1)
    x = swap_replica(zy)
    zyx = jnp.stack([zy, x])
    c = swap(zyx, 1, ranks)
    relative = jnp.stack([zyx, c], axis=3)
    relative = relative.reshape((2, ranks) + pooled.shape)
    own = relative[jnp.array([0, 1]) ^ replica][:, me ^ jnp.arange(ranks)]
    return own.reshape((2 * ranks * pooled.shape[0],) + pooled.shape[1:])


SMALL = ("bias_qv", "bias_out", "gain_one", "shift_one", "bias_up", "bias_down", "gain_two", "shift_two")
SMALL_SIZES = (2 * D, D, D, D, FF, D, D, D)


def body(
    ranks,
    replicas,
    tokens,
    lengths,
    w_qkv,
    bias_qv,
    w_out,
    bias_out,
    gain_one,
    shift_one,
    w_up,
    bias_up,
    w_down,
    bias_down,
    gain_two,
    shift_two,
    cotangent,
):
    direct = ranks == 16 and replicas == 2
    me = lax.axis_index("fsdp")
    replica = lax.axis_index("replica")
    where = jnp.stack([me, replica]).astype(jnp.int32)
    gather = lambda w: lax.all_gather(w, "fsdp", axis=0, tiled=True)

    small = jnp.concatenate(
        [bias_qv, bias_out, gain_one, shift_one, bias_up, bias_down, gain_two, shift_two]
    )
    if direct:
        small_all = gather_small(small, ranks, me)
    else:
        small_all = gather(small).reshape(ranks, -1)
    vectors, start = {}, 0
    for name, size in zip(SMALL, SMALL_SIZES):
        part = size // ranks
        vectors[name] = small_all[:, start : start + part].reshape(size).astype(F32)
        start += part
    if direct:
        w_qkv_full = assemble(where, gather_pieces(w_qkv, ranks))
    else:
        w_qkv_full = gather(w_qkv)
    w_out_full, w_up_full, w_down_full = gather(w_out), gather(w_up), gather(w_down)

    kept = []
    for g in range(GROUPS):
        cols = slice(g * GW, (g + 1) * GW)
        wq, wk, wv = (w_qkv_full[:, p * D + g * GW : p * D + (g + 1) * GW] for p in range(3))
        bias = jnp.stack([vectors["bias_qv"][:D][cols], vectors["bias_qv"][D:][cols]])
        kept.append(attend_forward(lengths, tokens, wq, wk, wv, bias))
    mixed = [item[4] for item in kept]
    vec_one = jnp.stack([vectors["bias_out"], vectors["gain_one"], vectors["shift_one"]])
    xhat, inverse, nl, active, gp = up(
        tokens, mixed, w_out_full, vec_one, w_up_full, vectors["bias_up"][None]
    )
    vec_two = jnp.stack(
        [vectors[n] for n in ("gain_one", "shift_one", "bias_down", "gain_two", "shift_two")]
    )
    layer_out, d_second, d_down, sums_two, pool = down(
        lengths, active, xhat, w_down_full, vec_two, cotangent
    )

    def reduce(a, b):
        m, n = a.shape[1], b.shape[1]
        if direct:
            return scatter_pieces(*weight_gradient(where, a, b, ranks), ranks)
        term = t_dot(a, b).astype(BF)
        shard = lax.psum_scatter(term, "fsdp", scatter_dimension=0, tiled=True)
        return lax.psum(shard, "replica").astype(F32)

    grad_w_down = reduce(active, d_down)
    d_upper, d_first, d_att, sums_one, sums_up = back(
        d_down, gp, d_second, xhat, inverse, w_down_full, w_up_full, vectors["gain_one"][None]
    )
    grad_w_up = reduce(nl, d_upper)
    grad_w_out = reduce(jnp.concatenate(mixed, axis=1), d_att)
    d_projected, sums_qv, grads_qkv = [], [], []
    for g in range(GROUPS):
        dp, sums = attend_backward(d_att, w_out_full, g, kept[g])
        d_projected.append(dp)
        sums_qv.append(sums)
        grads_qkv.append(reduce(tokens, dp))
    input_grad = input_gradient(d_first, d_projected, w_qkv_full)
    grad_w_qkv = jnp.concatenate(
        [grads_qkv[g][:, p * GW : (p + 1) * GW] for p in range(3) for g in range(GROUPS)], axis=1
    )

    pooled = (pool / lengths.astype(F32)[:, :, None]).astype(BF)
    if direct:
        pooled_all = gather_pooled(pooled, ranks, me, replica)
    else:
        pooled_all = lax.all_gather(pooled, ("replica", "fsdp"), axis=0, tiled=True)

    small_terms = {
        "bias_qv": jnp.concatenate([s[i] for i in range(2) for s in sums_qv]),
        "bias_out": sums_one[2],
        "gain_one": sums_one[0],
        "shift_one": sums_one[1],
        "bias_up": sums_up[0],
        "bias_down": sums_two[2],
        "gain_two": sums_two[0],
        "shift_two": sums_two[1],
    }
    packed = jnp.concatenate([small_terms[n].reshape(ranks, -1) for n in SMALL], axis=1)
    if direct:
        packed = scatter_small(packed, ranks, me)
    else:
        packed = lax.psum_scatter(packed, "fsdp", scatter_dimension=0, tiled=False)
        packed = lax.psum(packed, "replica")
    small_grads, start = {}, 0
    for name, size in zip(SMALL, SMALL_SIZES):
        part = size // ranks
        small_grads[name] = packed[start : start + part]
        start += part
    return (
        layer_out,
        input_grad,
        pooled_all.astype(F32),
        grad_w_qkv,
        small_grads["bias_qv"],
        grad_w_out,
        small_grads["bias_out"],
        small_grads["gain_one"],
        small_grads["shift_one"],
        grad_w_up,
        small_grads["bias_up"],
        grad_w_down,
        small_grads["bias_down"],
        small_grads["gain_two"],
        small_grads["shift_two"],
    )


def solution(mesh):
    rows = P(("replica", "fsdp"), None)
    matrix = P("fsdp", None)
    vector = P("fsdp")
    return jax.shard_map(
        functools.partial(body, mesh.shape["fsdp"], mesh.shape["replica"]),
        mesh=mesh,
        in_specs=(
            rows,
            rows,
            matrix,
            vector,
            matrix,
            vector,
            vector,
            vector,
            matrix,
            vector,
            matrix,
            vector,
            vector,
            vector,
            rows,
        ),
        out_specs=(
            rows,
            rows,
            P(),
            matrix,
            vector,
            matrix,
            vector,
            vector,
            vector,
            matrix,
            vector,
            matrix,
            vector,
            vector,
            vector,
        ),
        check_vma=False,
    )
```

```python
import functools

import jax
import jax.numpy as jnp
from jax import lax
from jax.experimental import pallas as pl
from jax.experimental.pallas import tpu as pltpu
from jax.sharding import PartitionSpec as P

D = 768
H = 12
HD = 64
FF = 3072
SEQ = 512
SEGS = 8
GROUPS = 3
GW = D // GROUPS
PAIRS = GW // 128
BLOCK = 128
BLOCKS = SEQ // BLOCK
WIDE = 3 * BLOCK

epsilon = 1e-12
root_half = 0.7071067811865476
masked_score = -1e30
pdf_scale = 0.3989422804014327

BF = jnp.bfloat16
F32 = jnp.float32
VMEM_LIMIT = 56 * 2**20


def dot(a, b):
    return jnp.dot(a, b, preferred_element_type=F32)


def dot_t(a, b):
    return lax.dot_general(a, b, (((1,), (1,)), ((), ())), preferred_element_type=F32)


def t_dot(a, b):
    return lax.dot_general(a, b, (((0,), (0,)), ((), ())), preferred_element_type=F32)


def window(qb):
    return max(0, (qb - 1) * BLOCK), min(SEQ, (qb + 2) * BLOCK)


def call(kernel, grid, in_specs, out_specs, out_shape, us, scratch=(), prefetch=0, after=()):
    first = prefetch + len(in_specs)

    def run(*refs):
        kernel(*refs[:first], *refs[first + len(after) :])

    return functools.partial(
        lambda extra, *args: pl.pallas_call(
            run,
            grid_spec=pltpu.PrefetchScalarGridSpec(
                num_scalar_prefetch=prefetch,
                grid=grid,
                in_specs=list(in_specs) + [pl.BlockSpec(memory_space=pl.ANY)] * len(extra),
                out_specs=out_specs,
                scratch_shapes=list(scratch),
            ),
            out_shape=out_shape,
            compiler_params=pltpu.CompilerParams(vmem_limit_bytes=VMEM_LIMIT),
            cost_estimate=pl.CostEstimate(
                flops=int(us * 1.15e9), bytes_accessed=int(us * 3.6e6), transcendentals=0
            ),
        )(*args, *extra),
        tuple(after),
    )


def shaped(shape, dtype):
    return jax.ShapeDtypeStruct(shape, dtype)


def whole(shape):
    return pl.BlockSpec(shape, lambda *_: (0,) * len(shape), pipeline_mode=pl.Buffered(1))


ANY = pl.BlockSpec(memory_space=pl.ANY)


def pack_weights(w_out, w_up, w_down):
    blocks = [w_up[:, i * D : (i + 1) * D] for i in range(FF // D)]
    return jnp.concatenate([w_out] + blocks + [w_down], axis=0)


def weight_copies(name, refs, target, sems):
    if len(refs) == 3:
        source = refs[("out", "up", "down").index(name)]
        return [pltpu.make_async_copy(source, target, sems.at[0])]
    packed = refs[0]
    ranks = packed.shape[0]
    r = D // ranks
    copies = []
    for o in range(ranks):
        if name == "out":
            parts = [(slice(0, r), target.at[o * r : (o + 1) * r])]
        elif name == "up":
            parts = [
                (
                    slice((1 + i) * r, (2 + i) * r),
                    target.at[o * r : (o + 1) * r, i * D : (i + 1) * D],
                )
                for i in range(FF // D)
            ]
        else:
            n = FF // ranks
            parts = [(slice(5 * r, 5 * r + n), target.at[o * n : (o + 1) * n])]
        for rows, where in parts:
            copies.append(pltpu.make_async_copy(packed.at[o, rows], where, sems.at[len(copies)]))
    return copies


def start_all(copies):
    for copy in copies:
        copy.start()


def wait_all(copies):
    for copy in copies:
        copy.wait()


def segment_of(places, lengths_ref, row):
    total = jnp.int32(0)
    segment = jnp.zeros(places.shape, jnp.int32)
    for s in range(SEGS):
        total = total + lengths_ref[row, s]
        segment = segment + (places >= total).astype(jnp.int32)
    return segment


def both_heads(x2):
    low = lax.broadcasted_iota(jnp.int32, (1, 128), 1) < HD
    zero = jnp.zeros_like(x2)
    return jnp.concatenate([jnp.where(low, x2, zero), jnp.where(low, zero, x2)], axis=0)


def attend_forward_kernel(
    lengths_ref, tok_ref, wq_ref, wk_ref, wv_ref, bias_ref, q_ref, k_ref, v_ref, p_ref, m_ref, vt, ot
):
    row = pl.program_id(1)
    tok = tok_ref[...]
    q_ref[...] = (dot(tok, wq_ref[...]) + bias_ref[0, 0:1, :]).astype(BF) * jnp.asarray(0.125, BF)
    k_ref[...] = dot(tok, wk_ref[...]).astype(BF)
    v = dot(tok, wv_ref[...]) + bias_ref[0, 1:2, :]
    v_ref[...] = v.astype(BF)
    vt[...] = v.T.astype(BF)
    for qb in range(BLOCKS):
        lo, hi = window(qb)
        width = hi - lo
        rows = slice(qb * BLOCK, (qb + 1) * BLOCK)
        seg_q = segment_of(
            lax.broadcasted_iota(jnp.int32, (1, BLOCK), 1) + qb * BLOCK, lengths_ref, row
        )
        seg_k = segment_of(
            lax.broadcasted_iota(jnp.int32, (width, 1), 0) + lo, lengths_ref, row
        )
        mask = jnp.where(jnp.concatenate([seg_q, seg_q], axis=1) == seg_k, 0.0, masked_score)
        for pair in range(PAIRS):
            lanes = slice(pair * 128, (pair + 1) * 128)
            s = dot_t(k_ref[lo:hi, lanes], both_heads(q_ref[rows, lanes])) + mask
            w = jnp.exp(s - jnp.max(s, axis=0, keepdims=True))
            p = (w * (1.0 / jnp.sum(w, axis=0, keepdims=True))).astype(BF)
            p_ref[0, pair, qb, :width, :] = p
            o = dot(vt[lanes, lo:hi], p)
            ot[pair * 128 : pair * 128 + HD, rows] = o[:HD, :BLOCK]
            ot[pair * 128 + HD : (pair + 1) * 128, rows] = o[HD:, BLOCK:]
    m_ref[...] = ot[...].T.astype(BF)


def attend_forward(lengths, tokens, w_qkv, bias, after=()):
    t = tokens.shape[0]
    rows = t // SEQ
    row_spec = pl.BlockSpec((SEQ, GW), lambda g, r, *_: (r, g))
    p_shape = (GROUPS * rows, PAIRS, BLOCKS, WIDE, 2 * BLOCK)
    column = lambda part: pl.BlockSpec((D, GW), lambda g, r, *_: (0, part * GROUPS + g))
    return call(
        attend_forward_kernel,
        (GROUPS, rows),
        [
            pl.BlockSpec((SEQ, D), lambda g, r, *_: (r, 0)),
            column(0),
            column(1),
            column(2),
            pl.BlockSpec((1, 2, GW), lambda g, r, *_: (g, 0, 0)),
        ],
        [row_spec] * 3
        + [pl.BlockSpec((1,) + p_shape[1:], lambda g, r, *_: (g * rows + r, 0, 0, 0, 0)), row_spec],
        [shaped((t, D), BF)] * 3 + [shaped(p_shape, BF), shaped((t, D), BF)],
        us=28,
        scratch=[pltpu.VMEM((GW, SEQ), BF), pltpu.VMEM((GW, SEQ), F32)],
        prefetch=1,
        after=after,
    )(lengths, tokens, w_qkv, w_qkv, w_qkv, bias)


def attend_backward_kernel(
    groups, direct, halves, where_ref, datt_ref, tok_ref, m_ref, wrefs, q_ref, k_ref, v_ref, p_ref, dp_ref,
    sums_ref, wg_refs, wo, kt, qt, dk_acc, dv_acc, dw_acc, dw_low, wsems, sems,
):
    g = pl.program_id(0)
    row = pl.program_id(1)
    first = groups[0]
    with_out = first == 0
    last = pl.num_programs(1) - 1
    span = 3 * GW

    def emit(place):
        if direct:
            part = span // halves
            copies = term_copies(
                where_ref,
                lambda owner_rows, h: dw_low.at[owner_rows, h * part : (h + 1) * part],
                D,
                lambda ref, where: ref.at[
                    where + (slice(None), pl.ds(pl.multiple_of(place * part, 128), part))
                ],
                wg_refs,
                sems,
                halves,
            )
        else:
            where = pl.ds(pl.multiple_of(place * span, 128), span)
            copies = [pltpu.make_async_copy(dw_low, wg_refs[0].at[:, where], sems.at[0])]
        start_all(copies)
        wait_all(copies)

    def add_term(term, place):
        @pl.when(row == 0)
        def _():
            dw_acc[...] = term

        @pl.when((row > 0) & (row < last))
        def _():
            dw_acc[...] += term

        @pl.when(row == last)
        def _():
            dw_low[...] = (dw_acc[...] + term).astype(BF)
            emit(place)

    if with_out:

        @pl.when(g == 0)
        def _():
            add_term(t_dot(m_ref[...], datt_ref[...]), 0)

    @pl.when((g == with_out) & (row == 0))
    def _():
        copies = weight_copies("out", wrefs, wo, wsems)
        start_all(copies)
        wait_all(copies)

    def group_step():
        place = g - with_out
        wo_rows = wo[pl.ds(pl.multiple_of((place + first) * GW, GW), GW), :]
        dmix = dot_t(datt_ref[...], wo_rows).astype(BF)
        kt[...] = k_ref[...].astype(F32).T.astype(BF)
        dk_acc[...] = jnp.zeros_like(dk_acc)
        dv_acc[...] = jnp.zeros_like(dv_acc)
        for qb in range(BLOCKS):
            lo, hi = window(qb)
            width = hi - lo
            rows = slice(qb * BLOCK, (qb + 1) * BLOCK)
            for pair in range(PAIRS):
                lanes = slice(pair * 128, (pair + 1) * 128)
                dos = both_heads(dmix[rows, lanes])
                p_low = p_ref[0, pair, qb, :width, :]
                p = p_low.astype(F32)
                dp = dot_t(v_ref[lo:hi, lanes], dos)
                delta = jnp.sum(p * dp, axis=0, keepdims=True)
                ds = (p * (dp - delta)).astype(BF)
                dk_acc[lo:hi, lanes] += dot(ds, both_heads(q_ref[rows, lanes]))
                dv_acc[lo:hi, lanes] += dot(p_low, dos)
                dq = dot(kt[lanes, lo:hi], ds)
                qt[pair * 128 : pair * 128 + HD, rows] = dq[:HD, :BLOCK]
                qt[pair * 128 + HD : (pair + 1) * 128, rows] = dq[HD:, BLOCK:]
        dq = (qt[...] * 0.125).T.astype(BF)
        dv = dv_acc[...].astype(BF)
        dp_ref[:, :GW] = dq
        dp_ref[:, GW : 2 * GW] = dk_acc[...].astype(BF)
        dp_ref[:, 2 * GW :] = dv
        sums = jnp.concatenate(
            [
                jnp.sum(dq.astype(F32), axis=0, keepdims=True),
                jnp.sum(dv.astype(F32), axis=0, keepdims=True),
            ],
            axis=0,
        )
        sums_ref[...] = jnp.where(row == 0, sums, sums_ref[...] + sums)
        add_term(t_dot(tok_ref[...], dp_ref[...]), g)

    if with_out:
        pl.when(g > 0)(group_step)
    else:
        group_step()


RANKS = 16


def term_copies(where_ref, source, total_rows, target, refs, sems, halves):
    me, replica = where_ref[0], where_ref[1]
    rows = total_rows // RANKS
    copies = []
    for j in range(RANKS):
        owner_rows = pl.ds(pl.multiple_of((me ^ j) * rows, rows), rows)
        place = ((j >> 1) & 1, j >> 2)
        for h in range(halves):
            where = ((h ^ replica,) if halves == 2 else ()) + place
            copies.append(
                pltpu.make_async_copy(
                    source(owner_rows, h), target(refs[j & 1], where), sems.at[halves * j + h]
                )
            )
    return copies


def attend_backward(where, datt, tokens, weights, groups, kept, direct, halves, after=()):
    q, k, v, p, mixed = kept
    t = datt.shape[0]
    rows = t // SEQ
    count, first = len(groups), groups[0]
    extra = int(first == 0)
    group = lambda g: jnp.maximum(g - extra, 0) + first
    row_spec = pl.BlockSpec((SEQ, GW), lambda g, r, *_: (r, group(g)))
    full_row = pl.BlockSpec((SEQ, D), lambda g, r, *_: (r, 0))
    columns = (count + extra) * 3 * GW
    if direct:
        lead = (2, 2, 4) if halves == 2 else (2, 4)
        wg_shapes = [shaped(lead + (D // RANKS, columns // halves), BF)] * 2
    else:
        wg_shapes = [shaped((D, columns), BF)]
    nw, ng = len(weights), len(wg_shapes)

    def kernel(where_ref, datt_ref, tok_ref, m_ref, *refs):
        wrefs, refs = refs[:nw], refs[nw:]
        q_ref, k_ref, v_ref, p_ref, dp_ref, sums_ref = refs[:6]
        wg_refs, scratch = refs[6 : 6 + ng], refs[6 + ng :]
        attend_backward_kernel(
            groups, direct, halves, where_ref, datt_ref, tok_ref, m_ref, wrefs, q_ref, k_ref, v_ref, p_ref,
            dp_ref, sums_ref, wg_refs, *scratch,
        )

    m_spec = pl.BlockSpec((SEQ, D), lambda g, r, *_: (jnp.where(g == 0, r, rows - 1), 0))
    return call(
        kernel,
        (count + extra, rows),
        [full_row, full_row, m_spec if extra else ANY]
        + [ANY] * nw
        + [
            row_spec,
            row_spec,
            row_spec,
            pl.BlockSpec((1,) + p.shape[1:], lambda g, r, *_: (group(g) * rows + r, 0, 0, 0, 0)),
        ],
        [
            pl.BlockSpec(
                (SEQ, 3 * GW), lambda g, r, *_: (jnp.where(g < extra, 0, r), jnp.maximum(g - extra, 0))
            ),
            pl.BlockSpec((2, GW), lambda g, r, *_: (0, jnp.maximum(g - extra, 0))),
        ]
        + [ANY] * ng,
        [shaped((t, count * 3 * GW), BF), shaped((2, count * GW), F32)] + wg_shapes,
        us=1,
        scratch=[
            pltpu.VMEM((D, D), BF),
            pltpu.VMEM((GW, SEQ), BF),
            pltpu.VMEM((GW, SEQ), F32),
            pltpu.VMEM((SEQ, GW), F32),
            pltpu.VMEM((SEQ, GW), F32),
            pltpu.VMEM((D, 3 * GW), F32),
            pltpu.VMEM((D, 3 * GW), BF),
            pltpu.SemaphoreType.DMA((16,)),
            pltpu.SemaphoreType.DMA((2 * RANKS,)),
        ],
        prefetch=1,
        after=after,
    )(where, datt, tokens, mixed, *weights, q, k, v, p)


TB = 256
CH = 768


def normalize(values):
    centered = values - jnp.mean(values, axis=-1, keepdims=True)
    variance = jnp.mean(centered * centered, axis=-1, keepdims=True)
    inverse = lax.rsqrt(variance + epsilon)
    return centered * inverse, inverse


def normalize_back(grad, xhat, inverse):
    mean = jnp.mean(grad, axis=-1, keepdims=True)
    along = jnp.mean(grad * xhat, axis=-1, keepdims=True)
    return (grad - mean - xhat * along) * inverse


def add_rows(ref, rows):
    stacked = jnp.concatenate([jnp.sum(r, axis=0, keepdims=True) for r in rows], axis=0)
    ref[...] = jnp.where(pl.program_id(0) == 0, stacked, ref[...] + stacked)


def up(tokens, mixed, weights, vec, bias_up, after=()):
    t = tokens.shape[0]
    nw = len(weights)

    def kernel(tok_ref, m_ref, vec_ref, bu_ref, *refs):
        wrefs, refs = refs[:nw], refs[nw:]
        xhat_ref, inv_ref, nl_ref, act_ref, gp_ref, wo, wu, so, su = refs
        out_copies = weight_copies("out", wrefs, wo, so)
        up_copies = weight_copies("up", wrefs, wu, su)

        @pl.when(pl.program_id(0) == 0)
        def _():
            start_all(out_copies)
            start_all(up_copies)
            wait_all(out_copies)

        att = dot(m_ref[...], wo[...]) + vec_ref[0:1, :]
        xhat, inverse = normalize(tok_ref[...].astype(F32) + att)
        xhat_ref[...] = xhat
        inv_ref[...] = inverse
        nl_ref[...] = (xhat * vec_ref[1:2, :] + vec_ref[2:3, :]).astype(BF)

        @pl.when(pl.program_id(0) == 0)
        def _():
            wait_all(up_copies)

        nl = nl_ref[...]
        for c in range(0, FF, CH):
            u = dot(nl, wu[:, c : c + CH]) + bu_ref[:, c : c + CH]
            cdf = 0.5 * (1.0 + lax.erf(u * root_half))
            act_ref[:, c : c + CH] = (u * cdf).astype(BF)
            gp_ref[:, c : c + CH] = (cdf + u * (jnp.exp(u * u * -0.5) * pdf_scale)).astype(BF)

    tok = lambda n: pl.BlockSpec((TB, n), lambda i: (i, 0))
    return call(
        kernel,
        (t // TB,),
        [tok(D), tok(D), whole((3, D)), whole((1, FF))] + [ANY] * nw,
        [tok(D), tok(1), tok(D), tok(FF), tok(FF)],
        [shaped((t, D), F32), shaped((t, 1), F32), shaped((t, D), BF), shaped((t, FF), BF), shaped((t, FF), BF)],
        us=18,
        scratch=[
            pltpu.VMEM((D, D), BF),
            pltpu.VMEM((D, FF), BF),
            pltpu.SemaphoreType.DMA((16,)),
            pltpu.SemaphoreType.DMA((64,)),
        ],
        after=after,
    )(tokens, mixed, vec, bias_up, *weights)


def down(lengths, active, xhat, weights, vec, cot, after=()):
    t = cot.shape[0]
    nw = len(weights)
    per_row = SEQ // TB

    def kernel(lengths_ref, act_ref, xhat_ref, vec_ref, cot_ref, *refs):
        wrefs, refs = refs[:nw], refs[nw:]
        out_ref, ds_ref, dd_ref, sums_ref, pool_ref, wd, sems = refs
        i = pl.program_id(0)

        @pl.when(i == 0)
        def _():
            copies = weight_copies("down", wrefs, wd, sems)
            start_all(copies)
            wait_all(copies)

        normed = xhat_ref[...] * vec_ref[0:1, :] + vec_ref[1:2, :]
        second = normed + (dot(act_ref[...], wd[...]) + vec_ref[2:3, :])
        xhat, inverse = normalize(second)
        out = (xhat * vec_ref[3:4, :] + vec_ref[4:5, :]).astype(BF)
        out_ref[...] = out
        cot = cot_ref[...].astype(F32)
        d_second = normalize_back(cot * vec_ref[3:4, :], xhat, inverse)
        ds_ref[...] = d_second
        d_down = d_second.astype(BF)
        dd_ref[...] = d_down
        add_rows(sums_ref, (d_down.astype(F32), cot * xhat, cot))
        row = i // per_row
        places = lax.broadcasted_iota(jnp.int32, (1, TB), 1) + (i % per_row) * TB
        segment = segment_of(places, lengths_ref, row)
        ids = lax.broadcasted_iota(jnp.int32, (SEGS, TB), 0)
        sums = dot(jnp.where(segment == ids, 1.0, 0.0).astype(BF), out)
        pool_ref[0] = jnp.where(i % per_row == 0, sums, pool_ref[0] + sums)

    tok = lambda n: pl.BlockSpec((TB, n), lambda i, *_: (i, 0))
    return call(
        kernel,
        (t // TB,),
        [tok(FF), tok(D), whole((5, D)), tok(D)] + [ANY] * nw,
        [
            tok(D),
            tok(D),
            tok(D),
            pl.BlockSpec((3, D), lambda i, *_: (0, 0)),
            pl.BlockSpec((1, SEGS, D), lambda i, *_: (i // per_row, 0, 0)),
        ],
        [
            shaped((t, D), BF),
            shaped((t, D), F32),
            shaped((t, D), BF),
            shaped((3, D), F32),
            shaped((t // SEQ, SEGS, D), F32),
        ],
        us=14,
        scratch=[pltpu.VMEM((FF, D), BF), pltpu.SemaphoreType.DMA((16,))],
        prefetch=1,
        after=after,
    )(lengths, active, xhat, vec, cot, *weights)


def back_up(d_down, gp, weights, after=()):
    t = d_down.shape[0]
    nw = len(weights)

    def kernel(dd_ref, gp_ref, *refs):
        wrefs, refs = refs[:nw], refs[nw:]
        du_ref, su_ref, wd, sd = refs
        i = pl.program_id(0)

        @pl.when(i == 0)
        def _():
            down_copies = weight_copies("down", wrefs, wd, sd)
            start_all(down_copies)
            wait_all(down_copies)

        dd = dd_ref[...]
        for c in range(0, FF, CH):
            du = (dot_t(dd, wd[c : c + CH, :]) * gp_ref[:, c : c + CH].astype(F32)).astype(BF)
            du_ref[:, c : c + CH] = du
            partial = jnp.sum(du.astype(F32), axis=0, keepdims=True)
            su_ref[:, c : c + CH] = jnp.where(i == 0, partial, su_ref[:, c : c + CH] + partial)

    tok = lambda n: pl.BlockSpec((TB, n), lambda i: (i, 0))
    return call(
        kernel,
        (t // TB,),
        [tok(D), tok(FF)] + [ANY] * nw,
        [tok(FF), pl.BlockSpec((1, FF), lambda i: (0, 0))],
        [shaped((t, FF), BF), shaped((1, FF), F32)],
        us=11,
        scratch=[pltpu.VMEM((FF, D), BF), pltpu.SemaphoreType.DMA((16,))],
        after=after,
    )(d_down, gp, *weights)


def back_first(d_upper, d_second, xhat, inverse, weights, gain, after=()):
    t = d_upper.shape[0]
    nw = len(weights)

    def kernel(du_ref, ds_ref, xhat_ref, inv_ref, gain_ref, *refs):
        wrefs, refs = refs[:nw], refs[nw:]
        df_ref, da_ref, sums_ref, wu, su = refs

        @pl.when(pl.program_id(0) == 0)
        def _():
            up_copies = weight_copies("up", wrefs, wu, su)
            start_all(up_copies)
            wait_all(up_copies)

        d_normed = ds_ref[...] + dot_t(du_ref[...], wu[...])
        xhat = xhat_ref[...]
        d_first = normalize_back(d_normed * gain_ref[...], xhat, inv_ref[...])
        df_ref[...] = d_first
        d_att = d_first.astype(BF)
        da_ref[...] = d_att
        add_rows(sums_ref, (d_att.astype(F32), d_normed * xhat, d_normed))

    tok = lambda n: pl.BlockSpec((TB, n), lambda i: (i, 0))
    return call(
        kernel,
        (t // TB,),
        [tok(FF), tok(D), tok(D), tok(1), whole((1, D))] + [ANY] * nw,
        [tok(D), tok(D), pl.BlockSpec((3, D), lambda i: (0, 0))],
        [shaped((t, D), F32), shaped((t, D), BF), shaped((3, D), F32)],
        us=1,
        scratch=[pltpu.VMEM((D, FF), BF), pltpu.SemaphoreType.DMA((64,))],
        after=after,
    )(d_upper, d_second, xhat, inverse, gain, *weights)


def input_gradient(d_first, d_projected, w_qkv, after=()):
    t = d_first.shape[0]

    def kernel(df_ref, p0, p1, w_ref, out_ref):
        total = df_ref[...]
        g = 0
        for p in (p0, p1):
            for local in range(p.shape[1] // D):
                for part in range(3):
                    start = part * D + g * GW
                    at = local * D + part * GW
                    total = total + dot_t(p[:, at : at + GW], w_ref[:, start : start + GW])
                g += 1
        out_ref[...] = total

    tok = lambda n: pl.BlockSpec((TB, n), lambda i: (i, 0))
    return call(
        kernel,
        (t // TB,),
        [tok(D), tok(d_projected[0].shape[1]), tok(d_projected[1].shape[1]), whole((D, 3 * D))],
        tok(D),
        shaped((t, D), F32),
        us=9,
        after=after,
    )(d_first, *d_projected, w_qkv)


def grad_down(where, active, d_down, direct, after=()):
    t = d_down.shape[0]
    half = D // 2
    blocks = 4
    n = FF // blocks

    def kernel(where_ref, a_ref, b_ref, *refs):
        outs, (acc, sems) = refs[:-2], refs[-2:]
        i = pl.program_id(0)
        if not direct:
            outs[0][...] = t_dot(a_ref[...], b_ref[...]).astype(BF)
            return
        acc[pl.ds(pl.multiple_of(i * n, n), n), :] = t_dot(a_ref[...], b_ref[...]).astype(BF)

        @pl.when(i == blocks - 1)
        def _():
            copies = term_copies(
                where_ref,
                lambda owner_rows, h: acc.at[owner_rows, h * half : (h + 1) * half],
                FF,
                lambda ref, where: ref.at[where],
                outs,
                sems,
                2,
            )
            start_all(copies)
            wait_all(copies)

    if direct:
        out_shapes, out_specs = [shaped((2, 2, 4, FF // RANKS, half), BF)] * 2, [ANY] * 2
    else:
        out_shapes, out_specs = [shaped((FF, D), BF)], [pl.BlockSpec((n, D), lambda i, *_: (i, 0))]
    return call(
        kernel,
        (blocks,),
        [pl.BlockSpec((t, n), lambda i, *_: (0, i)), whole((t, D))],
        out_specs,
        out_shapes,
        us=10,
        scratch=[pltpu.VMEM((FF, D), BF), pltpu.SemaphoreType.DMA((2 * RANKS,))],
        prefetch=1,
        after=after,
    )(where, active, d_down)


def grad_up(nl, d_upper, after=()):
    t = nl.shape[0]
    n = 768

    def kernel(nl_ref, du_ref, out_ref):
        out_ref[...] = t_dot(nl_ref[...], du_ref[...]).astype(BF)

    return call(
        kernel,
        (FF // n,),
        [whole((t, D)), pl.BlockSpec((t, n), lambda i: (0, i))],
        pl.BlockSpec((D, n), lambda i: (0, i)),
        shaped((D, FF), BF),
        us=9,
        after=after,
    )(nl, d_upper)


def swap(x, mask):
    return lax.ppermute(x, "fsdp", [(i, i ^ mask) for i in range(RANKS)])


def swap_replica(x):
    return lax.ppermute(x, "replica", [(0, 1), (1, 0)])


def added(*terms):
    total = terms[0].astype(F32)
    for term in terms[1:]:
        total = total + term.astype(F32)
    return total


def gather_qkv(where, w, replica):
    rows, columns = w.shape
    half = columns // 2
    own = lax.dynamic_slice_in_dim(w, replica * half, half, 1)
    z = jnp.stack([own] + [swap(own, m) for m in (4, 8, 12)])
    zy = jnp.stack([z, swap(z, 2)])
    x = swap_replica(zy)
    pieces = (zy, x, swap(zy, 1), swap(x, 1))

    def kernel(where_ref, p0, p1, p2, p3, out_ref, sems):
        me, other = where_ref[0], where_ref[1]
        copies = []
        for index, piece in enumerate((p0, p1, p2, p3)):
            start = pl.multiple_of((other ^ (index % 2)) * half, 128)
            for y in range(2):
                for k in range(4):
                    owner = me ^ (4 * k + 2 * y + index // 2)
                    target = out_ref.at[
                        pl.ds(pl.multiple_of(owner * rows, rows), rows), pl.ds(start, half)
                    ]
                    copies.append(
                        pltpu.make_async_copy(piece.at[y, k], target, sems.at[len(copies)])
                    )
        start_all(copies)
        wait_all(copies)

    return call(
        kernel,
        (1,),
        [ANY] * 4,
        pl.BlockSpec((RANKS * rows, columns), lambda *_: (0, 0)),
        shaped((RANKS * rows, columns), BF),
        us=4,
        scratch=[pltpu.SemaphoreType.DMA((32,))],
        prefetch=1,
    )(where, *pieces)


def ordered(own, other, replica):
    first = jnp.where(replica == 0, own, other)
    second = jnp.where(replica == 0, other, own)
    return first, second


class Chain:
    def __init__(self, keep, send, lines=None, grow=False):
        self.columns = keep.shape[-1]
        flat = lambda x: x.reshape(-1, self.columns)
        halves = [(swap_replica,)] if keep.ndim == 5 else []
        over = lambda m: lambda x: swap(x, m)
        along_z = [(over(8),), (over(4),)] if grow else [(over(4), over(8), over(12))]
        fsdp = [(over(1),)] + halves + [(over(2),)] + along_z
        self.moves = fsdp + [(swap_replica,)]
        self.owner_rows = keep.shape[-2]
        self.stay, self.away = flat(keep), [flat(send)]
        self.lines = None if lines is None else flat(lines)
        self.rides = (len(fsdp) + 1 - len(halves)) if lines is not None else 0
        self.grow = grow

    def send(self):
        moves = self.moves.pop(0)
        self.received = [move(x) for move, x in zip(moves, self.away)]
        self.beside = []
        if self.rides and len(self.received[0]) == len(self.stay):
            self.beside = [moves[0](self.lines)]
        self.arriving = self.rides > 0
        self.rides = max(self.rides - 1, 0)


def add_all(chains, after=()):
    operands, shapes, plans = [], [], []
    for c in chains:
        n = c.stay.shape[0]
        parts = len(c.moves[0]) + 1 if n > c.owner_rows else 1
        part = n // parts
        held = c.lines.shape[0] if c.arriving else 0
        grown = held * (2 if c.grow else 1)
        rides = grown if c.rides else 0
        ins = [c.stay] + c.received + (c.beside + [c.lines] if held else [])
        outs = [shaped((part, c.columns), BF)]
        sends = parts - 1 if parts > 1 else int(rides > 0)
        outs += [shaped((part + rides, c.columns), BF)] * sends
        if held:
            outs.append(shaped((grown, c.columns), BF))
        plans.append((len(ins), len(outs), n, part, parts, sends, held, rides, len(c.received), len(c.beside), c.grow))
        operands += ins
        shapes += outs

    def kernel(*refs):
        sources, targets = refs[: len(operands)], refs[len(operands) :]
        for n_in, n_out, n, part, parts, sends, held, rides, arrivals, beside, grow in plans:
            ins, sources = sources[:n_in], sources[n_in:]
            outs, targets = targets[:n_out], targets[n_out:]
            received = ins[1 : 1 + arrivals]
            for p in range(parts):
                rows = slice(p * part, (p + 1) * part)
                total = ins[0][rows, :].astype(F32)
                for r in received:
                    total = total + r[rows, :].astype(F32)
                total = total.astype(BF)
                outs[p][:part, :] = total
                if parts == 1 and sends:
                    outs[1][:part, :] = total
            if held:
                mine = ins[-1][...]
                if beside:
                    others = [ins[1 + arrivals][...]]
                else:
                    others = [r[n : n + held, :] for r in received]
                if grow:
                    lines = jnp.concatenate([mine, others[0]], axis=0)
                else:
                    total = mine.astype(F32)
                    for other in others:
                        total = total + other.astype(F32)
                    lines = total.astype(BF)
                outs[-1][...] = lines
                if rides:
                    for out in outs[1 : 1 + sends]:
                        out[part:, :] = lines

    results = list(
        call(
            kernel,
            (1,),
            [whole(x.shape) for x in operands],
            [whole(x.shape) for x in shapes],
            shapes,
            us=2,
            after=after,
        )(*operands)
    )
    for c, plan in zip(chains, plans):
        n_out, sends, held = plan[1], plan[5], plan[6]
        mine, results = results[:n_out], results[n_out:]
        c.stay = mine[0]
        c.away = mine[1 : 1 + sends] if sends else [mine[0]]
        if held:
            c.lines = mine[-1]


SMALL = ("bias_qv", "bias_out", "gain_one", "shift_one", "bias_up", "bias_down", "gain_two", "shift_two")
SMALL_SIZES = (2 * D, D, D, D, FF, D, D, D)
PAD = 256


def body(
    ranks,
    replicas,
    tokens,
    lengths,
    w_qkv,
    bias_qv,
    w_out,
    bias_out,
    gain_one,
    shift_one,
    w_up,
    bias_up,
    w_down,
    bias_down,
    gain_two,
    shift_two,
    cotangent,
):
    direct = ranks == RANKS and replicas == 2
    me = lax.axis_index("fsdp")
    replica = lax.axis_index("replica")
    where = jnp.stack([me, replica]).astype(jnp.int32)
    gather = lambda w: lax.all_gather(w, "fsdp", axis=0, tiled=True)

    small = jnp.concatenate(
        [bias_qv, bias_out, gain_one, shift_one, bias_up, bias_down, gain_two, shift_two]
    )
    count = small.shape[0]
    lines = -(-count // PAD)
    small = jnp.pad(small, (0, lines * PAD - count)).reshape(lines, PAD)
    small = jnp.pad(small, ((0, w_qkv.shape[0] - lines), (0, 0)))
    first = jnp.concatenate([w_qkv, small], axis=1)
    if direct:
        w_first = gather_qkv(where, first, replica)
        packed = gather(pack_weights(w_out, w_up, w_down))
        weights = (packed.reshape(ranks, -1, D),)
    else:
        w_first = gather(first)
        weights = (gather(w_out), gather(w_up), gather(w_down))
    small_all = w_first.reshape(ranks, -1, 3 * D + PAD)[:, :lines, 3 * D :].reshape(ranks, -1)
    vectors, start = {}, 0
    for name, size in zip(SMALL, SMALL_SIZES):
        part = size // ranks
        vectors[name] = small_all[:, start : start + part].reshape(size).astype(F32)
        start += part

    bias = vectors["bias_qv"].reshape(2, GROUPS, GW).transpose(1, 0, 2)
    kept = attend_forward(lengths, tokens, w_first, bias)
    mixed = kept[4]
    vec_one = jnp.stack([vectors["bias_out"], vectors["gain_one"], vectors["shift_one"]])
    xhat, inverse, nl, active, gp = up(tokens, mixed, weights, vec_one, vectors["bias_up"][None])
    vec_two = jnp.stack(
        [vectors[n] for n in ("gain_one", "shift_one", "bias_down", "gain_two", "shift_two")]
    )
    layer_out, d_second, d_down, sums_two, pool = down(
        lengths, active, xhat, weights, vec_two, cotangent
    )
    pooled = pool / lengths.astype(F32)[:, :, None]

    terms_down = grad_down(where, active, d_down, direct)
    if direct:
        chain_w = Chain(*terms_down, pooled.astype(BF), True)
        chain_w.send()
    d_upper, sums_up = back_up(d_down, gp, weights, after=(terms_down[0],))
    if direct:
        add_all([chain_w], after=(sums_up,))
        chain_w.send()
        term_up = grad_up(nl, d_upper, after=(chain_w.away[0],))
    else:
        term_up = grad_up(nl, d_upper)
    first_args = (d_upper, d_second, xhat, inverse, weights, vectors["gain_one"][None])
    scatter = lambda x: lax.psum_scatter(x, "fsdp", scatter_dimension=0, tiled=True)

    def small_lines(sums_one, sums_a, sums_b):
        return jnp.concatenate(
            [
                jnp.concatenate([sums_a, sums_b], axis=1),
                sums_one,
                sums_up.reshape(-1, D),
                sums_two,
            ]
        )

    shard_up = scatter(term_up)
    if direct:
        d_first, d_att, sums_one = back_first(*first_args, after=(term_up,))
        attend_back = functools.partial(attend_backward, where, d_att, tokens, weights)
        dp_a, sums_a, *terms_a = attend_back((0, 1), kept, True, 2, after=(chain_w.away[0],))
        chain_a = Chain(*terms_a)
        add_all([chain_w], after=(sums_a,))
        chain_w.send()
        chain_a.send()
        dp_b, sums_b, *terms_b = attend_back((2,), kept, True, 1, after=(chain_w.away[0],))
        small = small_lines(sums_one, sums_a, sums_b)
        small = jnp.pad(small, ((0, -small.shape[0] % 16), (0, 0))).astype(BF)
        chain_b = Chain(*terms_b, small, False)
        chain_b.send()
        add_all([chain_w, chain_a], after=(sums_b,))
        chain_w.send()
        chain_a.send()
        input_grad = input_gradient(
            d_first, (dp_a, dp_b), w_first, after=(chain_a.away[0], shard_up)
        )
        add_all([chain_w, chain_a, chain_b], after=(input_grad,))
        chain_w.send()
        chain_a.send()
        chain_b.send()
        while chain_w.moves or chain_a.moves or chain_b.moves:
            moving = [c for c in (chain_w, chain_a, chain_b) if c.moves]
            add_all(moving)
            for c in moving:
                c.send()
        h0, h1 = ordered(chain_w.stay, chain_w.received[0][: chain_w.owner_rows], replica)
        grad_w_down = jnp.concatenate([h0, h1], axis=1).astype(F32)
        grad_w_up = added(shard_up, swap_replica(shard_up))
        h0, h1 = ordered(chain_a.stay, chain_a.received[0], replica)
        span = 3 * GW // 2
        halves_a = [
            jnp.concatenate([h[:, i * span : (i + 1) * span] for h in (h0, h1)], axis=1).astype(F32)
            for i in range(3)
        ]
        sum_b = added(chain_b.stay, chain_b.received[0][: chain_b.owner_rows])
        lines = added(chain_b.lines, chain_b.received[0][chain_b.owner_rows :])
        grad_w_out = halves_a[0]
        parts = halves_a[1:] + [sum_b]
        relative = chain_w.lines.reshape((2,) * 5 + pooled.shape)
        relative = relative.transpose(3, 1, 0, 2, 4, 5, 6, 7).reshape((2, ranks) + pooled.shape)
        pooled_all = relative[jnp.arange(2) ^ replica][:, me ^ jnp.arange(ranks)]
        pooled_all = pooled_all.reshape((2 * ranks * pooled.shape[0],) + pooled.shape[1:]).astype(F32)
    else:
        d_first, d_att, sums_one = back_first(*first_args)
        attend_back = functools.partial(attend_backward, where, d_att, tokens, weights)
        dp_a, sums_a, term_a = attend_back((0, 1), kept, False, 1)
        dp_b, sums_b, term_b = attend_back((2,), kept, False, 1)
        input_grad = input_gradient(d_first, (dp_a, dp_b), w_first)
        pooled_all = lax.all_gather(pooled, ("replica", "fsdp"), axis=0, tiled=True)
        reduce = lambda x: lax.psum(scatter(x), "replica").astype(F32)
        grad_w_down = reduce(terms_down[0])
        grad_w_up = lax.psum(shard_up, "replica").astype(F32)
        sum_a, sum_b = reduce(term_a), reduce(term_b)
        lines = lax.psum(small_lines(sums_one, sums_a, sums_b), ("replica", "fsdp"))
        grad_w_out = sum_a[:, :D]
        parts = [sum_a[:, D : 2 * D], sum_a[:, 2 * D :], sum_b]
    grad_w_qkv = jnp.concatenate(
        [p[:, i * GW : (i + 1) * GW] for i in range(3) for p in parts], axis=1
    )
    small_grads, start = {}, 0
    for name, size in zip(SMALL, SMALL_SIZES):
        values = lines[start // D : (start + size) // D].reshape(ranks, -1)
        small_grads[name] = lax.dynamic_index_in_dim(values, me, keepdims=False)
        start += size
    return (
        layer_out,
        input_grad,
        pooled_all,
        grad_w_qkv,
        small_grads["bias_qv"],
        grad_w_out,
        small_grads["bias_out"],
        small_grads["gain_one"],
        small_grads["shift_one"],
        grad_w_up,
        small_grads["bias_up"],
        grad_w_down,
        small_grads["bias_down"],
        small_grads["gain_two"],
        small_grads["shift_two"],
    )


def solution(mesh):
    rows = P(("replica", "fsdp"), None)
    matrix = P("fsdp", None)
    vector = P("fsdp")
    return jax.shard_map(
        functools.partial(body, mesh.shape["fsdp"], mesh.shape["replica"]),
        mesh=mesh,
        in_specs=(
            rows,
            rows,
            matrix,
            vector,
            matrix,
            vector,
            vector,
            vector,
            matrix,
            vector,
            matrix,
            vector,
            vector,
            vector,
            rows,
        ),
        out_specs=(
            rows,
            rows,
            P(),
            matrix,
            vector,
            matrix,
            vector,
            vector,
            vector,
            matrix,
            vector,
            matrix,
            vector,
            vector,
            vector,
        ),
        check_vma=False,
    )
```

```python
import functools

import jax
import jax.numpy as jnp
from jax import lax
from jax.experimental import pallas as pl
from jax.experimental.pallas import tpu as pltpu
from jax.sharding import PartitionSpec as P

D = 768
H = 12
HD = 64
FF = 3072
SEQ = 512
SEGS = 8
GROUPS = 3
GW = D // GROUPS
PAIRS = GW // 128
BLOCK = 128
BLOCKS = SEQ // BLOCK
WIDE = 3 * BLOCK

epsilon = 1e-12
root_half = 0.7071067811865476
masked_score = -1e30
pdf_scale = 0.3989422804014327

BF = jnp.bfloat16
F32 = jnp.float32
VMEM_LIMIT = 56 * 2**20


def dot(a, b):
    return jnp.dot(a, b, preferred_element_type=F32)


def dot_t(a, b):
    return lax.dot_general(a, b, (((1,), (1,)), ((), ())), preferred_element_type=F32)


def t_dot(a, b):
    return lax.dot_general(a, b, (((0,), (0,)), ((), ())), preferred_element_type=F32)


def window(qb):
    return max(0, (qb - 1) * BLOCK), min(SEQ, (qb + 2) * BLOCK)


def call(
    kernel, grid, in_specs, out_specs, out_shape, us, scratch=(), prefetch=0, after=(), aliases=None
):
    first = prefetch + len(in_specs)

    def run(*refs):
        kernel(*refs[:first], *refs[first + len(after) :])

    return functools.partial(
        lambda extra, *args: pl.pallas_call(
            run,
            grid_spec=pltpu.PrefetchScalarGridSpec(
                num_scalar_prefetch=prefetch,
                grid=grid,
                in_specs=list(in_specs) + [pl.BlockSpec(memory_space=pl.ANY)] * len(extra),
                out_specs=out_specs,
                scratch_shapes=list(scratch),
            ),
            out_shape=out_shape,
            input_output_aliases=aliases or {},
            compiler_params=pltpu.CompilerParams(vmem_limit_bytes=VMEM_LIMIT),
            cost_estimate=pl.CostEstimate(
                flops=int(us * 1.15e9), bytes_accessed=int(us * 3.6e6), transcendentals=0
            ),
        )(*args, *extra),
        tuple(after),
    )


def shaped(shape, dtype):
    return jax.ShapeDtypeStruct(shape, dtype)


def whole(shape):
    return pl.BlockSpec(shape, lambda *_: (0,) * len(shape), pipeline_mode=pl.Buffered(1))


ANY = pl.BlockSpec(memory_space=pl.ANY)


def pack_weights(where, w_qkv, small, w_out, w_up, w_down):
    r, f = w_out.shape[0], w_down.shape[0]
    columns = w_qkv.shape[1]
    half = (columns + PAD) // 2
    count = len(small)

    def kernel(where_ref, q_ref, wo_ref, wu_ref, wd_ref, *refs):
        s_refs, (out_ref, own_ref) = refs[:count], refs[count:]
        out_ref[:r, :] = wo_ref[...]
        for i in range(FF // D):
            out_ref[(1 + i) * r : (2 + i) * r, :] = wu_ref[:, i * D : (i + 1) * D]
        out_ref[5 * r :, :] = wd_ref[...]

        @pl.when(where_ref[1] == 0)
        def _():
            own_ref[...] = q_ref[:, :half]

        @pl.when(where_ref[1] > 0)
        def _():
            own_ref[:, : columns - half] = q_ref[:, half:]
            rows = []
            for s_ref in s_refs:
                v = s_ref[...].astype(F32)
                rows.append(jnp.concatenate([v, jnp.zeros((1, PAD - v.shape[1]), F32)], axis=1))
            rows.append(jnp.zeros((r - count, PAD), F32))
            own_ref[:, columns - half :] = jnp.concatenate(rows, axis=0).astype(BF)

    operands = (w_qkv, w_out, w_up, w_down) + tuple(v[None] for v in small)
    shapes = [shaped((5 * r + f, D), BF), shaped((r, half), BF)]
    return call(
        kernel,
        (1,),
        [whole(x.shape) for x in operands],
        [whole(x.shape) for x in shapes],
        shapes,
        us=2,
        prefetch=1,
    )(where, *operands)


def weight_copies(name, refs, target, sems):
    if len(refs) == 3:
        source = refs[("out", "up", "down").index(name)]
        return [pltpu.make_async_copy(source, target, sems.at[0])]
    packed = refs[0]
    ranks = packed.shape[0]
    r = D // ranks
    copies = []
    for o in range(ranks):
        if name == "out":
            parts = [(slice(0, r), target.at[o * r : (o + 1) * r])]
        elif name == "up":
            parts = [
                (
                    slice((1 + i) * r, (2 + i) * r),
                    target.at[o * r : (o + 1) * r, i * D : (i + 1) * D],
                )
                for i in range(FF // D)
            ]
        else:
            n = FF // ranks
            parts = [(slice(5 * r, 5 * r + n), target.at[o * n : (o + 1) * n])]
        for rows, where in parts:
            copies.append(pltpu.make_async_copy(packed.at[o, rows], where, sems.at[len(copies)]))
    return copies


def start_all(copies):
    for copy in copies:
        copy.start()


def wait_all(copies):
    for copy in copies:
        copy.wait()


def segment_of(places, lengths_ref, row):
    total = jnp.int32(0)
    segment = jnp.zeros(places.shape, jnp.int32)
    for s in range(SEGS):
        total = total + lengths_ref[row, s]
        segment = segment + (places >= total).astype(jnp.int32)
    return segment


def both_heads(x2):
    low = lax.broadcasted_iota(jnp.int32, (1, 128), 1) < HD
    zero = jnp.zeros_like(x2)
    return jnp.concatenate([jnp.where(low, x2, zero), jnp.where(low, zero, x2)], axis=0)


def attend_forward_kernel(
    lengths_ref, tok_ref, wq_ref, wk_ref, wv_ref, bias_ref, q_ref, k_ref, v_ref, p_ref, m_ref, vt, ot
):
    row = pl.program_id(1)
    tok = tok_ref[...]
    q_ref[...] = (dot(tok, wq_ref[...]) + bias_ref[0, 0:1, :]).astype(BF) * jnp.asarray(0.125, BF)
    k_ref[...] = dot(tok, wk_ref[...]).astype(BF)
    v = dot(tok, wv_ref[...]) + bias_ref[0, 1:2, :]
    v_ref[...] = v.astype(BF)
    vt[...] = v.T.astype(BF)
    for qb in range(BLOCKS):
        lo, hi = window(qb)
        width = hi - lo
        rows = slice(qb * BLOCK, (qb + 1) * BLOCK)
        seg_q = segment_of(
            lax.broadcasted_iota(jnp.int32, (1, BLOCK), 1) + qb * BLOCK, lengths_ref, row
        )
        seg_k = segment_of(
            lax.broadcasted_iota(jnp.int32, (width, 1), 0) + lo, lengths_ref, row
        )
        mask = jnp.where(jnp.concatenate([seg_q, seg_q], axis=1) == seg_k, 0.0, masked_score)
        for pair in range(PAIRS):
            lanes = slice(pair * 128, (pair + 1) * 128)
            s = dot_t(k_ref[lo:hi, lanes], both_heads(q_ref[rows, lanes])) + mask
            w = jnp.exp(s - jnp.max(s, axis=0, keepdims=True))
            p = (w * (1.0 / jnp.sum(w, axis=0, keepdims=True))).astype(BF)
            p_ref[0, pair, qb, :width, :] = p
            o = dot(vt[lanes, lo:hi], p)
            ot[pair * 128 : pair * 128 + HD, rows] = o[:HD, :BLOCK]
            ot[pair * 128 + HD : (pair + 1) * 128, rows] = o[HD:, BLOCK:]
    m_ref[...] = ot[...].T.astype(BF)


def attend_forward(lengths, tokens, w_qkv, bias, after=()):
    t = tokens.shape[0]
    rows = t // SEQ
    row_spec = pl.BlockSpec((SEQ, GW), lambda g, r, *_: (r, g))
    p_shape = (GROUPS * rows, PAIRS, BLOCKS, WIDE, 2 * BLOCK)
    column = lambda part: pl.BlockSpec((D, GW), lambda g, r, *_: (0, part * GROUPS + g))
    return call(
        attend_forward_kernel,
        (GROUPS, rows),
        [
            pl.BlockSpec((SEQ, D), lambda g, r, *_: (r, 0)),
            column(0),
            column(1),
            column(2),
            pl.BlockSpec((1, 2, GW), lambda g, r, *_: (g, 0, 0)),
        ],
        [row_spec] * 3
        + [pl.BlockSpec((1,) + p_shape[1:], lambda g, r, *_: (g * rows + r, 0, 0, 0, 0)), row_spec],
        [shaped((t, D), BF)] * 3 + [shaped(p_shape, BF), shaped((t, D), BF)],
        us=28,
        scratch=[pltpu.VMEM((GW, SEQ), BF), pltpu.VMEM((GW, SEQ), F32)],
        prefetch=1,
        after=after,
    )(lengths, tokens, w_qkv, w_qkv, w_qkv, bias)


def attend_backward_kernel(
    groups, direct, halves, where_ref, datt_ref, tok_ref, m_ref, wrefs, q_ref, k_ref, v_ref, p_ref, dp_ref,
    sums_ref, wg_refs, wo, kt, qt, dk_acc, dv_acc, dw_acc, dw_low, wsems, sems,
):
    g = pl.program_id(0)
    row = pl.program_id(1)
    first = groups[0]
    with_out = 0
    last = pl.num_programs(1) - 1
    span = 3 * GW

    def emit(place):
        if direct:
            part = span // halves
            copies = term_copies(
                where_ref,
                lambda owner_rows, h: dw_low.at[owner_rows, h * part : (h + 1) * part],
                D,
                lambda ref, where: ref.at[
                    where + (slice(None), pl.ds(pl.multiple_of(place * part, 128), part))
                ],
                wg_refs,
                sems,
                halves,
            )
        else:
            where = pl.ds(pl.multiple_of(place * span, 128), span)
            copies = [pltpu.make_async_copy(dw_low, wg_refs[0].at[:, where], sems.at[0])]
        start_all(copies)
        wait_all(copies)

    def add_term(term, place):
        @pl.when(row == 0)
        def _():
            dw_acc[...] = term

        @pl.when((row > 0) & (row < last))
        def _():
            dw_acc[...] += term

        @pl.when(row == last)
        def _():
            dw_low[...] = (dw_acc[...] + term).astype(BF)
            emit(place)

    if with_out:

        @pl.when(g == 0)
        def _():
            add_term(t_dot(m_ref[...], datt_ref[...]), 0)

    @pl.when((g == with_out) & (row == 0))
    def _():
        copies = weight_copies("out", wrefs, wo, wsems)
        start_all(copies)
        wait_all(copies)

    def group_step():
        place = g - with_out
        wo_rows = wo[pl.ds(pl.multiple_of((place + first) * GW, GW), GW), :]
        dmix = dot_t(datt_ref[...], wo_rows).astype(BF)
        kt[...] = k_ref[...].astype(F32).T.astype(BF)
        dk_acc[...] = jnp.zeros_like(dk_acc)
        dv_acc[...] = jnp.zeros_like(dv_acc)
        for qb in range(BLOCKS):
            lo, hi = window(qb)
            width = hi - lo
            rows = slice(qb * BLOCK, (qb + 1) * BLOCK)
            for pair in range(PAIRS):
                lanes = slice(pair * 128, (pair + 1) * 128)
                dos = both_heads(dmix[rows, lanes])
                p_low = p_ref[0, pair, qb, :width, :]
                p = p_low.astype(F32)
                dp = dot_t(v_ref[lo:hi, lanes], dos)
                delta = jnp.sum(p * dp, axis=0, keepdims=True)
                ds = (p * (dp - delta)).astype(BF)
                dk_acc[lo:hi, lanes] += dot(ds, both_heads(q_ref[rows, lanes]))
                dv_acc[lo:hi, lanes] += dot(p_low, dos)
                dq = dot(kt[lanes, lo:hi], ds)
                qt[pair * 128 : pair * 128 + HD, rows] = dq[:HD, :BLOCK]
                qt[pair * 128 + HD : (pair + 1) * 128, rows] = dq[HD:, BLOCK:]
        dq = (qt[...] * 0.125).T.astype(BF)
        dv = dv_acc[...].astype(BF)
        dp_ref[:, :GW] = dq
        dp_ref[:, GW : 2 * GW] = dk_acc[...].astype(BF)
        dp_ref[:, 2 * GW :] = dv
        sums = jnp.concatenate(
            [
                jnp.sum(dq.astype(F32), axis=0, keepdims=True),
                jnp.sum(dv.astype(F32), axis=0, keepdims=True),
            ],
            axis=0,
        )
        sums_ref[...] = jnp.where(row == 0, sums, sums_ref[...] + sums)
        add_term(t_dot(tok_ref[...], dp_ref[...]), g)

    if with_out:
        pl.when(g > 0)(group_step)
    else:
        group_step()


RANKS = 16


def term_copies(where_ref, source, total_rows, target, refs, sems, halves):
    me, replica = where_ref[0], where_ref[1]
    rows = total_rows // RANKS
    copies = []
    for j in range(RANKS):
        owner_rows = pl.ds(pl.multiple_of((me ^ j) * rows, rows), rows)
        place = ((j >> 1) & 1, j >> 2)
        for h in range(halves):
            where = ((h ^ replica,) if halves == 2 else ()) + place
            copies.append(
                pltpu.make_async_copy(
                    source(owner_rows, h), target(refs[j & 1], where), sems.at[halves * j + h]
                )
            )
    return copies


def attend_backward(where, datt, tokens, weights, groups, kept, direct, halves, after=()):
    q, k, v, p, mixed = kept
    t = datt.shape[0]
    rows = t // SEQ
    count, first = len(groups), groups[0]
    extra = 0
    group = lambda g: jnp.maximum(g - extra, 0) + first
    row_spec = pl.BlockSpec((SEQ, GW), lambda g, r, *_: (r, group(g)))
    full_row = pl.BlockSpec((SEQ, D), lambda g, r, *_: (r, 0))
    columns = (count + extra) * 3 * GW
    if direct:
        lead = (2, 2, 4) if halves == 2 else (2, 4)
        wg_shapes = [shaped(lead + (D // RANKS, columns // halves), BF)] * 2
    else:
        wg_shapes = [shaped((D, columns), BF)]
    nw, ng = len(weights), len(wg_shapes)

    def kernel(where_ref, datt_ref, tok_ref, m_ref, *refs):
        wrefs, refs = refs[:nw], refs[nw:]
        q_ref, k_ref, v_ref, p_ref, dp_ref, sums_ref = refs[:6]
        wg_refs, scratch = refs[6 : 6 + ng], refs[6 + ng :]
        attend_backward_kernel(
            groups, direct, halves, where_ref, datt_ref, tok_ref, m_ref, wrefs, q_ref, k_ref, v_ref, p_ref,
            dp_ref, sums_ref, wg_refs, *scratch,
        )

    m_spec = pl.BlockSpec((SEQ, D), lambda g, r, *_: (jnp.where(g == 0, r, rows - 1), 0))
    return call(
        kernel,
        (count + extra, rows),
        [full_row, full_row, m_spec if extra else ANY]
        + [ANY] * nw
        + [
            row_spec,
            row_spec,
            row_spec,
            pl.BlockSpec((1,) + p.shape[1:], lambda g, r, *_: (group(g) * rows + r, 0, 0, 0, 0)),
        ],
        [
            pl.BlockSpec(
                (SEQ, 3 * GW), lambda g, r, *_: (jnp.where(g < extra, 0, r), jnp.maximum(g - extra, 0))
            ),
            pl.BlockSpec((2, GW), lambda g, r, *_: (0, jnp.maximum(g - extra, 0))),
        ]
        + [ANY] * ng,
        [shaped((t, count * 3 * GW), BF), shaped((2, count * GW), F32)] + wg_shapes,
        us=1,
        scratch=[
            pltpu.VMEM((D, D), BF),
            pltpu.VMEM((GW, SEQ), BF),
            pltpu.VMEM((GW, SEQ), F32),
            pltpu.VMEM((SEQ, GW), F32),
            pltpu.VMEM((SEQ, GW), F32),
            pltpu.VMEM((D, 3 * GW), F32),
            pltpu.VMEM((D, 3 * GW), BF),
            pltpu.SemaphoreType.DMA((16,)),
            pltpu.SemaphoreType.DMA((2 * RANKS,)),
        ],
        prefetch=1,
        after=after,
    )(where, datt, tokens, mixed, *weights, q, k, v, p)


TB = 256
CH = 768


def normalize(values):
    centered = values - jnp.mean(values, axis=-1, keepdims=True)
    variance = jnp.mean(centered * centered, axis=-1, keepdims=True)
    inverse = lax.rsqrt(variance + epsilon)
    return centered * inverse, inverse


def normalize_back(grad, xhat, inverse):
    mean = jnp.mean(grad, axis=-1, keepdims=True)
    along = jnp.mean(grad * xhat, axis=-1, keepdims=True)
    return (grad - mean - xhat * along) * inverse


def add_rows(ref, rows):
    stacked = jnp.concatenate([jnp.sum(r, axis=0, keepdims=True) for r in rows], axis=0)
    ref[...] = jnp.where(pl.program_id(0) == 0, stacked, ref[...] + stacked)


def middle(lengths, tokens, mixed, weights, vec, bias_up, cot, after=()):
    t = tokens.shape[0]
    nw = len(weights)
    per_row = SEQ // TB

    def kernel(lengths_ref, tok_ref, m_ref, vec_ref, bu_ref, cot_ref, *refs):
        wrefs, refs = refs[:nw], refs[nw:]
        out_ref, nl_ref, act_ref, dd_ref, du_ref, df_ref, da_ref, sums_ref, su_ref, pool_ref = refs[:10]
        wo, wu, wd, gp, so, su, sd = refs[10:]
        i = pl.program_id(0)
        out_copies = weight_copies("out", wrefs, wo, so)
        up_copies = weight_copies("up", wrefs, wu, su)
        down_copies = weight_copies("down", wrefs, wd, sd)

        @pl.when(i == 0)
        def _():
            start_all(out_copies)
            start_all(up_copies)
            start_all(down_copies)
            wait_all(out_copies)

        att = dot(m_ref[...], wo[...]) + vec_ref[0:1, :]
        xhat, inverse = normalize(tok_ref[...].astype(F32) + att)
        normed = xhat * vec_ref[1:2, :] + vec_ref[2:3, :]
        nl = normed.astype(BF)
        nl_ref[...] = nl

        @pl.when(i == 0)
        def _():
            wait_all(up_copies)

        for c in range(0, FF, CH):
            u = dot(nl, wu[:, c : c + CH]) + bu_ref[:, c : c + CH]
            cdf = 0.5 * (1.0 + lax.erf(u * root_half))
            act_ref[:, c : c + CH] = (u * cdf).astype(BF)
            gp[:, c : c + CH] = cdf + u * (jnp.exp(u * u * -0.5) * pdf_scale)

        @pl.when(i == 0)
        def _():
            wait_all(down_copies)

        second = normed + (dot(act_ref[...], wd[...]) + vec_ref[3:4, :])
        xhat_two, inverse_two = normalize(second)
        out = (xhat_two * vec_ref[4:5, :] + vec_ref[5:6, :]).astype(BF)
        out_ref[...] = out
        cot = cot_ref[...].astype(F32)
        d_second = normalize_back(cot * vec_ref[4:5, :], xhat_two, inverse_two)
        dd = d_second.astype(BF)
        dd_ref[...] = dd
        row = i // per_row
        places = lax.broadcasted_iota(jnp.int32, (1, TB), 1) + (i % per_row) * TB
        segment = segment_of(places, lengths_ref, row)
        ids = lax.broadcasted_iota(jnp.int32, (SEGS, TB), 0)
        pooled = dot(jnp.where(segment == ids, 1.0, 0.0).astype(BF), out)
        pool_ref[0] = jnp.where(i % per_row == 0, pooled, pool_ref[0] + pooled)
        for c in range(0, FF, CH):
            du = (dot_t(dd, wd[c : c + CH, :]) * gp[:, c : c + CH]).astype(BF)
            du_ref[:, c : c + CH] = du
            partial = jnp.sum(du.astype(F32), axis=0, keepdims=True)
            su_ref[:, c : c + CH] = jnp.where(i == 0, partial, su_ref[:, c : c + CH] + partial)
        d_normed = d_second + dot_t(du_ref[...], wu[...])
        d_first = normalize_back(d_normed * vec_ref[1:2, :], xhat, inverse)
        df_ref[...] = d_first
        d_att = d_first.astype(BF)
        da_ref[...] = d_att
        add_rows(
            sums_ref,
            (dd.astype(F32), cot * xhat_two, cot, d_att.astype(F32), d_normed * xhat, d_normed),
        )

    tok = lambda n: pl.BlockSpec((TB, n), lambda i, *_: (i, 0))
    return call(
        kernel,
        (t // TB,),
        [tok(D), tok(D), whole((6, D)), whole((1, FF)), tok(D)] + [ANY] * nw,
        [
            tok(D),
            tok(D),
            tok(FF),
            tok(D),
            tok(FF),
            tok(D),
            tok(D),
            pl.BlockSpec((6, D), lambda i, *_: (0, 0)),
            pl.BlockSpec((1, FF), lambda i, *_: (0, 0)),
            pl.BlockSpec((1, SEGS, D), lambda i, *_: (i // per_row, 0, 0)),
        ],
        [
            shaped((t, D), BF),
            shaped((t, D), BF),
            shaped((t, FF), BF),
            shaped((t, D), BF),
            shaped((t, FF), BF),
            shaped((t, D), F32),
            shaped((t, D), BF),
            shaped((6, D), F32),
            shaped((1, FF), F32),
            shaped((t // SEQ, SEGS, D), F32),
        ],
        us=45,
        scratch=[
            pltpu.VMEM((D, D), BF),
            pltpu.VMEM((D, FF), BF),
            pltpu.VMEM((FF, D), BF),
            pltpu.VMEM((TB, FF), F32),
            pltpu.SemaphoreType.DMA((16,)),
            pltpu.SemaphoreType.DMA((64,)),
            pltpu.SemaphoreType.DMA((16,)),
        ],
        prefetch=1,
        after=after,
    )(lengths, tokens, mixed, vec, bias_up, cot, *weights)


def input_gradient(d_first, d_projected, w_qkv, after=()):
    t = d_first.shape[0]

    def kernel(df_ref, p0, p1, w_ref, out_ref):
        total = df_ref[...]
        g = 0
        for p in (p0, p1):
            for local in range(p.shape[1] // D):
                for part in range(3):
                    start = part * D + g * GW
                    at = local * D + part * GW
                    total = total + dot_t(p[:, at : at + GW], w_ref[:, start : start + GW])
                g += 1
        out_ref[...] = total

    tok = lambda n: pl.BlockSpec((TB, n), lambda i: (i, 0))
    return call(
        kernel,
        (t // TB,),
        [tok(D), tok(d_projected[0].shape[1]), tok(d_projected[1].shape[1]), whole((D, 3 * D))],
        tok(D),
        shaped((t, D), F32),
        us=9,
        after=after,
    )(d_first, *d_projected, w_qkv)


def grad_down(active, d_down, after=()):
    t = d_down.shape[0]
    n = 768

    def kernel(a_ref, b_ref, out_ref):
        out_ref[...] = t_dot(a_ref[...], b_ref[...]).astype(BF)

    return call(
        kernel,
        (FF // n,),
        [pl.BlockSpec((t, n), lambda i: (0, i)), whole((t, D))],
        pl.BlockSpec((n, D), lambda i: (i, 0)),
        shaped((FF, D), BF),
        us=9,
        after=after,
    )(active, d_down)


STRIP = 384
STRIPS = (FF + D) // 2 // STRIP


def grad_up_out(where, nl, d_upper, mixed, d_att, direct, after=()):
    t = nl.shape[0]

    def kernel(where_ref, nl_ref, du_ref, m_ref, da_ref, *refs):
        outs, (acc, sems) = refs[:-2], refs[-2:]
        h = pl.program_id(0)
        acc[h, :, : FF // 2] = t_dot(nl_ref[...], du_ref[...]).astype(BF)
        acc[h, :, FF // 2 :] = t_dot(m_ref[...], da_ref[...]).astype(BF)

        def copies_of(h):
            if not direct:
                return [pltpu.make_async_copy(acc.at[h], outs[0].at[h], sems.at[h, 0])]
            me, replica = where_ref[0], where_ref[1]
            rows = D // RANKS
            copies = []
            for j in range(RANKS):
                owner_rows = pl.ds(pl.multiple_of((me ^ j) * rows, rows), rows)
                for strip in range(STRIPS):
                    target = outs[j & 1].at[
                        h ^ replica, (j >> 1) & 1, j >> 2, strip * rows : (strip + 1) * rows
                    ]
                    source = acc.at[h, owner_rows, strip * STRIP : (strip + 1) * STRIP]
                    copies.append(pltpu.make_async_copy(source, target, sems.at[h, len(copies)]))
            return copies

        start_all(copies_of(h))

        @pl.when(h == 1)
        def _():
            wait_all(copies_of(0))
            wait_all(copies_of(1))

    if direct:
        out_shapes = [shaped((2, 2, 4, STRIPS * D // RANKS, STRIP), BF)] * 2
    else:
        out_shapes = [shaped((2, D, (FF + D) // 2), BF)]
    return call(
        kernel,
        (2,),
        [
            whole((t, D)),
            pl.BlockSpec((t, FF // 2), lambda h, *_: (0, h)),
            whole((t, D)),
            pl.BlockSpec((t, D // 2), lambda h, *_: (0, h)),
        ],
        [ANY] * len(out_shapes),
        out_shapes,
        us=13,
        scratch=[
            pltpu.VMEM((2, D, (FF + D) // 2), BF),
            pltpu.SemaphoreType.DMA((2, RANKS * STRIPS)),
        ],
        prefetch=1,
        after=after,
    )(where, nl, d_upper, mixed, d_att)


def swap(x, mask):
    return lax.ppermute(x, "fsdp", [(i, i ^ mask) for i in range(RANKS)])


def swap_replica(x):
    return lax.ppermute(x, "replica", [(0, 1), (1, 0)])


def added(*terms):
    total = terms[0].astype(F32)
    for term in terms[1:]:
        total = total + term.astype(F32)
    return total


def gather_qkv(where, own):
    rows, half = own.shape
    columns = 2 * half
    z = jnp.stack([own] + [swap(own, m) for m in (4, 8, 12)])
    zy = jnp.stack([z, swap(z, 2)])
    x = swap_replica(zy)
    pieces = (zy, x, swap(zy, 1), swap(x, 1))

    def kernel(where_ref, p0, p1, p2, p3, out_ref, sems):
        me, other = where_ref[0], where_ref[1]
        copies = []
        for index, piece in enumerate((p0, p1, p2, p3)):
            start = pl.multiple_of((other ^ (index % 2)) * half, 128)
            for y in range(2):
                for k in range(4):
                    owner = me ^ (4 * k + 2 * y + index // 2)
                    target = out_ref.at[
                        pl.ds(pl.multiple_of(owner * rows, rows), rows), pl.ds(start, half)
                    ]
                    copies.append(
                        pltpu.make_async_copy(piece.at[y, k], target, sems.at[len(copies)])
                    )
        start_all(copies)
        wait_all(copies)

    return call(
        kernel,
        (1,),
        [ANY] * 4,
        pl.BlockSpec((RANKS * rows, columns), lambda *_: (0, 0)),
        shaped((RANKS * rows, columns), BF),
        us=4,
        scratch=[pltpu.SemaphoreType.DMA((32,))],
        prefetch=1,
    )(where, *pieces)


def ordered(own, other, replica):
    first = jnp.where(replica == 0, own, other)
    second = jnp.where(replica == 0, other, own)
    return first, second


class Chain:
    def __init__(self, keep, send, lines=None, two_steps=False):
        self.columns = keep.shape[-1]
        flat = lambda x: x.reshape(-1, self.columns)
        halves = [(swap_replica,)] if keep.ndim == 5 else []
        over = lambda m: lambda x: swap(x, m)
        along_z = [(over(8),), (over(4),)] if two_steps else [(over(4), over(8), over(12))]
        fsdp = [(over(1),)] + halves + [(over(2),)] + along_z
        self.moves = fsdp + [(swap_replica,)]
        self.owner_rows = keep.shape[-2]
        self.stay, self.away = flat(keep), [flat(send)]
        self.lines = None if lines is None else flat(lines)
        self.rides = (len(fsdp) + 1 - len(halves)) if lines is not None else 0

    def send(self):
        moves = self.moves.pop(0)
        self.received = [move(x) for move, x in zip(moves, self.away)]
        self.beside = []
        if self.rides and len(self.received[0]) == len(self.stay):
            self.beside = [moves[0](self.lines)]
        self.arriving = self.rides > 0
        self.rides = max(self.rides - 1, 0)


def add_all(chains, after=(), passing=()):
    operands, shapes, plans = [], [], []
    for c in chains:
        n = c.stay.shape[0]
        parts = len(c.moves[0]) + 1 if n > c.owner_rows else 1
        part = n // parts
        held = c.lines.shape[0] if c.arriving else 0
        rides = held if c.rides else 0
        ins = [c.stay] + c.received + (c.beside + [c.lines] if held else [])
        outs = [shaped((part, c.columns), BF)]
        sends = parts - 1 if parts > 1 else int(rides > 0)
        outs += [shaped((part + rides, c.columns), BF)] * sends
        if held:
            outs.append(shaped((held, c.columns), BF))
        plans.append((len(ins), len(outs), n, part, parts, sends, held, rides, len(c.received), len(c.beside)))
        operands += ins
        shapes += outs

    passed, inputs = len(passing), len(operands)

    def kernel(*refs):
        sources, targets = refs[: len(operands)], refs[len(operands) + passed :]
        for n_in, n_out, n, part, parts, sends, held, rides, arrivals, beside in plans:
            ins, sources = sources[:n_in], sources[n_in:]
            outs, targets = targets[:n_out], targets[n_out:]
            received = ins[1 : 1 + arrivals]
            for p in range(parts):
                rows = slice(p * part, (p + 1) * part)
                total = ins[0][rows, :].astype(F32)
                for r in received:
                    total = total + r[rows, :].astype(F32)
                total = total.astype(BF)
                outs[p][:part, :] = total
                if parts == 1 and sends:
                    outs[1][:part, :] = total
            if held:
                mine = ins[-1][...]
                if beside:
                    others = [ins[1 + arrivals][...]]
                else:
                    others = [r[n : n + held, :] for r in received]
                total = mine.astype(F32)
                for other in others:
                    total = total + other.astype(F32)
                lines = total.astype(BF)
                outs[-1][...] = lines
                if rides:
                    for out in outs[1 : 1 + sends]:
                        out[part:, :] = lines

    results = list(
        call(
            kernel,
            (1,),
            [whole(x.shape) for x in operands] + [ANY] * passed,
            [whole(x.shape) for x in shapes] + [ANY] * passed,
            shapes + [shaped(x.shape, x.dtype) for x in passing],
            us=2,
            after=after,
            aliases={inputs + i: len(shapes) + i for i in range(passed)},
        )(*operands, *passing)
    )
    for c, plan in zip(chains, plans):
        n_out, sends, held = plan[1], plan[5], plan[6]
        mine, results = results[:n_out], results[n_out:]
        c.stay = mine[0]
        c.away = mine[1 : 1 + sends] if sends else [mine[0]]
        if held:
            c.lines = mine[-1]
    return results


SMALL = ("bias_qv", "bias_out", "gain_one", "shift_one", "bias_up", "bias_down", "gain_two", "shift_two")
SMALL_SIZES = (2 * D, D, D, D, FF, D, D, D)
PAD = 256


def body(
    ranks,
    replicas,
    tokens,
    lengths,
    w_qkv,
    bias_qv,
    w_out,
    bias_out,
    gain_one,
    shift_one,
    w_up,
    bias_up,
    w_down,
    bias_down,
    gain_two,
    shift_two,
    cotangent,
):
    direct = ranks == RANKS and replicas == 2
    me = lax.axis_index("fsdp")
    replica = lax.axis_index("replica")
    where = jnp.stack([me, replica]).astype(jnp.int32)
    gather = lambda w: lax.all_gather(w, "fsdp", axis=0, tiled=True)

    small = (bias_qv, bias_out, gain_one, shift_one, bias_up, bias_down, gain_two, shift_two)
    if direct:
        packed, own = pack_weights(where, w_qkv, small, w_out, w_up, w_down)
        w_first = gather_qkv(where, own)
        weights = (gather(packed).reshape(ranks, -1, D),)
    else:
        w_first = gather(w_qkv)
        weights = (gather(w_out), gather(w_up), gather(w_down))
    vectors = {}
    if direct:
        beside = w_first[:, 3 * D :].reshape(ranks, -1, PAD)
    for k, (name, value) in enumerate(zip(SMALL, small)):
        got = beside[:, k, : value.shape[0]].reshape(-1) if direct else gather(value)
        vectors[name] = got.astype(F32)

    bias = vectors["bias_qv"].reshape(2, GROUPS, GW).transpose(1, 0, 2)
    kept = attend_forward(lengths, tokens, w_first, bias)
    mixed = kept[4]
    vec = jnp.stack(
        [
            vectors[n]
            for n in ("bias_out", "gain_one", "shift_one", "bias_down", "gain_two", "shift_two")
        ]
    )
    (layer_out, nl, active, d_down, d_upper, d_first, d_att, sums, sums_up, pool) = middle(
        lengths, tokens, mixed, weights, vec, vectors["bias_up"][None], cotangent
    )
    pooled = pool / lengths.astype(F32)[:, :, None]

    terms_up = grad_up_out(where, nl, d_upper, mixed, d_att, direct)
    term_down = grad_down(active, d_down, after=(terms_up[0],))
    scatter = lambda x: lax.psum_scatter(x, "fsdp", scatter_dimension=0, tiled=True)

    def small_lines(sums_a, sums_b):
        both = jnp.concatenate([sums_a, sums_b], axis=1)
        return jnp.concatenate([both, sums[3:], sums_up.reshape(-1, D), sums[:3]])

    shard_down = scatter(term_down)
    attend_back = functools.partial(attend_backward, where, d_att, tokens, weights)
    if direct:
        chain_u = Chain(*terms_up, two_steps=True)
        chain_u.send()
        add_all([chain_u], after=(term_down,))
        chain_u.send()
        dp_a, sums_a, *terms_a = attend_back((0, 1), kept, True, 2, after=(chain_u.away[0],))
        chain_a = Chain(*terms_a)
        chain_a.away[0], pooled = add_all([chain_u], after=(sums_a,), passing=(chain_a.away[0], pooled))
        pooled_all = lax.all_gather(pooled, ("replica", "fsdp"), axis=0, tiled=True)
        chain_u.send()
        chain_a.send()
        add_all([chain_a])
        chain_a.send()
        dp_b, sums_b, *terms_b = attend_back((2,), kept, True, 1, after=(chain_a.away[0],))
        small = small_lines(sums_a, sums_b)
        small = jnp.pad(small, ((0, -small.shape[0] % 16), (0, 0))).astype(BF)
        chain_b = Chain(*terms_b, small)
        chain_b.send()
        add_all([chain_u, chain_a], after=(sums_b,))
        chain_u.send()
        chain_a.send()
        input_grad = input_gradient(
            d_first, (dp_a, dp_b), w_first, after=(chain_a.away[0],)
        )
        add_all([chain_u, chain_a, chain_b], after=(input_grad,))
        chain_u.send()
        chain_a.send()
        chain_b.send()
        while chain_u.moves or chain_a.moves or chain_b.moves:
            moving = [c for c in (chain_u, chain_a, chain_b) if c.moves]
            add_all(moving, after=(shard_down,) if len(moving) > 1 else (shard_down, pooled_all))
            for c in moving:
                c.send()
        halves_u = ordered(chain_u.stay, chain_u.received[0][: chain_u.owner_rows], replica)
        halves_u = [
            h.reshape(STRIPS, -1, STRIP).transpose(1, 0, 2).reshape(-1, STRIPS * STRIP)
            for h in halves_u
        ]
        grad_w_down = added(shard_down, swap_replica(shard_down))
        h0, h1 = ordered(chain_a.stay, chain_a.received[0], replica)
        span = 3 * GW // 2
        halves_a = [
            jnp.concatenate([h[:, i * span : (i + 1) * span] for h in (h0, h1)], axis=1).astype(F32)
            for i in range(2)
        ]
        sum_b = added(chain_b.stay, chain_b.received[0][: chain_b.owner_rows])
        lines = added(chain_b.lines, chain_b.received[0][chain_b.owner_rows :])
        parts = halves_a + [sum_b]
    else:
        dp_a, sums_a, term_a = attend_back((0, 1), kept, False, 1)
        dp_b, sums_b, term_b = attend_back((2,), kept, False, 1)
        input_grad = input_gradient(d_first, (dp_a, dp_b), w_first)
        pooled_all = lax.all_gather(pooled, ("replica", "fsdp"), axis=0, tiled=True)
        reduce = lambda x: lax.psum(scatter(x), "replica").astype(F32)
        grad_w_down = lax.psum(shard_down, "replica").astype(F32)
        halves_u = [reduce(terms_up[0][h]) for h in range(2)]
        sum_a, sum_b = reduce(term_a), reduce(term_b)
        lines = lax.psum(small_lines(sums_a, sums_b), ("replica", "fsdp"))
        parts = [sum_a[:, :D], sum_a[:, D:], sum_b]
    grad_w_up = jnp.concatenate([h[:, : FF // 2] for h in halves_u], axis=1).astype(F32)
    grad_w_out = jnp.concatenate([h[:, FF // 2 :] for h in halves_u], axis=1).astype(F32)
    grad_w_qkv = jnp.concatenate(
        [p[:, i * GW : (i + 1) * GW] for i in range(3) for p in parts], axis=1
    )
    small_grads, start = {}, 0
    for name, size in zip(SMALL, SMALL_SIZES):
        values = lines[start // D : (start + size) // D].reshape(ranks, -1)
        small_grads[name] = lax.dynamic_index_in_dim(values, me, keepdims=False)
        start += size
    return (
        layer_out,
        input_grad,
        pooled_all,
        grad_w_qkv,
        small_grads["bias_qv"],
        grad_w_out,
        small_grads["bias_out"],
        small_grads["gain_one"],
        small_grads["shift_one"],
        grad_w_up,
        small_grads["bias_up"],
        grad_w_down,
        small_grads["bias_down"],
        small_grads["gain_two"],
        small_grads["shift_two"],
    )


def solution(mesh):
    rows = P(("replica", "fsdp"), None)
    matrix = P("fsdp", None)
    vector = P("fsdp")
    return jax.shard_map(
        functools.partial(body, mesh.shape["fsdp"], mesh.shape["replica"]),
        mesh=mesh,
        in_specs=(
            rows,
            rows,
            matrix,
            vector,
            matrix,
            vector,
            vector,
            vector,
            matrix,
            vector,
            matrix,
            vector,
            vector,
            vector,
            rows,
        ),
        out_specs=(
            rows,
            rows,
            P(),
            matrix,
            vector,
            matrix,
            vector,
            vector,
            vector,
            matrix,
            vector,
            matrix,
            vector,
            vector,
            vector,
        ),
        check_vma=False,
    )
```

```python
import functools

import jax
import jax.numpy as jnp
from jax import lax
from jax.experimental import pallas as pl
from jax.experimental.pallas import tpu as pltpu
from jax.sharding import PartitionSpec as P

D = 768
H = 12
HD = 64
FF = 3072
SEQ = 512
SEGS = 8
GROUPS = 3
GW = D // GROUPS
PAIRS = GW // 128
BLOCK = 128
BLOCKS = SEQ // BLOCK
WIDE = 3 * BLOCK

epsilon = 1e-12
root_half = 0.7071067811865476
masked_score = -1e30
pdf_scale = 0.3989422804014327

BF = jnp.bfloat16
F32 = jnp.float32
VMEM_LIMIT = 56 * 2**20


def dot(a, b):
    return jnp.dot(a, b, preferred_element_type=F32)


def dot_t(a, b):
    return lax.dot_general(a, b, (((1,), (1,)), ((), ())), preferred_element_type=F32)


def t_dot(a, b):
    return lax.dot_general(a, b, (((0,), (0,)), ((), ())), preferred_element_type=F32)


def window(qb):
    return max(0, (qb - 1) * BLOCK), min(SEQ, (qb + 2) * BLOCK)


def call(
    kernel, grid, in_specs, out_specs, out_shape, us, scratch=(), prefetch=0, after=(), aliases=None
):
    first = prefetch + len(in_specs)

    def run(*refs):
        kernel(*refs[:first], *refs[first + len(after) :])

    return functools.partial(
        lambda extra, *args: pl.pallas_call(
            run,
            grid_spec=pltpu.PrefetchScalarGridSpec(
                num_scalar_prefetch=prefetch,
                grid=grid,
                in_specs=list(in_specs) + [pl.BlockSpec(memory_space=pl.ANY)] * len(extra),
                out_specs=out_specs,
                scratch_shapes=list(scratch),
            ),
            out_shape=out_shape,
            input_output_aliases=aliases or {},
            compiler_params=pltpu.CompilerParams(vmem_limit_bytes=VMEM_LIMIT),
            cost_estimate=pl.CostEstimate(
                flops=int(us * 1.15e9), bytes_accessed=int(us * 3.6e6), transcendentals=0
            ),
        )(*args, *extra),
        tuple(after),
    )


def shaped(shape, dtype):
    return jax.ShapeDtypeStruct(shape, dtype)


def whole(shape):
    return pl.BlockSpec(shape, lambda *_: (0,) * len(shape), pipeline_mode=pl.Buffered(1))


ANY = pl.BlockSpec(memory_space=pl.ANY)


def pack_weights(where, w_qkv, small, w_out, w_up, w_down):
    r, f = w_out.shape[0], w_down.shape[0]
    columns = w_qkv.shape[1]
    half = (columns + PAD) // 2
    count = len(small)

    def kernel(where_ref, q_ref, wo_ref, wu_ref, wd_ref, *refs):
        s_refs, (out_ref, own_ref) = refs[:count], refs[count:]
        out_ref[:r, :] = wo_ref[...]
        for i in range(FF // D):
            out_ref[(1 + i) * r : (2 + i) * r, :] = wu_ref[:, i * D : (i + 1) * D]
        out_ref[5 * r :, :] = wd_ref[...]

        @pl.when(where_ref[1] == 0)
        def _():
            own_ref[...] = q_ref[:, :half]

        @pl.when(where_ref[1] > 0)
        def _():
            own_ref[:, : columns - half] = q_ref[:, half:]
            rows = []
            for s_ref in s_refs:
                v = s_ref[...].astype(F32)
                rows.append(jnp.concatenate([v, jnp.zeros((1, PAD - v.shape[1]), F32)], axis=1))
            rows.append(jnp.zeros((r - count, PAD), F32))
            own_ref[:, columns - half :] = jnp.concatenate(rows, axis=0).astype(BF)

    operands = (w_qkv, w_out, w_up, w_down) + tuple(v[None] for v in small)
    shapes = [shaped((5 * r + f, D), BF), shaped((r, half), BF)]
    return call(
        kernel,
        (1,),
        [whole(x.shape) for x in operands],
        [whole(x.shape) for x in shapes],
        shapes,
        us=2,
        prefetch=1,
    )(where, *operands)


def weight_copies(name, refs, target, sems):
    if len(refs) == 3:
        source = refs[("out", "up", "down").index(name)]
        return [pltpu.make_async_copy(source, target, sems.at[0])]
    packed = refs[0]
    ranks = packed.shape[0]
    r = D // ranks
    copies = []
    for o in range(ranks):
        if name == "out":
            parts = [(slice(0, r), target.at[o * r : (o + 1) * r])]
        elif name == "up":
            parts = [
                (
                    slice((1 + i) * r, (2 + i) * r),
                    target.at[o * r : (o + 1) * r, i * D : (i + 1) * D],
                )
                for i in range(FF // D)
            ]
        else:
            n = FF // ranks
            parts = [(slice(5 * r, 5 * r + n), target.at[o * n : (o + 1) * n])]
        for rows, where in parts:
            copies.append(pltpu.make_async_copy(packed.at[o, rows], where, sems.at[len(copies)]))
    return copies


def start_all(copies):
    for copy in copies:
        copy.start()


def wait_all(copies):
    for copy in copies:
        copy.wait()


def segment_of(places, lengths_ref, row):
    total = jnp.int32(0)
    segment = jnp.zeros(places.shape, jnp.int32)
    for s in range(SEGS):
        total = total + lengths_ref[row, s]
        segment = segment + (places >= total).astype(jnp.int32)
    return segment


def both_heads(x2):
    low = lax.broadcasted_iota(jnp.int32, (1, 128), 1) < HD
    zero = jnp.zeros_like(x2)
    return jnp.concatenate([jnp.where(low, x2, zero), jnp.where(low, zero, x2)], axis=0)


def attend_forward_kernel(
    lengths_ref, tok_ref, wq_ref, wk_ref, wv_ref, bias_ref, q_ref, k_ref, v_ref, p_ref, m_ref, vt, ot
):
    row = pl.program_id(1)
    tok = tok_ref[...]
    q_ref[...] = (dot(tok, wq_ref[...]) + bias_ref[0, 0:1, :]).astype(BF) * jnp.asarray(0.125, BF)
    k_ref[...] = dot(tok, wk_ref[...]).astype(BF)
    v = dot(tok, wv_ref[...]) + bias_ref[0, 1:2, :]
    v_ref[...] = v.astype(BF)
    vt[...] = v.T.astype(BF)
    for qb in range(BLOCKS):
        lo, hi = window(qb)
        width = hi - lo
        rows = slice(qb * BLOCK, (qb + 1) * BLOCK)
        seg_q = segment_of(
            lax.broadcasted_iota(jnp.int32, (1, BLOCK), 1) + qb * BLOCK, lengths_ref, row
        )
        seg_k = segment_of(
            lax.broadcasted_iota(jnp.int32, (width, 1), 0) + lo, lengths_ref, row
        )
        mask = jnp.where(jnp.concatenate([seg_q, seg_q], axis=1) == seg_k, 0.0, masked_score)
        for pair in range(PAIRS):
            lanes = slice(pair * 128, (pair + 1) * 128)
            s = dot_t(k_ref[lo:hi, lanes], both_heads(q_ref[rows, lanes])) + mask
            w = jnp.exp(s - jnp.max(s, axis=0, keepdims=True))
            p = (w * (1.0 / jnp.sum(w, axis=0, keepdims=True))).astype(BF)
            p_ref[0, pair, qb, :width, :] = p
            o = dot(vt[lanes, lo:hi], p)
            ot[pair * 128 : pair * 128 + HD, rows] = o[:HD, :BLOCK]
            ot[pair * 128 + HD : (pair + 1) * 128, rows] = o[HD:, BLOCK:]
    m_ref[...] = ot[...].T.astype(BF)


def attend_forward(lengths, tokens, w_qkv, bias, after=()):
    t = tokens.shape[0]
    rows = t // SEQ
    row_spec = pl.BlockSpec((SEQ, GW), lambda g, r, *_: (r, g))
    p_shape = (GROUPS * rows, PAIRS, BLOCKS, WIDE, 2 * BLOCK)
    column = lambda part: pl.BlockSpec((D, GW), lambda g, r, *_: (0, part * GROUPS + g))
    return call(
        attend_forward_kernel,
        (GROUPS, rows),
        [
            pl.BlockSpec((SEQ, D), lambda g, r, *_: (r, 0)),
            column(0),
            column(1),
            column(2),
            pl.BlockSpec((1, 2, GW), lambda g, r, *_: (g, 0, 0)),
        ],
        [row_spec] * 3
        + [pl.BlockSpec((1,) + p_shape[1:], lambda g, r, *_: (g * rows + r, 0, 0, 0, 0)), row_spec],
        [shaped((t, D), BF)] * 3 + [shaped(p_shape, BF), shaped((t, D), BF)],
        us=28,
        scratch=[pltpu.VMEM((GW, SEQ), BF), pltpu.VMEM((GW, SEQ), F32)],
        prefetch=1,
        after=after,
    )(lengths, tokens, w_qkv, w_qkv, w_qkv, bias)


def attend_backward_kernel(
    groups, direct, halves, where_ref, datt_ref, tok_ref, m_ref, wrefs, q_ref, k_ref, v_ref, p_ref, dp_ref,
    sums_ref, wg_refs, wo, kt, qt, dk_acc, dv_acc, dw_acc, dw_low, wsems, sems,
):
    g = pl.program_id(0)
    row = pl.program_id(1)
    first = groups[0]
    with_out = 0
    last = pl.num_programs(1) - 1
    span = 3 * GW

    def emit(place):
        if direct:
            part = span // halves
            copies = term_copies(
                where_ref,
                lambda owner_rows, h: dw_low.at[owner_rows, h * part : (h + 1) * part],
                D,
                lambda ref, where: ref.at[
                    where + (slice(None), pl.ds(pl.multiple_of(place * part, 128), part))
                ],
                wg_refs,
                sems,
                halves,
            )
        else:
            where = pl.ds(pl.multiple_of(place * span, 128), span)
            copies = [pltpu.make_async_copy(dw_low, wg_refs[0].at[:, where], sems.at[0])]
        start_all(copies)
        wait_all(copies)

    def add_term(term, place):
        @pl.when(row == 0)
        def _():
            dw_acc[...] = term

        @pl.when((row > 0) & (row < last))
        def _():
            dw_acc[...] += term

        @pl.when(row == last)
        def _():
            dw_low[...] = (dw_acc[...] + term).astype(BF)
            emit(place)

    if with_out:

        @pl.when(g == 0)
        def _():
            add_term(t_dot(m_ref[...], datt_ref[...]), 0)

    @pl.when((g == with_out) & (row == 0))
    def _():
        copies = weight_copies("out", wrefs, wo, wsems)
        start_all(copies)
        wait_all(copies)

    def group_step():
        place = g - with_out
        wo_rows = wo[pl.ds(pl.multiple_of((place + first) * GW, GW), GW), :]
        dmix = dot_t(datt_ref[...], wo_rows).astype(BF)
        kt[...] = k_ref[...].astype(F32).T.astype(BF)
        dk_acc[...] = jnp.zeros_like(dk_acc)
        dv_acc[...] = jnp.zeros_like(dv_acc)
        for qb in range(BLOCKS):
            lo, hi = window(qb)
            width = hi - lo
            rows = slice(qb * BLOCK, (qb + 1) * BLOCK)
            for pair in range(PAIRS):
                lanes = slice(pair * 128, (pair + 1) * 128)
                dos = both_heads(dmix[rows, lanes])
                p_low = p_ref[0, pair, qb, :width, :]
                p = p_low.astype(F32)
                dp = dot_t(v_ref[lo:hi, lanes], dos)
                delta = jnp.sum(p * dp, axis=0, keepdims=True)
                ds = (p * (dp - delta)).astype(BF)
                dk_acc[lo:hi, lanes] += dot(ds, both_heads(q_ref[rows, lanes]))
                dv_acc[lo:hi, lanes] += dot(p_low, dos)
                dq = dot(kt[lanes, lo:hi], ds)
                qt[pair * 128 : pair * 128 + HD, rows] = dq[:HD, :BLOCK]
                qt[pair * 128 + HD : (pair + 1) * 128, rows] = dq[HD:, BLOCK:]
        dq = (qt[...] * 0.125).T.astype(BF)
        dv = dv_acc[...].astype(BF)
        dp_ref[:, :GW] = dq
        dp_ref[:, GW : 2 * GW] = dk_acc[...].astype(BF)
        dp_ref[:, 2 * GW :] = dv
        sums = jnp.concatenate(
            [
                jnp.sum(dq.astype(F32), axis=0, keepdims=True),
                jnp.sum(dv.astype(F32), axis=0, keepdims=True),
            ],
            axis=0,
        )
        sums_ref[...] = jnp.where(row == 0, sums, sums_ref[...] + sums)
        add_term(t_dot(tok_ref[...], dp_ref[...]), g)

    if with_out:
        pl.when(g > 0)(group_step)
    else:
        group_step()


RANKS = 16


def term_copies(where_ref, source, total_rows, target, refs, sems, halves):
    me, replica = where_ref[0], where_ref[1]
    rows = total_rows // RANKS
    copies = []
    for j in range(RANKS):
        owner_rows = pl.ds(pl.multiple_of((me ^ j) * rows, rows), rows)
        place = ((j >> 1) & 1, j >> 2)
        for h in range(halves):
            where = ((h ^ replica,) if halves == 2 else ()) + place
            copies.append(
                pltpu.make_async_copy(
                    source(owner_rows, h), target(refs[j & 1], where), sems.at[halves * j + h]
                )
            )
    return copies


def attend_backward(where, datt, tokens, weights, groups, kept, direct, halves, after=()):
    q, k, v, p, mixed = kept
    t = datt.shape[0]
    rows = t // SEQ
    count, first = len(groups), groups[0]
    extra = 0
    group = lambda g: jnp.maximum(g - extra, 0) + first
    row_spec = pl.BlockSpec((SEQ, GW), lambda g, r, *_: (r, group(g)))
    full_row = pl.BlockSpec((SEQ, D), lambda g, r, *_: (r, 0))
    columns = (count + extra) * 3 * GW
    if direct:
        lead = (2, 2, 4) if halves == 2 else (2, 4)
        wg_shapes = [shaped(lead + (D // RANKS, columns // halves), BF)] * 2
    else:
        wg_shapes = [shaped((D, columns), BF)]
    nw, ng = len(weights), len(wg_shapes)

    def kernel(where_ref, datt_ref, tok_ref, m_ref, *refs):
        wrefs, refs = refs[:nw], refs[nw:]
        q_ref, k_ref, v_ref, p_ref, dp_ref, sums_ref = refs[:6]
        wg_refs, scratch = refs[6 : 6 + ng], refs[6 + ng :]
        attend_backward_kernel(
            groups, direct, halves, where_ref, datt_ref, tok_ref, m_ref, wrefs, q_ref, k_ref, v_ref, p_ref,
            dp_ref, sums_ref, wg_refs, *scratch,
        )

    m_spec = pl.BlockSpec((SEQ, D), lambda g, r, *_: (jnp.where(g == 0, r, rows - 1), 0))
    return call(
        kernel,
        (count + extra, rows),
        [full_row, full_row, m_spec if extra else ANY]
        + [ANY] * nw
        + [
            row_spec,
            row_spec,
            row_spec,
            pl.BlockSpec((1,) + p.shape[1:], lambda g, r, *_: (group(g) * rows + r, 0, 0, 0, 0)),
        ],
        [
            pl.BlockSpec(
                (SEQ, 3 * GW), lambda g, r, *_: (jnp.where(g < extra, 0, r), jnp.maximum(g - extra, 0))
            ),
            pl.BlockSpec((2, GW), lambda g, r, *_: (0, jnp.maximum(g - extra, 0))),
        ]
        + [ANY] * ng,
        [shaped((t, count * 3 * GW), BF), shaped((2, count * GW), F32)] + wg_shapes,
        us=1,
        scratch=[
            pltpu.VMEM((D, D), BF),
            pltpu.VMEM((GW, SEQ), BF),
            pltpu.VMEM((GW, SEQ), F32),
            pltpu.VMEM((SEQ, GW), F32),
            pltpu.VMEM((SEQ, GW), F32),
            pltpu.VMEM((D, 3 * GW), F32),
            pltpu.VMEM((D, 3 * GW), BF),
            pltpu.SemaphoreType.DMA((16,)),
            pltpu.SemaphoreType.DMA((2 * RANKS,)),
        ],
        prefetch=1,
        after=after,
    )(where, datt, tokens, mixed, *weights, q, k, v, p)


TB = 256
CH = 768


def normalize(values):
    centered = values - jnp.mean(values, axis=-1, keepdims=True)
    variance = jnp.mean(centered * centered, axis=-1, keepdims=True)
    inverse = lax.rsqrt(variance + epsilon)
    return centered * inverse, inverse


def normalize_back(grad, xhat, inverse):
    mean = jnp.mean(grad, axis=-1, keepdims=True)
    along = jnp.mean(grad * xhat, axis=-1, keepdims=True)
    return (grad - mean - xhat * along) * inverse


def add_rows(ref, rows):
    stacked = jnp.concatenate([jnp.sum(r, axis=0, keepdims=True) for r in rows], axis=0)
    ref[...] = jnp.where(pl.program_id(0) == 0, stacked, ref[...] + stacked)


def middle(lengths, tokens, mixed, weights, vec, bias_up, cot, after=()):
    t = tokens.shape[0]
    nw = len(weights)
    per_row = SEQ // TB

    def kernel(lengths_ref, tok_ref, m_ref, vec_ref, bu_ref, cot_ref, *refs):
        wrefs, refs = refs[:nw], refs[nw:]
        out_ref, nl_ref, act_ref, dd_ref, du_ref, df_ref, da_ref, sums_ref, su_ref, pool_ref = refs[:10]
        wo, wu, wd, gp, so, su, sd = refs[10:]
        i = pl.program_id(0)
        out_copies = weight_copies("out", wrefs, wo, so)
        up_copies = weight_copies("up", wrefs, wu, su)
        down_copies = weight_copies("down", wrefs, wd, sd)

        @pl.when(i == 0)
        def _():
            start_all(out_copies)
            start_all(up_copies)
            start_all(down_copies)
            wait_all(out_copies)

        att = dot(m_ref[...], wo[...]) + vec_ref[0:1, :]
        xhat, inverse = normalize(tok_ref[...].astype(F32) + att)
        normed = xhat * vec_ref[1:2, :] + vec_ref[2:3, :]
        nl = normed.astype(BF)
        nl_ref[...] = nl

        @pl.when(i == 0)
        def _():
            wait_all(up_copies)

        for c in range(0, FF, CH):
            u = dot(nl, wu[:, c : c + CH]) + bu_ref[:, c : c + CH]
            cdf = 0.5 * (1.0 + lax.erf(u * root_half))
            act_ref[:, c : c + CH] = (u * cdf).astype(BF)
            gp[:, c : c + CH] = cdf + u * (jnp.exp(u * u * -0.5) * pdf_scale)

        @pl.when(i == 0)
        def _():
            wait_all(down_copies)

        second = normed + (dot(act_ref[...], wd[...]) + vec_ref[3:4, :])
        xhat_two, inverse_two = normalize(second)
        out = (xhat_two * vec_ref[4:5, :] + vec_ref[5:6, :]).astype(BF)
        out_ref[...] = out
        cot = cot_ref[...].astype(F32)
        d_second = normalize_back(cot * vec_ref[4:5, :], xhat_two, inverse_two)
        dd = d_second.astype(BF)
        dd_ref[...] = dd
        row = i // per_row
        places = lax.broadcasted_iota(jnp.int32, (1, TB), 1) + (i % per_row) * TB
        segment = segment_of(places, lengths_ref, row)
        ids = lax.broadcasted_iota(jnp.int32, (SEGS, TB), 0)
        pooled = dot(jnp.where(segment == ids, 1.0, 0.0).astype(BF), out)
        pooled = jnp.where(i % per_row == 0, pooled, pool_ref[0] + pooled)
        counts = jnp.zeros((SEGS, 1), F32)
        places = lax.broadcasted_iota(jnp.int32, (SEGS, 1), 0)
        for s in range(SEGS):
            counts = jnp.where(places == s, lengths_ref[row, s].astype(F32), counts)
        pool_ref[0] = jnp.where(i % per_row == per_row - 1, pooled / counts, pooled)
        for c in range(0, FF, CH):
            du = (dot_t(dd, wd[c : c + CH, :]) * gp[:, c : c + CH]).astype(BF)
            du_ref[:, c : c + CH] = du
            partial = jnp.sum(du.astype(F32), axis=0, keepdims=True)
            su_ref[:, c : c + CH] = jnp.where(i == 0, partial, su_ref[:, c : c + CH] + partial)
        d_normed = d_second + dot_t(du_ref[...], wu[...])
        d_first = normalize_back(d_normed * vec_ref[1:2, :], xhat, inverse)
        df_ref[...] = d_first
        d_att = d_first.astype(BF)
        da_ref[...] = d_att
        add_rows(
            sums_ref,
            (dd.astype(F32), cot * xhat_two, cot, d_att.astype(F32), d_normed * xhat, d_normed),
        )

    tok = lambda n: pl.BlockSpec((TB, n), lambda i, *_: (i, 0))
    return call(
        kernel,
        (t // TB,),
        [tok(D), tok(D), whole((6, D)), whole((1, FF)), tok(D)] + [ANY] * nw,
        [
            tok(D),
            tok(D),
            tok(FF),
            tok(D),
            tok(FF),
            tok(D),
            tok(D),
            pl.BlockSpec((6, D), lambda i, *_: (0, 0)),
            pl.BlockSpec((1, FF), lambda i, *_: (0, 0)),
            pl.BlockSpec((1, SEGS, D), lambda i, *_: (i // per_row, 0, 0)),
        ],
        [
            shaped((t, D), BF),
            shaped((t, D), BF),
            shaped((t, FF), BF),
            shaped((t, D), BF),
            shaped((t, FF), BF),
            shaped((t, D), F32),
            shaped((t, D), BF),
            shaped((6, D), F32),
            shaped((1, FF), F32),
            shaped((t // SEQ, SEGS, D), F32),
        ],
        us=45,
        scratch=[
            pltpu.VMEM((D, D), BF),
            pltpu.VMEM((D, FF), BF),
            pltpu.VMEM((FF, D), BF),
            pltpu.VMEM((TB, FF), F32),
            pltpu.SemaphoreType.DMA((16,)),
            pltpu.SemaphoreType.DMA((64,)),
            pltpu.SemaphoreType.DMA((16,)),
        ],
        prefetch=1,
        after=after,
    )(lengths, tokens, mixed, vec, bias_up, cot, *weights)


def input_gradient(d_first, d_projected, w_qkv, after=()):
    t = d_first.shape[0]

    def kernel(df_ref, p0, p1, w_ref, out_ref):
        total = df_ref[...]
        g = 0
        for p in (p0, p1):
            for local in range(p.shape[1] // D):
                for part in range(3):
                    start = part * D + g * GW
                    at = local * D + part * GW
                    total = total + dot_t(p[:, at : at + GW], w_ref[:, start : start + GW])
                g += 1
        out_ref[...] = total

    tok = lambda n: pl.BlockSpec((TB, n), lambda i: (i, 0))
    return call(
        kernel,
        (t // TB,),
        [tok(D), tok(d_projected[0].shape[1]), tok(d_projected[1].shape[1]), whole((D, 3 * D))],
        tok(D),
        shaped((t, D), F32),
        us=9,
        after=after,
    )(d_first, *d_projected, w_qkv)


def grad_down(active, d_down, after=()):
    t = d_down.shape[0]
    n = 768

    def kernel(a_ref, b_ref, out_ref):
        out_ref[...] = t_dot(a_ref[...], b_ref[...]).astype(BF)

    return call(
        kernel,
        (FF // n,),
        [pl.BlockSpec((t, n), lambda i: (0, i)), whole((t, D))],
        pl.BlockSpec((n, D), lambda i: (i, 0)),
        shaped((FF, D), BF),
        us=9,
        after=after,
    )(active, d_down)


STRIP = 384
STRIPS = (FF + D) // 2 // STRIP


def grad_up_out(where, nl, d_upper, mixed, d_att, direct, after=()):
    t = nl.shape[0]

    def kernel(where_ref, nl_ref, du_ref, m_ref, da_ref, *refs):
        outs, (acc, sems) = refs[:-2], refs[-2:]
        h = pl.program_id(0)
        acc[h, :, : FF // 2] = t_dot(nl_ref[...], du_ref[...]).astype(BF)
        acc[h, :, FF // 2 :] = t_dot(m_ref[...], da_ref[...]).astype(BF)

        def copies_of(h):
            if not direct:
                return [pltpu.make_async_copy(acc.at[h], outs[0].at[h], sems.at[h, 0])]
            me, replica = where_ref[0], where_ref[1]
            rows = D // RANKS
            copies = []
            for j in range(RANKS):
                owner_rows = pl.ds(pl.multiple_of((me ^ j) * rows, rows), rows)
                for strip in range(STRIPS):
                    target = outs[j & 1].at[
                        h ^ replica, (j >> 1) & 1, j >> 2, strip * rows : (strip + 1) * rows
                    ]
                    source = acc.at[h, owner_rows, strip * STRIP : (strip + 1) * STRIP]
                    copies.append(pltpu.make_async_copy(source, target, sems.at[h, len(copies)]))
            return copies

        start_all(copies_of(h))

        @pl.when(h == 1)
        def _():
            wait_all(copies_of(0))
            wait_all(copies_of(1))

    if direct:
        out_shapes = [shaped((2, 2, 4, STRIPS * D // RANKS, STRIP), BF)] * 2
    else:
        out_shapes = [shaped((2, D, (FF + D) // 2), BF)]
    return call(
        kernel,
        (2,),
        [
            whole((t, D)),
            pl.BlockSpec((t, FF // 2), lambda h, *_: (0, h)),
            whole((t, D)),
            pl.BlockSpec((t, D // 2), lambda h, *_: (0, h)),
        ],
        [ANY] * len(out_shapes),
        out_shapes,
        us=13,
        scratch=[
            pltpu.VMEM((2, D, (FF + D) // 2), BF),
            pltpu.SemaphoreType.DMA((2, RANKS * STRIPS)),
        ],
        prefetch=1,
        after=after,
    )(where, nl, d_upper, mixed, d_att)


def swap(x, mask):
    return lax.ppermute(x, "fsdp", [(i, i ^ mask) for i in range(RANKS)])


def swap_replica(x):
    return lax.ppermute(x, "replica", [(0, 1), (1, 0)])


def added(*terms):
    total = terms[0].astype(F32)
    for term in terms[1:]:
        total = total + term.astype(F32)
    return total


def gather_qkv(where, own):
    rows, half = own.shape
    columns = 2 * half
    z = jnp.stack([own] + [swap(own, m) for m in (4, 8, 12)])
    zy = jnp.stack([z, swap(z, 2)])
    x = swap_replica(zy)
    pieces = (zy, x, swap(zy, 1), swap(x, 1))

    def kernel(where_ref, p0, p1, p2, p3, out_ref, sems):
        me, other = where_ref[0], where_ref[1]
        copies = []
        for index, piece in enumerate((p0, p1, p2, p3)):
            start = pl.multiple_of((other ^ (index % 2)) * half, 128)
            for y in range(2):
                for k in range(4):
                    owner = me ^ (4 * k + 2 * y + index // 2)
                    target = out_ref.at[
                        pl.ds(pl.multiple_of(owner * rows, rows), rows), pl.ds(start, half)
                    ]
                    copies.append(
                        pltpu.make_async_copy(piece.at[y, k], target, sems.at[len(copies)])
                    )
        start_all(copies)
        wait_all(copies)

    return call(
        kernel,
        (1,),
        [ANY] * 4,
        pl.BlockSpec((RANKS * rows, columns), lambda *_: (0, 0)),
        shaped((RANKS * rows, columns), BF),
        us=4,
        scratch=[pltpu.SemaphoreType.DMA((32,))],
        prefetch=1,
    )(where, *pieces)


def ordered(own, other, replica):
    first = jnp.where(replica == 0, own, other)
    second = jnp.where(replica == 0, other, own)
    return first, second


class Chain:
    def __init__(self, keep, send, lines=None, grow=False, two_steps=False):
        self.columns = keep.shape[-1]
        flat = lambda x: x.reshape(-1, self.columns)
        halves = [(swap_replica,)] if keep.ndim == 5 else []
        over = lambda m: lambda x: swap(x, m)
        along_z = [(over(8),), (over(4),)] if two_steps else [(over(4), over(8), over(12))]
        fsdp = [(over(1),)] + halves + [(over(2),)] + along_z
        self.moves = fsdp + [(swap_replica,)]
        self.owner_rows = keep.shape[-2]
        self.stay, self.away = flat(keep), [flat(send)]
        self.lines = None if lines is None else flat(lines)
        self.ride = [False] * len(self.moves)
        if lines is not None:
            self.ride = [not grow] + [True] * (len(fsdp) - 1) + [not halves]
        self.grow = grow

    def send(self):
        moves = self.moves.pop(0)
        self.received = [move(x) for move, x in zip(moves, self.away)]
        self.beside = []
        self.arriving = self.ride.pop(0)
        if self.arriving and len(self.received[0]) == len(self.stay):
            self.beside = [moves[0](self.lines)]


def add_all(chains, after=(), passing=()):
    operands, shapes, plans = [], [], []
    for c in chains:
        n = c.stay.shape[0]
        parts = len(c.moves[0]) + 1 if n > c.owner_rows else 1
        part = n // parts
        lines = c.lines.shape[0] if c.arriving or c.ride[0] else 0
        held = lines if c.arriving else 0
        grown = held * (2 if c.grow else 1)
        rides = (grown or lines) if c.ride[0] else 0
        ins = [c.stay] + c.received + (c.beside + [c.lines] if lines else [])
        outs = [shaped((part, c.columns), BF)]
        sends = parts - 1 if parts > 1 else int(rides > 0)
        outs += [shaped((part + rides, c.columns), BF)] * sends
        if held:
            outs.append(shaped((grown, c.columns), BF))
        plans.append((len(ins), len(outs), n, part, parts, sends, held, rides, len(c.received), len(c.beside), c.grow))
        operands += ins
        shapes += outs

    passed, inputs = len(passing), len(operands)

    def kernel(*refs):
        sources, targets = refs[: len(operands)], refs[len(operands) + passed :]
        for n_in, n_out, n, part, parts, sends, held, rides, arrivals, beside, grow in plans:
            ins, sources = sources[:n_in], sources[n_in:]
            outs, targets = targets[:n_out], targets[n_out:]
            received = ins[1 : 1 + arrivals]
            for p in range(parts):
                rows = slice(p * part, (p + 1) * part)
                total = ins[0][rows, :].astype(F32)
                for r in received:
                    total = total + r[rows, :].astype(F32)
                total = total.astype(BF)
                outs[p][:part, :] = total
                if parts == 1 and sends:
                    outs[1][:part, :] = total
            if held:
                mine = ins[-1][...]
                if beside:
                    others = [ins[1 + arrivals][...]]
                else:
                    others = [r[n : n + held, :] for r in received]
                if grow:
                    lines = jnp.concatenate([mine, others[0]], axis=0)
                else:
                    total = mine.astype(F32)
                    for other in others:
                        total = total + other.astype(F32)
                    lines = total.astype(BF)
                outs[-1][...] = lines
            elif rides:
                lines = ins[-1][...]
            if rides:
                for out in outs[1 : 1 + sends]:
                    out[part:, :] = lines

    results = list(
        call(
            kernel,
            (1,),
            [whole(x.shape) for x in operands] + [ANY] * passed,
            [whole(x.shape) for x in shapes] + [ANY] * passed,
            shapes + [shaped(x.shape, x.dtype) for x in passing],
            us=2,
            after=after,
            aliases={inputs + i: len(shapes) + i for i in range(passed)},
        )(*operands, *passing)
    )
    for c, plan in zip(chains, plans):
        n_out, sends, held = plan[1], plan[5], plan[6]
        mine, results = results[:n_out], results[n_out:]
        c.stay = mine[0]
        c.away = mine[1 : 1 + sends] if sends else [mine[0]]
        if held:
            c.lines = mine[-1]
    return results


SMALL = ("bias_qv", "bias_out", "gain_one", "shift_one", "bias_up", "bias_down", "gain_two", "shift_two")
SMALL_SIZES = (2 * D, D, D, D, FF, D, D, D)
PAD = 256


def body(
    ranks,
    replicas,
    tokens,
    lengths,
    w_qkv,
    bias_qv,
    w_out,
    bias_out,
    gain_one,
    shift_one,
    w_up,
    bias_up,
    w_down,
    bias_down,
    gain_two,
    shift_two,
    cotangent,
):
    direct = ranks == RANKS and replicas == 2
    me = lax.axis_index("fsdp")
    replica = lax.axis_index("replica")
    where = jnp.stack([me, replica]).astype(jnp.int32)
    gather = lambda w: lax.all_gather(w, "fsdp", axis=0, tiled=True)

    small = (bias_qv, bias_out, gain_one, shift_one, bias_up, bias_down, gain_two, shift_two)
    if direct:
        packed, own = pack_weights(where, w_qkv, small, w_out, w_up, w_down)
        w_first = gather_qkv(where, own)
        weights = (gather(packed).reshape(ranks, -1, D),)
    else:
        w_first = gather(w_qkv)
        weights = (gather(w_out), gather(w_up), gather(w_down))
    vectors = {}
    if direct:
        beside = w_first[:, 3 * D :].reshape(ranks, -1, PAD)
    for k, (name, value) in enumerate(zip(SMALL, small)):
        got = beside[:, k, : value.shape[0]].reshape(-1) if direct else gather(value)
        vectors[name] = got.astype(F32)

    bias = vectors["bias_qv"].reshape(2, GROUPS, GW).transpose(1, 0, 2)
    kept = attend_forward(lengths, tokens, w_first, bias)
    mixed = kept[4]
    vec = jnp.stack(
        [
            vectors[n]
            for n in ("bias_out", "gain_one", "shift_one", "bias_down", "gain_two", "shift_two")
        ]
    )
    (layer_out, nl, active, d_down, d_upper, d_first, d_att, sums, sums_up, pooled) = middle(
        lengths, tokens, mixed, weights, vec, vectors["bias_up"][None], cotangent
    )

    terms_up = grad_up_out(where, nl, d_upper, mixed, d_att, direct)
    term_down = grad_down(active, d_down, after=(terms_up[0],))
    scatter = lambda x: lax.psum_scatter(x, "fsdp", scatter_dimension=0, tiled=True)

    def small_lines(sums_a, sums_b):
        both = jnp.concatenate([sums_a, sums_b], axis=1)
        return jnp.concatenate([both, sums[3:], sums_up.reshape(-1, D), sums[:3]])

    attend_back = functools.partial(attend_backward, where, d_att, tokens, weights)
    if direct:
        chain_u = Chain(*terms_up, two_steps=True)
        chain_u.send()
        (term_down,) = add_all([chain_u], passing=(term_down,))
        shard_down = scatter(term_down)
        chain_u.send()
        dp_a, sums_a, *terms_a = attend_back((0, 1), kept, True, 2, after=(chain_u.away[0],))
        chain_a = Chain(*terms_a, pooled.astype(BF), grow=True, two_steps=True)
        (chain_a.away[0],) = add_all([chain_u], after=(sums_a,), passing=(chain_a.away[0],))
        chain_u.send()
        chain_a.send()
        add_all([chain_a])
        chain_a.send()
        dp_b, sums_b, *terms_b = attend_back((2,), kept, True, 1, after=(chain_a.away[0],))
        small = small_lines(sums_a, sums_b)
        small = jnp.pad(small, ((0, -small.shape[0] % 16), (0, 0))).astype(BF)
        chain_b = Chain(*terms_b, small)
        chain_b.send()
        add_all([chain_u, chain_a], after=(sums_b,))
        chain_u.send()
        chain_a.send()
        input_grad = input_gradient(
            d_first, (dp_a, dp_b), w_first, after=(chain_a.away[0],)
        )
        add_all([chain_u, chain_a, chain_b], after=(input_grad,))
        chain_u.send()
        chain_a.send()
        chain_b.send()
        while chain_u.moves or chain_a.moves or chain_b.moves:
            moving = [c for c in (chain_u, chain_a, chain_b) if c.moves]
            add_all(moving, after=(shard_down,))
            for c in moving:
                c.send()
        halves_u = ordered(chain_u.stay, chain_u.received[0][: chain_u.owner_rows], replica)
        halves_u = [
            h.reshape(STRIPS, -1, STRIP).transpose(1, 0, 2).reshape(-1, STRIPS * STRIP)
            for h in halves_u
        ]
        grad_w_down = added(shard_down, swap_replica(shard_down))
        lines = chain_a.lines.reshape((2,) * 4 + pooled.shape)
        relative = jnp.stack([lines, swap(lines, 1)]).transpose(4, 2, 1, 3, 0, 5, 6, 7)
        relative = relative.reshape((2, ranks) + pooled.shape)
        pooled_all = relative[jnp.arange(2) ^ replica][:, me ^ jnp.arange(ranks)]
        pooled_all = pooled_all.reshape((2 * ranks * pooled.shape[0],) + pooled.shape[1:]).astype(F32)
        h0, h1 = ordered(chain_a.stay, chain_a.received[0], replica)
        span = 3 * GW // 2
        halves_a = [
            jnp.concatenate([h[:, i * span : (i + 1) * span] for h in (h0, h1)], axis=1).astype(F32)
            for i in range(2)
        ]
        sum_b = added(chain_b.stay, chain_b.received[0][: chain_b.owner_rows])
        lines = added(chain_b.lines, chain_b.received[0][chain_b.owner_rows :])
        parts = halves_a + [sum_b]
    else:
        dp_a, sums_a, term_a = attend_back((0, 1), kept, False, 1)
        dp_b, sums_b, term_b = attend_back((2,), kept, False, 1)
        input_grad = input_gradient(d_first, (dp_a, dp_b), w_first)
        pooled_all = lax.all_gather(pooled, ("replica", "fsdp"), axis=0, tiled=True)
        reduce = lambda x: lax.psum(scatter(x), "replica").astype(F32)
        grad_w_down = reduce(term_down)
        halves_u = [reduce(terms_up[0][h]) for h in range(2)]
        sum_a, sum_b = reduce(term_a), reduce(term_b)
        lines = lax.psum(small_lines(sums_a, sums_b), ("replica", "fsdp"))
        parts = [sum_a[:, :D], sum_a[:, D:], sum_b]
    grad_w_up = jnp.concatenate([h[:, : FF // 2] for h in halves_u], axis=1).astype(F32)
    grad_w_out = jnp.concatenate([h[:, FF // 2 :] for h in halves_u], axis=1).astype(F32)
    grad_w_qkv = jnp.concatenate(
        [p[:, i * GW : (i + 1) * GW] for i in range(3) for p in parts], axis=1
    )
    small_grads, start = {}, 0
    for name, size in zip(SMALL, SMALL_SIZES):
        values = lines[start // D : (start + size) // D].reshape(ranks, -1)
        small_grads[name] = lax.dynamic_index_in_dim(values, me, keepdims=False)
        start += size
    return (
        layer_out,
        input_grad,
        pooled_all,
        grad_w_qkv,
        small_grads["bias_qv"],
        grad_w_out,
        small_grads["bias_out"],
        small_grads["gain_one"],
        small_grads["shift_one"],
        grad_w_up,
        small_grads["bias_up"],
        grad_w_down,
        small_grads["bias_down"],
        small_grads["gain_two"],
        small_grads["shift_two"],
    )


def solution(mesh):
    rows = P(("replica", "fsdp"), None)
    matrix = P("fsdp", None)
    vector = P("fsdp")
    return jax.shard_map(
        functools.partial(body, mesh.shape["fsdp"], mesh.shape["replica"]),
        mesh=mesh,
        in_specs=(
            rows,
            rows,
            matrix,
            vector,
            matrix,
            vector,
            vector,
            vector,
            matrix,
            vector,
            matrix,
            vector,
            vector,
            vector,
            rows,
        ),
        out_specs=(
            rows,
            rows,
            P(),
            matrix,
            vector,
            matrix,
            vector,
            vector,
            vector,
            matrix,
            vector,
            matrix,
            vector,
            vector,
            vector,
        ),
        check_vma=False,
    )
```

```python
import functools

import jax
import jax.numpy as jnp
from jax import lax
from jax.experimental import pallas as pl
from jax.experimental.pallas import tpu as pltpu
from jax.sharding import PartitionSpec as P

D = 768
H = 12
HD = 64
FF = 3072
SEQ = 512
SEGS = 8
GROUPS = 3
GW = D // GROUPS
PAIRS = GW // 128
BLOCK = 128
BLOCKS = SEQ // BLOCK
WIDE = 3 * BLOCK

epsilon = 1e-12
root_half = 0.7071067811865476
masked_score = -1e30
pdf_scale = 0.3989422804014327

BF = jnp.bfloat16
F32 = jnp.float32
VMEM_LIMIT = 56 * 2**20


def dot(a, b):
    return jnp.dot(a, b, preferred_element_type=F32)


def dot_t(a, b):
    return lax.dot_general(a, b, (((1,), (1,)), ((), ())), preferred_element_type=F32)


def t_dot(a, b):
    return lax.dot_general(a, b, (((0,), (0,)), ((), ())), preferred_element_type=F32)


def window(qb):
    return max(0, (qb - 1) * BLOCK), min(SEQ, (qb + 2) * BLOCK)


def call(
    kernel, grid, in_specs, out_specs, out_shape, us, scratch=(), prefetch=0, after=(), aliases=None
):
    first = prefetch + len(in_specs)

    def run(*refs):
        kernel(*refs[:first], *refs[first + len(after) :])

    return functools.partial(
        lambda extra, *args: pl.pallas_call(
            run,
            grid_spec=pltpu.PrefetchScalarGridSpec(
                num_scalar_prefetch=prefetch,
                grid=grid,
                in_specs=list(in_specs) + [pl.BlockSpec(memory_space=pl.ANY)] * len(extra),
                out_specs=out_specs,
                scratch_shapes=list(scratch),
            ),
            out_shape=out_shape,
            input_output_aliases=aliases or {},
            compiler_params=pltpu.CompilerParams(vmem_limit_bytes=VMEM_LIMIT),
            cost_estimate=pl.CostEstimate(
                flops=int(us * 1.15e9), bytes_accessed=int(us * 3.6e6), transcendentals=0
            ),
        )(*args, *extra),
        tuple(after),
    )


def shaped(shape, dtype):
    return jax.ShapeDtypeStruct(shape, dtype)


def whole(shape):
    return pl.BlockSpec(shape, lambda *_: (0,) * len(shape), pipeline_mode=pl.Buffered(1))


ANY = pl.BlockSpec(memory_space=pl.ANY)


def pack_weights(where, w_qkv, small, w_out, w_up, w_down):
    r, f = w_out.shape[0], w_down.shape[0]
    columns = w_qkv.shape[1]
    half = (columns + PAD) // 2
    count = len(small)

    def kernel(where_ref, q_ref, wo_ref, wu_ref, wd_ref, *refs):
        s_refs, (out_ref, own_ref) = refs[:count], refs[count:]
        out_ref[:r, :] = wo_ref[...]
        for i in range(FF // D):
            out_ref[(1 + i) * r : (2 + i) * r, :] = wu_ref[:, i * D : (i + 1) * D]
        out_ref[5 * r :, :] = wd_ref[...]

        @pl.when(where_ref[1] == 0)
        def _():
            own_ref[...] = q_ref[:, :half]

        @pl.when(where_ref[1] > 0)
        def _():
            own_ref[:, : columns - half] = q_ref[:, half:]
            rows = []
            for s_ref in s_refs:
                v = s_ref[...].astype(F32)
                rows.append(jnp.concatenate([v, jnp.zeros((1, PAD - v.shape[1]), F32)], axis=1))
            rows.append(jnp.zeros((r - count, PAD), F32))
            own_ref[:, columns - half :] = jnp.concatenate(rows, axis=0).astype(BF)

    operands = (w_qkv, w_out, w_up, w_down) + tuple(v[None] for v in small)
    shapes = [shaped((5 * r + f, D), BF), shaped((r, half), BF)]
    return call(
        kernel,
        (1,),
        [whole(x.shape) for x in operands],
        [whole(x.shape) for x in shapes],
        shapes,
        us=2,
        prefetch=1,
    )(where, *operands)


def weight_copies(name, refs, target, sems):
    if len(refs) == 3:
        source = refs[("out", "up", "down").index(name)]
        return [pltpu.make_async_copy(source, target, sems.at[0])]
    packed = refs[0]
    ranks = packed.shape[0]
    r = D // ranks
    copies = []
    for o in range(ranks):
        if name == "out":
            parts = [(slice(0, r), target.at[o * r : (o + 1) * r])]
        elif name == "up":
            parts = [
                (
                    slice((1 + i) * r, (2 + i) * r),
                    target.at[o * r : (o + 1) * r, i * D : (i + 1) * D],
                )
                for i in range(FF // D)
            ]
        else:
            n = FF // ranks
            parts = [(slice(5 * r, 5 * r + n), target.at[o * n : (o + 1) * n])]
        for rows, where in parts:
            copies.append(pltpu.make_async_copy(packed.at[o, rows], where, sems.at[len(copies)]))
    return copies


def start_all(copies):
    for copy in copies:
        copy.start()


def wait_all(copies):
    for copy in copies:
        copy.wait()


def segment_of(places, lengths_ref, row):
    total = jnp.int32(0)
    segment = jnp.zeros(places.shape, jnp.int32)
    for s in range(SEGS):
        total = total + lengths_ref[row, s]
        segment = segment + (places >= total).astype(jnp.int32)
    return segment


def both_heads(x2):
    low = lax.broadcasted_iota(jnp.int32, (1, 128), 1) < HD
    zero = jnp.zeros_like(x2)
    return jnp.concatenate([jnp.where(low, x2, zero), jnp.where(low, zero, x2)], axis=0)


def attend_forward_kernel(
    lengths_ref, tok_ref, wq_ref, wk_ref, wv_ref, bias_ref, q_ref, k_ref, v_ref, p_ref, m_ref, vt, ot
):
    row = pl.program_id(1)
    tok = tok_ref[...]
    q_ref[...] = (dot(tok, wq_ref[...]) + bias_ref[0, 0:1, :]).astype(BF) * jnp.asarray(0.125, BF)
    k_ref[...] = dot(tok, wk_ref[...]).astype(BF)
    v = dot(tok, wv_ref[...]) + bias_ref[0, 1:2, :]
    v_ref[...] = v.astype(BF)
    vt[...] = v.T.astype(BF)
    for qb in range(BLOCKS):
        lo, hi = window(qb)
        width = hi - lo
        rows = slice(qb * BLOCK, (qb + 1) * BLOCK)
        seg_q = segment_of(
            lax.broadcasted_iota(jnp.int32, (1, BLOCK), 1) + qb * BLOCK, lengths_ref, row
        )
        seg_k = segment_of(
            lax.broadcasted_iota(jnp.int32, (width, 1), 0) + lo, lengths_ref, row
        )
        mask = jnp.where(jnp.concatenate([seg_q, seg_q], axis=1) == seg_k, 0.0, masked_score)
        for pair in range(PAIRS):
            lanes = slice(pair * 128, (pair + 1) * 128)
            s = dot_t(k_ref[lo:hi, lanes], both_heads(q_ref[rows, lanes])) + mask
            w = jnp.exp(s - jnp.max(s, axis=0, keepdims=True))
            p = (w * (1.0 / jnp.sum(w, axis=0, keepdims=True))).astype(BF)
            p_ref[0, pair, qb, :width, :] = p
            o = dot(vt[lanes, lo:hi], p)
            ot[pair * 128 : pair * 128 + HD, rows] = o[:HD, :BLOCK]
            ot[pair * 128 + HD : (pair + 1) * 128, rows] = o[HD:, BLOCK:]
    m_ref[...] = ot[...].T.astype(BF)


def attend_forward(lengths, tokens, w_qkv, bias, after=()):
    t = tokens.shape[0]
    rows = t // SEQ
    row_spec = pl.BlockSpec((SEQ, GW), lambda g, r, *_: (r, g))
    p_shape = (GROUPS * rows, PAIRS, BLOCKS, WIDE, 2 * BLOCK)
    column = lambda part: pl.BlockSpec((D, GW), lambda g, r, *_: (0, part * GROUPS + g))
    return call(
        attend_forward_kernel,
        (GROUPS, rows),
        [
            pl.BlockSpec((SEQ, D), lambda g, r, *_: (r, 0)),
            column(0),
            column(1),
            column(2),
            pl.BlockSpec((1, 2, GW), lambda g, r, *_: (g, 0, 0)),
        ],
        [row_spec] * 3
        + [pl.BlockSpec((1,) + p_shape[1:], lambda g, r, *_: (g * rows + r, 0, 0, 0, 0)), row_spec],
        [shaped((t, D), BF)] * 3 + [shaped(p_shape, BF), shaped((t, D), BF)],
        us=28,
        scratch=[pltpu.VMEM((GW, SEQ), BF), pltpu.VMEM((GW, SEQ), F32)],
        prefetch=1,
        after=after,
    )(lengths, tokens, w_qkv, w_qkv, w_qkv, bias)


def attend_backward_kernel(
    groups, direct, halves, where_ref, datt_ref, tok_ref, m_ref, wrefs, q_ref, k_ref, v_ref, p_ref, dp_ref,
    sums_ref, wg_refs, wo, kt, qt, dk_acc, dv_acc, dw_acc, dw_low, wsems, sems,
):
    g = pl.program_id(0)
    row = pl.program_id(1)
    first = groups[0]
    with_out = 0
    last = pl.num_programs(1) - 1
    span = 3 * GW

    def emit(place):
        if direct:
            part = span // halves
            copies = term_copies(
                where_ref,
                lambda owner_rows, h: dw_low.at[owner_rows, h * part : (h + 1) * part],
                D,
                lambda ref, where: ref.at[
                    where + (slice(None), pl.ds(pl.multiple_of(place * part, 128), part))
                ],
                wg_refs,
                sems,
                halves,
            )
        else:
            where = pl.ds(pl.multiple_of(place * span, 128), span)
            copies = [pltpu.make_async_copy(dw_low, wg_refs[0].at[:, where], sems.at[0])]
        start_all(copies)
        wait_all(copies)

    def add_term(term, place):
        @pl.when(row == 0)
        def _():
            dw_acc[...] = term

        @pl.when((row > 0) & (row < last))
        def _():
            dw_acc[...] += term

        @pl.when(row == last)
        def _():
            dw_low[...] = (dw_acc[...] + term).astype(BF)
            emit(place)

    if with_out:

        @pl.when(g == 0)
        def _():
            add_term(t_dot(m_ref[...], datt_ref[...]), 0)

    @pl.when((g == with_out) & (row == 0))
    def _():
        copies = weight_copies("out", wrefs, wo, wsems)
        start_all(copies)
        wait_all(copies)

    def group_step():
        place = g - with_out
        wo_rows = wo[pl.ds(pl.multiple_of((place + first) * GW, GW), GW), :]
        dmix = dot_t(datt_ref[...], wo_rows).astype(BF)
        kt[...] = k_ref[...].astype(F32).T.astype(BF)
        dk_acc[...] = jnp.zeros_like(dk_acc)
        dv_acc[...] = jnp.zeros_like(dv_acc)
        for qb in range(BLOCKS):
            lo, hi = window(qb)
            width = hi - lo
            rows = slice(qb * BLOCK, (qb + 1) * BLOCK)
            for pair in range(PAIRS):
                lanes = slice(pair * 128, (pair + 1) * 128)
                dos = both_heads(dmix[rows, lanes])
                p_low = p_ref[0, pair, qb, :width, :]
                p = p_low.astype(F32)
                dp = dot_t(v_ref[lo:hi, lanes], dos)
                delta = jnp.sum(p * dp, axis=0, keepdims=True)
                ds = (p * (dp - delta)).astype(BF)
                dk_acc[lo:hi, lanes] += dot(ds, both_heads(q_ref[rows, lanes]))
                dv_acc[lo:hi, lanes] += dot(p_low, dos)
                dq = dot(kt[lanes, lo:hi], ds)
                qt[pair * 128 : pair * 128 + HD, rows] = dq[:HD, :BLOCK]
                qt[pair * 128 + HD : (pair + 1) * 128, rows] = dq[HD:, BLOCK:]
        dq = (qt[...] * 0.125).T.astype(BF)
        dv = dv_acc[...].astype(BF)
        dp_ref[:, :GW] = dq
        dp_ref[:, GW : 2 * GW] = dk_acc[...].astype(BF)
        dp_ref[:, 2 * GW :] = dv
        sums = jnp.concatenate(
            [
                jnp.sum(dq.astype(F32), axis=0, keepdims=True),
                jnp.sum(dv.astype(F32), axis=0, keepdims=True),
            ],
            axis=0,
        )
        sums_ref[...] = jnp.where(row == 0, sums, sums_ref[...] + sums)
        add_term(t_dot(tok_ref[...], dp_ref[...]), g)

    if with_out:
        pl.when(g > 0)(group_step)
    else:
        group_step()


RANKS = 16


def term_copies(where_ref, source, total_rows, target, refs, sems, halves):
    me, replica = where_ref[0], where_ref[1]
    rows = total_rows // RANKS
    copies = []
    for j in range(RANKS):
        owner_rows = pl.ds(pl.multiple_of((me ^ j) * rows, rows), rows)
        place = ((j >> 1) & 1, j >> 2)
        for h in range(halves):
            where = ((h ^ replica,) if halves == 2 else ()) + place
            copies.append(
                pltpu.make_async_copy(
                    source(owner_rows, h), target(refs[j & 1], where), sems.at[halves * j + h]
                )
            )
    return copies


def attend_backward(where, datt, tokens, weights, groups, kept, direct, halves, after=()):
    q, k, v, p, mixed = kept
    t = datt.shape[0]
    rows = t // SEQ
    count, first = len(groups), groups[0]
    extra = 0
    group = lambda g: jnp.maximum(g - extra, 0) + first
    row_spec = pl.BlockSpec((SEQ, GW), lambda g, r, *_: (r, group(g)))
    full_row = pl.BlockSpec((SEQ, D), lambda g, r, *_: (r, 0))
    columns = (count + extra) * 3 * GW
    if direct:
        lead = (2, 2, 4) if halves == 2 else (2, 4)
        wg_shapes = [shaped(lead + (D // RANKS, columns // halves), BF)] * 2
    else:
        wg_shapes = [shaped((D, columns), BF)]
    nw, ng = len(weights), len(wg_shapes)

    def kernel(where_ref, datt_ref, tok_ref, m_ref, *refs):
        wrefs, refs = refs[:nw], refs[nw:]
        q_ref, k_ref, v_ref, p_ref, dp_ref, sums_ref = refs[:6]
        wg_refs, scratch = refs[6 : 6 + ng], refs[6 + ng :]
        attend_backward_kernel(
            groups, direct, halves, where_ref, datt_ref, tok_ref, m_ref, wrefs, q_ref, k_ref, v_ref, p_ref,
            dp_ref, sums_ref, wg_refs, *scratch,
        )

    m_spec = pl.BlockSpec((SEQ, D), lambda g, r, *_: (jnp.where(g == 0, r, rows - 1), 0))
    return call(
        kernel,
        (count + extra, rows),
        [full_row, full_row, m_spec if extra else ANY]
        + [ANY] * nw
        + [
            row_spec,
            row_spec,
            row_spec,
            pl.BlockSpec((1,) + p.shape[1:], lambda g, r, *_: (group(g) * rows + r, 0, 0, 0, 0)),
        ],
        [
            pl.BlockSpec(
                (SEQ, 3 * GW), lambda g, r, *_: (jnp.where(g < extra, 0, r), jnp.maximum(g - extra, 0))
            ),
            pl.BlockSpec((2, GW), lambda g, r, *_: (0, jnp.maximum(g - extra, 0))),
        ]
        + [ANY] * ng,
        [shaped((t, count * 3 * GW), BF), shaped((2, count * GW), F32)] + wg_shapes,
        us=1,
        scratch=[
            pltpu.VMEM((D, D), BF),
            pltpu.VMEM((GW, SEQ), BF),
            pltpu.VMEM((GW, SEQ), F32),
            pltpu.VMEM((SEQ, GW), F32),
            pltpu.VMEM((SEQ, GW), F32),
            pltpu.VMEM((D, 3 * GW), F32),
            pltpu.VMEM((D, 3 * GW), BF),
            pltpu.SemaphoreType.DMA((16,)),
            pltpu.SemaphoreType.DMA((2 * RANKS,)),
        ],
        prefetch=1,
        after=after,
    )(where, datt, tokens, mixed, *weights, q, k, v, p)


TB = 256
CH = 768


def normalize(values):
    centered = values - jnp.mean(values, axis=-1, keepdims=True)
    variance = jnp.mean(centered * centered, axis=-1, keepdims=True)
    inverse = lax.rsqrt(variance + epsilon)
    return centered * inverse, inverse


def normalize_back(grad, xhat, inverse):
    mean = jnp.mean(grad, axis=-1, keepdims=True)
    along = jnp.mean(grad * xhat, axis=-1, keepdims=True)
    return (grad - mean - xhat * along) * inverse


def add_rows(ref, rows):
    stacked = jnp.concatenate([jnp.sum(r, axis=0, keepdims=True) for r in rows], axis=0)
    ref[...] = jnp.where(pl.program_id(0) == 0, stacked, ref[...] + stacked)


def middle(lengths, tokens, mixed, weights, vec, bias_up, cot, after=()):
    t = tokens.shape[0]
    nw = len(weights)
    per_row = SEQ // TB

    def kernel(lengths_ref, tok_ref, m_ref, vec_ref, bu_ref, cot_ref, *refs):
        wrefs, refs = refs[:nw], refs[nw:]
        out_ref, nl_ref, act_ref, dd_ref, du_ref, df_ref, da_ref, sums_ref, su_ref, pool_ref = refs[:10]
        wo, wu, wd, gp, so, su, sd = refs[10:]
        i = pl.program_id(0)
        out_copies = weight_copies("out", wrefs, wo, so)
        up_copies = weight_copies("up", wrefs, wu, su)
        down_copies = weight_copies("down", wrefs, wd, sd)

        @pl.when(i == 0)
        def _():
            start_all(out_copies)
            start_all(up_copies)
            start_all(down_copies)
            wait_all(out_copies)

        att = dot(m_ref[...], wo[...]) + vec_ref[0:1, :]
        xhat, inverse = normalize(tok_ref[...].astype(F32) + att)
        normed = xhat * vec_ref[1:2, :] + vec_ref[2:3, :]
        nl = normed.astype(BF)
        nl_ref[...] = nl

        @pl.when(i == 0)
        def _():
            wait_all(up_copies)

        for c in range(0, FF, CH):
            u = dot(nl, wu[:, c : c + CH]) + bu_ref[:, c : c + CH]
            cdf = 0.5 * (1.0 + lax.erf(u * root_half))
            act_ref[:, c : c + CH] = (u * cdf).astype(BF)
            gp[:, c : c + CH] = cdf + u * (jnp.exp(u * u * -0.5) * pdf_scale)

        @pl.when(i == 0)
        def _():
            wait_all(down_copies)

        second = normed + (dot(act_ref[...], wd[...]) + vec_ref[3:4, :])
        xhat_two, inverse_two = normalize(second)
        out = (xhat_two * vec_ref[4:5, :] + vec_ref[5:6, :]).astype(BF)
        out_ref[...] = out
        cot = cot_ref[...].astype(F32)
        d_second = normalize_back(cot * vec_ref[4:5, :], xhat_two, inverse_two)
        dd = d_second.astype(BF)
        dd_ref[...] = dd
        row = i // per_row
        places = lax.broadcasted_iota(jnp.int32, (1, TB), 1) + (i % per_row) * TB
        segment = segment_of(places, lengths_ref, row)
        ids = lax.broadcasted_iota(jnp.int32, (SEGS, TB), 0)
        pooled = dot(jnp.where(segment == ids, 1.0, 0.0).astype(BF), out)
        pooled = jnp.where(i % per_row == 0, pooled, pool_ref[0] + pooled)
        counts = jnp.zeros((SEGS, 1), F32)
        places = lax.broadcasted_iota(jnp.int32, (SEGS, 1), 0)
        for s in range(SEGS):
            counts = jnp.where(places == s, lengths_ref[row, s].astype(F32), counts)
        pool_ref[0] = jnp.where(i % per_row == per_row - 1, pooled / counts, pooled)
        for c in range(0, FF, CH):
            du = (dot_t(dd, wd[c : c + CH, :]) * gp[:, c : c + CH]).astype(BF)
            du_ref[:, c : c + CH] = du
            partial = jnp.sum(du.astype(F32), axis=0, keepdims=True)
            su_ref[:, c : c + CH] = jnp.where(i == 0, partial, su_ref[:, c : c + CH] + partial)
        d_normed = d_second + dot_t(du_ref[...], wu[...])
        d_first = normalize_back(d_normed * vec_ref[1:2, :], xhat, inverse)
        df_ref[...] = d_first
        d_att = d_first.astype(BF)
        da_ref[...] = d_att
        add_rows(
            sums_ref,
            (dd.astype(F32), cot * xhat_two, cot, d_att.astype(F32), d_normed * xhat, d_normed),
        )

    tok = lambda n: pl.BlockSpec((TB, n), lambda i, *_: (i, 0))
    return call(
        kernel,
        (t // TB,),
        [tok(D), tok(D), whole((6, D)), whole((1, FF)), tok(D)] + [ANY] * nw,
        [
            tok(D),
            tok(D),
            tok(FF),
            tok(D),
            tok(FF),
            tok(D),
            tok(D),
            pl.BlockSpec((6, D), lambda i, *_: (0, 0)),
            pl.BlockSpec((1, FF), lambda i, *_: (0, 0)),
            pl.BlockSpec((1, SEGS, D), lambda i, *_: (i // per_row, 0, 0)),
        ],
        [
            shaped((t, D), BF),
            shaped((t, D), BF),
            shaped((t, FF), BF),
            shaped((t, D), BF),
            shaped((t, FF), BF),
            shaped((t, D), F32),
            shaped((t, D), BF),
            shaped((6, D), F32),
            shaped((1, FF), F32),
            shaped((t // SEQ, SEGS, D), F32),
        ],
        us=45,
        scratch=[
            pltpu.VMEM((D, D), BF),
            pltpu.VMEM((D, FF), BF),
            pltpu.VMEM((FF, D), BF),
            pltpu.VMEM((TB, FF), F32),
            pltpu.SemaphoreType.DMA((16,)),
            pltpu.SemaphoreType.DMA((64,)),
            pltpu.SemaphoreType.DMA((16,)),
        ],
        prefetch=1,
        after=after,
    )(lengths, tokens, mixed, vec, bias_up, cot, *weights)


def input_gradient(d_first, d_projected, w_qkv, after=()):
    t = d_first.shape[0]

    def kernel(df_ref, p0, p1, w_ref, out_ref):
        total = df_ref[...]
        g = 0
        for p in (p0, p1):
            for local in range(p.shape[1] // D):
                for part in range(3):
                    start = part * D + g * GW
                    at = local * D + part * GW
                    total = total + dot_t(p[:, at : at + GW], w_ref[:, start : start + GW])
                g += 1
        out_ref[...] = total

    tok = lambda n: pl.BlockSpec((TB, n), lambda i: (i, 0))
    return call(
        kernel,
        (t // TB,),
        [tok(D), tok(d_projected[0].shape[1]), tok(d_projected[1].shape[1]), whole((D, 3 * D))],
        tok(D),
        shaped((t, D), F32),
        us=9,
        after=after,
    )(d_first, *d_projected, w_qkv)


def grad_down_out(active, d_down, mixed, d_att, ranks, direct, after=()):
    t = d_down.shape[0]
    n = 768
    steps = FF // n
    f, r = FF // ranks, D // ranks

    def kernel(a_ref, dd_ref, m_ref, da_ref, *refs):
        outs, (acc, sems) = refs[:-2], refs[-2:]
        i = pl.program_id(0)
        slot = i % 2

        def copies_of(i, slot, last):
            source = acc.at[slot]
            if not direct:
                target = outs[1] if last else outs[0].at[pl.ds(pl.multiple_of(i * n, n), n)]
                return [pltpu.make_async_copy(source, target, sems.at[slot, 0])]
            if last:
                return [
                    pltpu.make_async_copy(
                        source.at[o * r : (o + 1) * r], outs[0].at[o, f : f + r], sems.at[slot, o]
                    )
                    for o in range(ranks)
                ]
            count = n // f
            return [
                pltpu.make_async_copy(
                    source.at[k * f : (k + 1) * f], outs[0].at[i * count + k, :f], sems.at[slot, k]
                )
                for k in range(count)
            ]

        @pl.when(i >= 2)
        def _():
            wait_all(copies_of(i - 2, slot, False))

        @pl.when(i < steps)
        def _():
            acc[slot] = t_dot(a_ref[...], dd_ref[...]).astype(BF)
            start_all(copies_of(i, slot, False))

        @pl.when(i == steps)
        def _():
            acc[slot] = t_dot(m_ref[...], da_ref[...]).astype(BF)
            copies = copies_of(i, slot, True)
            start_all(copies)
            wait_all(copies_of(i - 1, (steps - 1) % 2, False))
            wait_all(copies)

    if direct:
        out_shapes = [shaped((ranks, f + r, D), BF)]
    else:
        out_shapes = [shaped((FF, D), BF), shaped((D, D), BF)]
    return call(
        kernel,
        (steps + 1,),
        [
            pl.BlockSpec((t, n), lambda i: (0, jnp.minimum(i, steps - 1))),
            whole((t, D)),
            whole((t, D)),
            whole((t, D)),
        ],
        [ANY] * len(out_shapes),
        out_shapes,
        us=11,
        scratch=[pltpu.VMEM((2, n, D), BF), pltpu.SemaphoreType.DMA((2, 16))],
        after=after,
    )(active, d_down, mixed, d_att)


STRIP = 384
STRIPS = FF // 2 // STRIP


def grad_up(where, nl, d_upper, direct, after=()):
    t = nl.shape[0]

    def kernel(where_ref, nl_ref, du_ref, *refs):
        outs, (acc, sems) = refs[:-2], refs[-2:]
        h = pl.program_id(0)
        acc[h] = t_dot(nl_ref[...], du_ref[...]).astype(BF)

        def copies_of(h):
            if not direct:
                return [pltpu.make_async_copy(acc.at[h], outs[0].at[h], sems.at[h, 0])]
            me, replica = where_ref[0], where_ref[1]
            rows = D // RANKS
            copies = []
            for j in range(RANKS):
                owner_rows = pl.ds(pl.multiple_of((me ^ j) * rows, rows), rows)
                for strip in range(STRIPS):
                    target = outs[j & 1].at[
                        h ^ replica, (j >> 1) & 1, j >> 2, strip * rows : (strip + 1) * rows
                    ]
                    source = acc.at[h, owner_rows, strip * STRIP : (strip + 1) * STRIP]
                    copies.append(pltpu.make_async_copy(source, target, sems.at[h, len(copies)]))
            return copies

        start_all(copies_of(h))

        @pl.when(h == 1)
        def _():
            wait_all(copies_of(0))
            wait_all(copies_of(1))

    if direct:
        out_shapes = [shaped((2, 2, 4, STRIPS * D // RANKS, STRIP), BF)] * 2
    else:
        out_shapes = [shaped((2, D, FF // 2), BF)]
    return call(
        kernel,
        (2,),
        [whole((t, D)), pl.BlockSpec((t, FF // 2), lambda h, *_: (0, h))],
        [ANY] * len(out_shapes),
        out_shapes,
        us=11,
        scratch=[
            pltpu.VMEM((2, D, FF // 2), BF),
            pltpu.SemaphoreType.DMA((2, RANKS * STRIPS)),
        ],
        prefetch=1,
        after=after,
    )(where, nl, d_upper)


def swap(x, mask):
    return lax.ppermute(x, "fsdp", [(i, i ^ mask) for i in range(RANKS)])


def swap_replica(x):
    return lax.ppermute(x, "replica", [(0, 1), (1, 0)])


def added(*terms):
    total = terms[0].astype(F32)
    for term in terms[1:]:
        total = total + term.astype(F32)
    return total


def gather_qkv(where, own):
    rows, half = own.shape
    columns = 2 * half
    z = jnp.stack([own] + [swap(own, m) for m in (4, 8, 12)])
    zy = jnp.stack([z, swap(z, 2)])
    x = swap_replica(zy)
    pieces = (zy, x, swap(zy, 1), swap(x, 1))

    def kernel(where_ref, p0, p1, p2, p3, out_ref, sems):
        me, other = where_ref[0], where_ref[1]
        copies = []
        for index, piece in enumerate((p0, p1, p2, p3)):
            start = pl.multiple_of((other ^ (index % 2)) * half, 128)
            for y in range(2):
                for k in range(4):
                    owner = me ^ (4 * k + 2 * y + index // 2)
                    target = out_ref.at[
                        pl.ds(pl.multiple_of(owner * rows, rows), rows), pl.ds(start, half)
                    ]
                    copies.append(
                        pltpu.make_async_copy(piece.at[y, k], target, sems.at[len(copies)])
                    )
        start_all(copies)
        wait_all(copies)

    return call(
        kernel,
        (1,),
        [ANY] * 4,
        pl.BlockSpec((RANKS * rows, columns), lambda *_: (0, 0)),
        shaped((RANKS * rows, columns), BF),
        us=4,
        scratch=[pltpu.SemaphoreType.DMA((32,))],
        prefetch=1,
    )(where, *pieces)


def ordered(own, other, replica):
    first = jnp.where(replica == 0, own, other)
    second = jnp.where(replica == 0, other, own)
    return first, second


class Chain:
    def __init__(self, keep, send, lines=None, grow=False, two_steps=False):
        self.columns = keep.shape[-1]
        flat = lambda x: x.reshape(-1, self.columns)
        halves = [(swap_replica,)] if keep.ndim == 5 else []
        over = lambda m: lambda x: swap(x, m)
        along_z = [(over(8),), (over(4),)] if two_steps else [(over(4), over(8), over(12))]
        fsdp = [(over(1),)] + halves + [(over(2),)] + along_z
        self.moves = fsdp + [(swap_replica,)]
        self.owner_rows = keep.shape[-2]
        self.stay, self.away = flat(keep), [flat(send)]
        self.lines = None if lines is None else flat(lines)
        self.ride = [False] * len(self.moves)
        if lines is not None:
            self.ride = [not grow] + [True] * (len(fsdp) - 1) + [not halves]
        self.grow = grow

    def send(self):
        moves = self.moves.pop(0)
        self.received = [move(x) for move, x in zip(moves, self.away)]
        self.beside = []
        self.arriving = self.ride.pop(0)
        if self.arriving and len(self.received[0]) == len(self.stay):
            self.beside = [moves[0](self.lines)]


def add_all(chains, after=(), passing=()):
    operands, shapes, plans = [], [], []
    for c in chains:
        n = c.stay.shape[0]
        parts = len(c.moves[0]) + 1 if n > c.owner_rows else 1
        part = n // parts
        lines = c.lines.shape[0] if c.arriving or c.ride[0] else 0
        held = lines if c.arriving else 0
        grown = held * (2 if c.grow else 1)
        rides = (grown or lines) if c.ride[0] else 0
        ins = [c.stay] + c.received + (c.beside + [c.lines] if lines else [])
        outs = [shaped((part, c.columns), BF)]
        sends = parts - 1 if parts > 1 else int(rides > 0)
        outs += [shaped((part + rides, c.columns), BF)] * sends
        if held:
            outs.append(shaped((grown, c.columns), BF))
        plans.append((len(ins), len(outs), n, part, parts, sends, held, rides, len(c.received), len(c.beside), c.grow))
        operands += ins
        shapes += outs

    passed, inputs = len(passing), len(operands)

    def kernel(*refs):
        sources, targets = refs[: len(operands)], refs[len(operands) + passed :]
        for n_in, n_out, n, part, parts, sends, held, rides, arrivals, beside, grow in plans:
            ins, sources = sources[:n_in], sources[n_in:]
            outs, targets = targets[:n_out], targets[n_out:]
            received = ins[1 : 1 + arrivals]
            for p in range(parts):
                rows = slice(p * part, (p + 1) * part)
                total = ins[0][rows, :].astype(F32)
                for r in received:
                    total = total + r[rows, :].astype(F32)
                total = total.astype(BF)
                outs[p][:part, :] = total
                if parts == 1 and sends:
                    outs[1][:part, :] = total
            if held:
                mine = ins[-1][...]
                if beside:
                    others = [ins[1 + arrivals][...]]
                else:
                    others = [r[n : n + held, :] for r in received]
                if grow:
                    lines = jnp.concatenate([mine, others[0]], axis=0)
                else:
                    total = mine.astype(F32)
                    for other in others:
                        total = total + other.astype(F32)
                    lines = total.astype(BF)
                outs[-1][...] = lines
            elif rides:
                lines = ins[-1][...]
            if rides:
                for out in outs[1 : 1 + sends]:
                    out[part:, :] = lines

    results = list(
        call(
            kernel,
            (1,),
            [whole(x.shape) for x in operands] + [ANY] * passed,
            [whole(x.shape) for x in shapes] + [ANY] * passed,
            shapes + [shaped(x.shape, x.dtype) for x in passing],
            us=2,
            after=after,
            aliases={inputs + i: len(shapes) + i for i in range(passed)},
        )(*operands, *passing)
    )
    for c, plan in zip(chains, plans):
        n_out, sends, held = plan[1], plan[5], plan[6]
        mine, results = results[:n_out], results[n_out:]
        c.stay = mine[0]
        c.away = mine[1 : 1 + sends] if sends else [mine[0]]
        if held:
            c.lines = mine[-1]
    return results


SMALL = ("bias_qv", "bias_out", "gain_one", "shift_one", "bias_up", "bias_down", "gain_two", "shift_two")
SMALL_SIZES = (2 * D, D, D, D, FF, D, D, D)
PAD = 256


def body(
    ranks,
    replicas,
    tokens,
    lengths,
    w_qkv,
    bias_qv,
    w_out,
    bias_out,
    gain_one,
    shift_one,
    w_up,
    bias_up,
    w_down,
    bias_down,
    gain_two,
    shift_two,
    cotangent,
):
    direct = ranks == RANKS and replicas == 2
    me = lax.axis_index("fsdp")
    replica = lax.axis_index("replica")
    where = jnp.stack([me, replica]).astype(jnp.int32)
    gather = lambda w: lax.all_gather(w, "fsdp", axis=0, tiled=True)

    small = (bias_qv, bias_out, gain_one, shift_one, bias_up, bias_down, gain_two, shift_two)
    if direct:
        packed, own = pack_weights(where, w_qkv, small, w_out, w_up, w_down)
        w_first = gather_qkv(where, own)
        weights = (gather(packed).reshape(ranks, -1, D),)
    else:
        w_first = gather(w_qkv)
        weights = (gather(w_out), gather(w_up), gather(w_down))
    vectors = {}
    if direct:
        beside = w_first[:, 3 * D :].reshape(ranks, -1, PAD)
    for k, (name, value) in enumerate(zip(SMALL, small)):
        got = beside[:, k, : value.shape[0]].reshape(-1) if direct else gather(value)
        vectors[name] = got.astype(F32)

    bias = vectors["bias_qv"].reshape(2, GROUPS, GW).transpose(1, 0, 2)
    kept = attend_forward(lengths, tokens, w_first, bias)
    mixed = kept[4]
    vec = jnp.stack(
        [
            vectors[n]
            for n in ("bias_out", "gain_one", "shift_one", "bias_down", "gain_two", "shift_two")
        ]
    )
    (layer_out, nl, active, d_down, d_upper, d_first, d_att, sums, sums_up, pooled) = middle(
        lengths, tokens, mixed, weights, vec, vectors["bias_up"][None], cotangent
    )

    terms_down = grad_down_out(active, d_down, mixed, d_att, ranks, direct)
    terms_up = grad_up(where, nl, d_upper, direct, after=(terms_down[0],))
    scatter = lambda x: lax.psum_scatter(x, "fsdp", scatter_dimension=0, tiled=True)

    def small_lines(sums_a, sums_b):
        both = jnp.concatenate([sums_a, sums_b], axis=1)
        return jnp.concatenate([both, sums[3:], sums_up.reshape(-1, D), sums[:3]])

    attend_back = functools.partial(attend_backward, where, d_att, tokens, weights)
    if direct:
        chain_u = Chain(*terms_up, two_steps=True)
        chain_u.send()
        add_all([chain_u])
        shard_down = scatter(terms_down[0].reshape(-1, D))
        shard_other = swap_replica(shard_down)
        chain_u.send()
        dp_a, sums_a, *terms_a = attend_back((0, 1), kept, True, 2, after=(chain_u.away[0],))
        chain_a = Chain(*terms_a, pooled.astype(BF), grow=True, two_steps=True)
        (chain_a.away[0],) = add_all([chain_u], after=(sums_a,), passing=(chain_a.away[0],))
        chain_u.send()
        chain_a.send()
        add_all([chain_a])
        chain_a.send()
        dp_b, sums_b, *terms_b = attend_back((2,), kept, True, 1, after=(chain_a.away[0],))
        small = small_lines(sums_a, sums_b)
        small = jnp.pad(small, ((0, -small.shape[0] % 16), (0, 0))).astype(BF)
        chain_b = Chain(*terms_b, small)
        chain_b.send()
        add_all([chain_u, chain_a], after=(sums_b,))
        chain_u.send()
        chain_a.send()
        input_grad = input_gradient(
            d_first, (dp_a, dp_b), w_first, after=(chain_a.away[0],)
        )
        add_all([chain_u, chain_a, chain_b], after=(input_grad,))
        chain_u.send()
        chain_a.send()
        chain_b.send()
        while chain_u.moves or chain_a.moves or chain_b.moves:
            moving = [c for c in (chain_u, chain_a, chain_b) if c.moves]
            last = all(len(c.moves) == 1 for c in moving)
            add_all(moving, after=(shard_other,) if last else ())
            for c in moving:
                c.send()
        halves_u = ordered(chain_u.stay, chain_u.received[0][: chain_u.owner_rows], replica)
        halves_u = [
            h.reshape(STRIPS, -1, STRIP).transpose(1, 0, 2).reshape(-1, STRIPS * STRIP)
            for h in halves_u
        ]
        both = added(shard_down, shard_other)
        grad_w_down, grad_w_out = both[: FF // ranks], both[FF // ranks :]
        lines = chain_a.lines.reshape((2,) * 4 + pooled.shape)
        relative = jnp.stack([lines, swap(lines, 1)]).transpose(4, 2, 1, 3, 0, 5, 6, 7)
        relative = relative.reshape((2, ranks) + pooled.shape)
        pooled_all = relative[jnp.arange(2) ^ replica][:, me ^ jnp.arange(ranks)]
        pooled_all = pooled_all.reshape((2 * ranks * pooled.shape[0],) + pooled.shape[1:]).astype(F32)
        h0, h1 = ordered(chain_a.stay, chain_a.received[0], replica)
        span = 3 * GW // 2
        halves_a = [
            jnp.concatenate([h[:, i * span : (i + 1) * span] for h in (h0, h1)], axis=1).astype(F32)
            for i in range(2)
        ]
        sum_b = added(chain_b.stay, chain_b.received[0][: chain_b.owner_rows])
        lines = added(chain_b.lines, chain_b.received[0][chain_b.owner_rows :])
        parts = halves_a + [sum_b]
    else:
        dp_a, sums_a, term_a = attend_back((0, 1), kept, False, 1)
        dp_b, sums_b, term_b = attend_back((2,), kept, False, 1)
        input_grad = input_gradient(d_first, (dp_a, dp_b), w_first)
        pooled_all = lax.all_gather(pooled, ("replica", "fsdp"), axis=0, tiled=True)
        reduce = lambda x: lax.psum(scatter(x), "replica").astype(F32)
        grad_w_down, grad_w_out = reduce(terms_down[0]), reduce(terms_down[1])
        halves_u = [reduce(terms_up[0][h]) for h in range(2)]
        sum_a, sum_b = reduce(term_a), reduce(term_b)
        lines = lax.psum(small_lines(sums_a, sums_b), ("replica", "fsdp"))
        parts = [sum_a[:, :D], sum_a[:, D:], sum_b]
    grad_w_up = jnp.concatenate(halves_u, axis=1).astype(F32)
    grad_w_qkv = jnp.concatenate(
        [p[:, i * GW : (i + 1) * GW] for i in range(3) for p in parts], axis=1
    )
    small_grads, start = {}, 0
    for name, size in zip(SMALL, SMALL_SIZES):
        values = lines[start // D : (start + size) // D].reshape(ranks, -1)
        small_grads[name] = lax.dynamic_index_in_dim(values, me, keepdims=False)
        start += size
    return (
        layer_out,
        input_grad,
        pooled_all,
        grad_w_qkv,
        small_grads["bias_qv"],
        grad_w_out,
        small_grads["bias_out"],
        small_grads["gain_one"],
        small_grads["shift_one"],
        grad_w_up,
        small_grads["bias_up"],
        grad_w_down,
        small_grads["bias_down"],
        small_grads["gain_two"],
        small_grads["shift_two"],
    )


def solution(mesh):
    rows = P(("replica", "fsdp"), None)
    matrix = P("fsdp", None)
    vector = P("fsdp")
    return jax.shard_map(
        functools.partial(body, mesh.shape["fsdp"], mesh.shape["replica"]),
        mesh=mesh,
        in_specs=(
            rows,
            rows,
            matrix,
            vector,
            matrix,
            vector,
            vector,
            vector,
            matrix,
            vector,
            matrix,
            vector,
            vector,
            vector,
            rows,
        ),
        out_specs=(
            rows,
            rows,
            P(),
            matrix,
            vector,
            matrix,
            vector,
            vector,
            vector,
            matrix,
            vector,
            matrix,
            vector,
            vector,
            vector,
        ),
        check_vma=False,
    )
```

```python
import functools

import jax
import jax.numpy as jnp
from jax import lax
from jax.experimental import pallas as pl
from jax.experimental.pallas import tpu as pltpu
from jax.sharding import PartitionSpec as P

D = 768
H = 12
HD = 64
FF = 3072
SEQ = 512
SEGS = 8
GROUPS = 3
GW = D // GROUPS
PAIRS = GW // 128
BLOCK = 128
BLOCKS = SEQ // BLOCK
WIDE = 3 * BLOCK

epsilon = 1e-12
root_half = 0.7071067811865476
masked_score = -1e30
pdf_scale = 0.3989422804014327

BF = jnp.bfloat16
F32 = jnp.float32
VMEM_LIMIT = 56 * 2**20


def dot(a, b):
    return jnp.dot(a, b, preferred_element_type=F32)


def dot_t(a, b):
    return lax.dot_general(a, b, (((1,), (1,)), ((), ())), preferred_element_type=F32)


def t_dot(a, b):
    return lax.dot_general(a, b, (((0,), (0,)), ((), ())), preferred_element_type=F32)


def window(qb):
    return max(0, (qb - 1) * BLOCK), min(SEQ, (qb + 2) * BLOCK)


def call(
    kernel, grid, in_specs, out_specs, out_shape, us, scratch=(), prefetch=0, after=(), aliases=None
):
    first = prefetch + len(in_specs)

    def run(*refs):
        kernel(*refs[:first], *refs[first + len(after) :])

    return functools.partial(
        lambda extra, *args: pl.pallas_call(
            run,
            grid_spec=pltpu.PrefetchScalarGridSpec(
                num_scalar_prefetch=prefetch,
                grid=grid,
                in_specs=list(in_specs) + [pl.BlockSpec(memory_space=pl.ANY)] * len(extra),
                out_specs=out_specs,
                scratch_shapes=list(scratch),
            ),
            out_shape=out_shape,
            input_output_aliases=aliases or {},
            compiler_params=pltpu.CompilerParams(vmem_limit_bytes=VMEM_LIMIT),
            cost_estimate=pl.CostEstimate(
                flops=int(us * 1.15e9), bytes_accessed=int(us * 3.6e6), transcendentals=0
            ),
        )(*args, *extra),
        tuple(after),
    )


def shaped(shape, dtype):
    return jax.ShapeDtypeStruct(shape, dtype)


def whole(shape):
    return pl.BlockSpec(shape, lambda *_: (0,) * len(shape), pipeline_mode=pl.Buffered(1))


ANY = pl.BlockSpec(memory_space=pl.ANY)


def pack_weights(where, w_qkv, small, w_out, w_up, w_down):
    r, f = w_out.shape[0], w_down.shape[0]
    columns = w_qkv.shape[1]
    half = (columns + PAD) // 2
    count = len(small)

    def kernel(where_ref, q_ref, wo_ref, wu_ref, wd_ref, *refs):
        s_refs, (out_ref, own_ref) = refs[:count], refs[count:]
        out_ref[:r, :] = wo_ref[...]
        for i in range(FF // D):
            out_ref[(1 + i) * r : (2 + i) * r, :] = wu_ref[:, i * D : (i + 1) * D]
        out_ref[5 * r :, :] = wd_ref[...]

        @pl.when(where_ref[1] == 0)
        def _():
            own_ref[...] = q_ref[:, :half]

        @pl.when(where_ref[1] > 0)
        def _():
            own_ref[:, : columns - half] = q_ref[:, half:]
            rows = []
            for s_ref in s_refs:
                v = s_ref[...].astype(F32)
                rows.append(jnp.concatenate([v, jnp.zeros((1, PAD - v.shape[1]), F32)], axis=1))
            rows.append(jnp.zeros((r - count, PAD), F32))
            own_ref[:, columns - half :] = jnp.concatenate(rows, axis=0).astype(BF)

    operands = (w_qkv, w_out, w_up, w_down) + tuple(v[None] for v in small)
    shapes = [shaped((5 * r + f, D), BF), shaped((r, half), BF)]
    return call(
        kernel,
        (1,),
        [whole(x.shape) for x in operands],
        [whole(x.shape) for x in shapes],
        shapes,
        us=2,
        prefetch=1,
    )(where, *operands)


def weight_copies(name, refs, target, sems):
    if len(refs) == 3:
        source = refs[("out", "up", "down").index(name)]
        return [pltpu.make_async_copy(source, target, sems.at[0])]
    packed = refs[0]
    ranks = packed.shape[0]
    r = D // ranks
    copies = []
    for o in range(ranks):
        if name == "out":
            parts = [(slice(0, r), target.at[o * r : (o + 1) * r])]
        elif name == "up":
            parts = [
                (
                    slice((1 + i) * r, (2 + i) * r),
                    target.at[o * r : (o + 1) * r, i * D : (i + 1) * D],
                )
                for i in range(FF // D)
            ]
        else:
            n = FF // ranks
            parts = [(slice(5 * r, 5 * r + n), target.at[o * n : (o + 1) * n])]
        for rows, where in parts:
            copies.append(pltpu.make_async_copy(packed.at[o, rows], where, sems.at[len(copies)]))
    return copies


def start_all(copies):
    for copy in copies:
        copy.start()


def wait_all(copies):
    for copy in copies:
        copy.wait()


def segment_of(places, lengths_ref, row):
    total = jnp.int32(0)
    segment = jnp.zeros(places.shape, jnp.int32)
    for s in range(SEGS):
        total = total + lengths_ref[row, s]
        segment = segment + (places >= total).astype(jnp.int32)
    return segment


def both_heads(x2):
    low = lax.broadcasted_iota(jnp.int32, (1, 128), 1) < HD
    zero = jnp.zeros_like(x2)
    return jnp.concatenate([jnp.where(low, x2, zero), jnp.where(low, zero, x2)], axis=0)


def attend_forward_kernel(
    lengths_ref, tok_ref, wq_ref, wk_ref, wv_ref, bias_ref, q_ref, k_ref, v_ref, p_ref, m_ref, vt, ot
):
    row = pl.program_id(1)
    tok = tok_ref[...]
    q_ref[...] = (dot(tok, wq_ref[...]) + bias_ref[0, 0:1, :]).astype(BF) * jnp.asarray(0.125, BF)
    k_ref[...] = dot(tok, wk_ref[...]).astype(BF)
    v = dot(tok, wv_ref[...]) + bias_ref[0, 1:2, :]
    v_ref[...] = v.astype(BF)
    vt[...] = v.T.astype(BF)
    for qb in range(BLOCKS):
        lo, hi = window(qb)
        width = hi - lo
        rows = slice(qb * BLOCK, (qb + 1) * BLOCK)
        seg_q = segment_of(
            lax.broadcasted_iota(jnp.int32, (1, BLOCK), 1) + qb * BLOCK, lengths_ref, row
        )
        seg_k = segment_of(
            lax.broadcasted_iota(jnp.int32, (width, 1), 0) + lo, lengths_ref, row
        )
        mask = jnp.where(jnp.concatenate([seg_q, seg_q], axis=1) == seg_k, 0.0, masked_score)
        for pair in range(PAIRS):
            lanes = slice(pair * 128, (pair + 1) * 128)
            s = dot_t(k_ref[lo:hi, lanes], both_heads(q_ref[rows, lanes])) + mask
            w = jnp.exp(s - jnp.max(s, axis=0, keepdims=True))
            p = (w * (1.0 / jnp.sum(w, axis=0, keepdims=True))).astype(BF)
            p_ref[0, pair, qb, :width, :] = p
            o = dot(vt[lanes, lo:hi], p)
            ot[pair * 128 : pair * 128 + HD, rows] = o[:HD, :BLOCK]
            ot[pair * 128 + HD : (pair + 1) * 128, rows] = o[HD:, BLOCK:]
    m_ref[...] = ot[...].T.astype(BF)


def attend_forward(lengths, tokens, w_qkv, bias, after=()):
    t = tokens.shape[0]
    rows = t // SEQ
    row_spec = pl.BlockSpec((SEQ, GW), lambda g, r, *_: (r, g))
    p_shape = (GROUPS * rows, PAIRS, BLOCKS, WIDE, 2 * BLOCK)
    column = lambda part: pl.BlockSpec((D, GW), lambda g, r, *_: (0, part * GROUPS + g))
    return call(
        attend_forward_kernel,
        (GROUPS, rows),
        [
            pl.BlockSpec((SEQ, D), lambda g, r, *_: (r, 0)),
            column(0),
            column(1),
            column(2),
            pl.BlockSpec((1, 2, GW), lambda g, r, *_: (g, 0, 0)),
        ],
        [row_spec] * 3
        + [pl.BlockSpec((1,) + p_shape[1:], lambda g, r, *_: (g * rows + r, 0, 0, 0, 0)), row_spec],
        [shaped((t, D), BF)] * 3 + [shaped(p_shape, BF), shaped((t, D), BF)],
        us=28,
        scratch=[pltpu.VMEM((GW, SEQ), BF), pltpu.VMEM((GW, SEQ), F32)],
        prefetch=1,
        after=after,
    )(lengths, tokens, w_qkv, w_qkv, w_qkv, bias)


def attend_backward_kernel(
    groups, direct, halves, where_ref, datt_ref, tok_ref, m_ref, wrefs, q_ref, k_ref, v_ref, p_ref, dp_ref,
    sums_ref, wg_refs, wo, kt, qt, dk_acc, dv_acc, dw_acc, dw_low, wsems, sems,
):
    g = pl.program_id(0)
    row = pl.program_id(1)
    first = groups[0]
    with_out = 0
    last = pl.num_programs(1) - 1
    span = 3 * GW

    def emit(place):
        if direct:
            part = span // halves
            copies = term_copies(
                where_ref,
                lambda owner_rows, h: dw_low.at[owner_rows, h * part : (h + 1) * part],
                D,
                lambda ref, where: ref.at[
                    where + (slice(None), pl.ds(pl.multiple_of(place * part, 128), part))
                ],
                wg_refs,
                sems,
                halves,
            )
        else:
            where = pl.ds(pl.multiple_of(place * span, 128), span)
            copies = [pltpu.make_async_copy(dw_low, wg_refs[0].at[:, where], sems.at[0])]
        start_all(copies)
        wait_all(copies)

    def add_term(term, place):
        @pl.when(row == 0)
        def _():
            dw_acc[...] = term

        @pl.when((row > 0) & (row < last))
        def _():
            dw_acc[...] += term

        @pl.when(row == last)
        def _():
            dw_low[...] = (dw_acc[...] + term).astype(BF)
            emit(place)

    if with_out:

        @pl.when(g == 0)
        def _():
            add_term(t_dot(m_ref[...], datt_ref[...]), 0)

    @pl.when((g == with_out) & (row == 0))
    def _():
        copies = weight_copies("out", wrefs, wo, wsems)
        start_all(copies)
        wait_all(copies)

    def group_step():
        place = g - with_out
        wo_rows = wo[pl.ds(pl.multiple_of((place + first) * GW, GW), GW), :]
        dmix = dot_t(datt_ref[...], wo_rows).astype(BF)
        kt[...] = k_ref[...].astype(F32).T.astype(BF)
        dk_acc[...] = jnp.zeros_like(dk_acc)
        dv_acc[...] = jnp.zeros_like(dv_acc)
        for qb in range(BLOCKS):
            lo, hi = window(qb)
            width = hi - lo
            rows = slice(qb * BLOCK, (qb + 1) * BLOCK)
            for pair in range(PAIRS):
                lanes = slice(pair * 128, (pair + 1) * 128)
                dos = both_heads(dmix[rows, lanes])
                p_low = p_ref[0, pair, qb, :width, :]
                p = p_low.astype(F32)
                dp = dot_t(v_ref[lo:hi, lanes], dos)
                delta = jnp.sum(p * dp, axis=0, keepdims=True)
                ds = (p * (dp - delta)).astype(BF)
                dk_acc[lo:hi, lanes] += dot(ds, both_heads(q_ref[rows, lanes]))
                dv_acc[lo:hi, lanes] += dot(p_low, dos)
                dq = dot(kt[lanes, lo:hi], ds)
                qt[pair * 128 : pair * 128 + HD, rows] = dq[:HD, :BLOCK]
                qt[pair * 128 + HD : (pair + 1) * 128, rows] = dq[HD:, BLOCK:]
        dq = (qt[...] * 0.125).T.astype(BF)
        dv = dv_acc[...].astype(BF)
        dp_ref[:, :GW] = dq
        dp_ref[:, GW : 2 * GW] = dk_acc[...].astype(BF)
        dp_ref[:, 2 * GW :] = dv
        sums = jnp.concatenate(
            [
                jnp.sum(dq.astype(F32), axis=0, keepdims=True),
                jnp.sum(dv.astype(F32), axis=0, keepdims=True),
            ],
            axis=0,
        )
        sums_ref[...] = jnp.where(row == 0, sums, sums_ref[...] + sums)
        add_term(t_dot(tok_ref[...], dp_ref[...]), g)

    if with_out:
        pl.when(g > 0)(group_step)
    else:
        group_step()


RANKS = 16


def term_copies(where_ref, source, total_rows, target, refs, sems, halves):
    me, replica = where_ref[0], where_ref[1]
    rows = total_rows // RANKS
    copies = []
    for j in range(RANKS):
        owner_rows = pl.ds(pl.multiple_of((me ^ j) * rows, rows), rows)
        place = ((j >> 1) & 1, j >> 2)
        for h in range(halves):
            where = ((h ^ replica,) if halves == 2 else ()) + place
            copies.append(
                pltpu.make_async_copy(
                    source(owner_rows, h), target(refs[j & 1], where), sems.at[halves * j + h]
                )
            )
    return copies


def attend_backward(where, datt, tokens, weights, groups, kept, direct, halves, after=()):
    q, k, v, p, mixed = kept
    t = datt.shape[0]
    rows = t // SEQ
    count, first = len(groups), groups[0]
    extra = 0
    group = lambda g: jnp.maximum(g - extra, 0) + first
    row_spec = pl.BlockSpec((SEQ, GW), lambda g, r, *_: (r, group(g)))
    full_row = pl.BlockSpec((SEQ, D), lambda g, r, *_: (r, 0))
    columns = (count + extra) * 3 * GW
    if direct:
        lead = (2, 2, 4) if halves == 2 else (2, 4)
        wg_shapes = [shaped(lead + (D // RANKS, columns // halves), BF)] * 2
    else:
        wg_shapes = [shaped((D, columns), BF)]
    nw, ng = len(weights), len(wg_shapes)

    def kernel(where_ref, datt_ref, tok_ref, m_ref, *refs):
        wrefs, refs = refs[:nw], refs[nw:]
        q_ref, k_ref, v_ref, p_ref, dp_ref, sums_ref = refs[:6]
        wg_refs, scratch = refs[6 : 6 + ng], refs[6 + ng :]
        attend_backward_kernel(
            groups, direct, halves, where_ref, datt_ref, tok_ref, m_ref, wrefs, q_ref, k_ref, v_ref, p_ref,
            dp_ref, sums_ref, wg_refs, *scratch,
        )

    m_spec = pl.BlockSpec((SEQ, D), lambda g, r, *_: (jnp.where(g == 0, r, rows - 1), 0))
    return call(
        kernel,
        (count + extra, rows),
        [full_row, full_row, m_spec if extra else ANY]
        + [ANY] * nw
        + [
            row_spec,
            row_spec,
            row_spec,
            pl.BlockSpec((1,) + p.shape[1:], lambda g, r, *_: (group(g) * rows + r, 0, 0, 0, 0)),
        ],
        [
            pl.BlockSpec(
                (SEQ, 3 * GW), lambda g, r, *_: (jnp.where(g < extra, 0, r), jnp.maximum(g - extra, 0))
            ),
            pl.BlockSpec((2, GW), lambda g, r, *_: (0, jnp.maximum(g - extra, 0))),
        ]
        + [ANY] * ng,
        [shaped((t, count * 3 * GW), BF), shaped((2, count * GW), F32)] + wg_shapes,
        us=1,
        scratch=[
            pltpu.VMEM((D, D), BF),
            pltpu.VMEM((GW, SEQ), BF),
            pltpu.VMEM((GW, SEQ), F32),
            pltpu.VMEM((SEQ, GW), F32),
            pltpu.VMEM((SEQ, GW), F32),
            pltpu.VMEM((D, 3 * GW), F32),
            pltpu.VMEM((D, 3 * GW), BF),
            pltpu.SemaphoreType.DMA((16,)),
            pltpu.SemaphoreType.DMA((2 * RANKS,)),
        ],
        prefetch=1,
        after=after,
    )(where, datt, tokens, mixed, *weights, q, k, v, p)


TB = 256
CH = 768


def normalize(values):
    centered = values - jnp.mean(values, axis=-1, keepdims=True)
    variance = jnp.mean(centered * centered, axis=-1, keepdims=True)
    inverse = lax.rsqrt(variance + epsilon)
    return centered * inverse, inverse


def normalize_back(grad, xhat, inverse):
    mean = jnp.mean(grad, axis=-1, keepdims=True)
    along = jnp.mean(grad * xhat, axis=-1, keepdims=True)
    return (grad - mean - xhat * along) * inverse


def add_rows(ref, rows):
    stacked = jnp.concatenate([jnp.sum(r, axis=0, keepdims=True) for r in rows], axis=0)
    ref[...] = jnp.where(pl.program_id(0) == 0, stacked, ref[...] + stacked)


def middle(lengths, tokens, mixed, weights, vec, bias_up, cot, after=()):
    t = tokens.shape[0]
    nw = len(weights)
    per_row = SEQ // TB

    def kernel(lengths_ref, tok_ref, m_ref, vec_ref, bu_ref, cot_ref, *refs):
        wrefs, refs = refs[:nw], refs[nw:]
        out_ref, nl_ref, act_ref, dd_ref, du_ref, df_ref, da_ref, sums_ref, su_ref, pool_ref = refs[:10]
        wo, wu, wd, gp, so, su, sd = refs[10:]
        i = pl.program_id(0)
        out_copies = weight_copies("out", wrefs, wo, so)
        up_copies = weight_copies("up", wrefs, wu, su)
        down_copies = weight_copies("down", wrefs, wd, sd)

        @pl.when(i == 0)
        def _():
            start_all(out_copies)
            start_all(up_copies)
            start_all(down_copies)
            wait_all(out_copies)

        att = dot(m_ref[...], wo[...]) + vec_ref[0:1, :]
        xhat, inverse = normalize(tok_ref[...].astype(F32) + att)
        normed = xhat * vec_ref[1:2, :] + vec_ref[2:3, :]
        nl = normed.astype(BF)
        nl_ref[...] = nl

        @pl.when(i == 0)
        def _():
            wait_all(up_copies)

        for c in range(0, FF, CH):
            u = dot(nl, wu[:, c : c + CH]) + bu_ref[:, c : c + CH]
            cdf = 0.5 * (1.0 + lax.erf(u * root_half))
            act_ref[:, c : c + CH] = (u * cdf).astype(BF)
            gp[:, c : c + CH] = cdf + u * (jnp.exp(u * u * -0.5) * pdf_scale)

        @pl.when(i == 0)
        def _():
            wait_all(down_copies)

        second = normed + (dot(act_ref[...], wd[...]) + vec_ref[3:4, :])
        xhat_two, inverse_two = normalize(second)
        out = (xhat_two * vec_ref[4:5, :] + vec_ref[5:6, :]).astype(BF)
        out_ref[...] = out
        cot = cot_ref[...].astype(F32)
        d_second = normalize_back(cot * vec_ref[4:5, :], xhat_two, inverse_two)
        dd = d_second.astype(BF)
        dd_ref[...] = dd
        row = i // per_row
        places = lax.broadcasted_iota(jnp.int32, (1, TB), 1) + (i % per_row) * TB
        segment = segment_of(places, lengths_ref, row)
        ids = lax.broadcasted_iota(jnp.int32, (SEGS, TB), 0)
        pooled = dot(jnp.where(segment == ids, 1.0, 0.0).astype(BF), out)
        pooled = jnp.where(i % per_row == 0, pooled, pool_ref[0] + pooled)
        counts = jnp.zeros((SEGS, 1), F32)
        places = lax.broadcasted_iota(jnp.int32, (SEGS, 1), 0)
        for s in range(SEGS):
            counts = jnp.where(places == s, lengths_ref[row, s].astype(F32), counts)
        pool_ref[0] = jnp.where(i % per_row == per_row - 1, pooled / counts, pooled)
        for c in range(0, FF, CH):
            du = (dot_t(dd, wd[c : c + CH, :]) * gp[:, c : c + CH]).astype(BF)
            du_ref[:, c : c + CH] = du
            partial = jnp.sum(du.astype(F32), axis=0, keepdims=True)
            su_ref[:, c : c + CH] = jnp.where(i == 0, partial, su_ref[:, c : c + CH] + partial)
        d_normed = d_second + dot_t(du_ref[...], wu[...])
        d_first = normalize_back(d_normed * vec_ref[1:2, :], xhat, inverse)
        df_ref[...] = d_first
        d_att = d_first.astype(BF)
        da_ref[...] = d_att
        add_rows(
            sums_ref,
            (dd.astype(F32), cot * xhat_two, cot, d_att.astype(F32), d_normed * xhat, d_normed),
        )

    tok = lambda n: pl.BlockSpec((TB, n), lambda i, *_: (i, 0))
    return call(
        kernel,
        (t // TB,),
        [tok(D), tok(D), whole((6, D)), whole((1, FF)), tok(D)] + [ANY] * nw,
        [
            tok(D),
            tok(D),
            tok(FF),
            tok(D),
            tok(FF),
            tok(D),
            tok(D),
            pl.BlockSpec((6, D), lambda i, *_: (0, 0)),
            pl.BlockSpec((1, FF), lambda i, *_: (0, 0)),
            pl.BlockSpec((1, SEGS, D), lambda i, *_: (i // per_row, 0, 0)),
        ],
        [
            shaped((t, D), BF),
            shaped((t, D), BF),
            shaped((t, FF), BF),
            shaped((t, D), BF),
            shaped((t, FF), BF),
            shaped((t, D), F32),
            shaped((t, D), BF),
            shaped((6, D), F32),
            shaped((1, FF), F32),
            shaped((t // SEQ, SEGS, D), F32),
        ],
        us=45,
        scratch=[
            pltpu.VMEM((D, D), BF),
            pltpu.VMEM((D, FF), BF),
            pltpu.VMEM((FF, D), BF),
            pltpu.VMEM((TB, FF), F32),
            pltpu.SemaphoreType.DMA((16,)),
            pltpu.SemaphoreType.DMA((64,)),
            pltpu.SemaphoreType.DMA((16,)),
        ],
        prefetch=1,
        after=after,
    )(lengths, tokens, mixed, vec, bias_up, cot, *weights)


def input_gradient(d_first, d_projected, w_qkv, after=()):
    t = d_first.shape[0]

    def kernel(df_ref, p0, p1, w_ref, out_ref):
        total = df_ref[...]
        g = 0
        for p in (p0, p1):
            for local in range(p.shape[1] // D):
                for part in range(3):
                    start = part * D + g * GW
                    at = local * D + part * GW
                    total = total + dot_t(p[:, at : at + GW], w_ref[:, start : start + GW])
                g += 1
        out_ref[...] = total

    tok = lambda n: pl.BlockSpec((TB, n), lambda i: (i, 0))
    return call(
        kernel,
        (t // TB,),
        [tok(D), tok(d_projected[0].shape[1]), tok(d_projected[1].shape[1]), whole((D, 3 * D))],
        tok(D),
        shaped((t, D), F32),
        us=9,
        after=after,
    )(d_first, *d_projected, w_qkv)


def grad_down_out(active, d_down, mixed, d_att, ranks, direct, after=()):
    t = d_down.shape[0]
    n = 768
    steps = FF // n
    f, r = FF // ranks, D // ranks

    def kernel(a_ref, dd_ref, m_ref, da_ref, *refs):
        outs, (acc, sems) = refs[:-2], refs[-2:]
        i = pl.program_id(0)
        slot = i % 2

        def copies_of(i, slot, last):
            source = acc.at[slot]
            if not direct:
                target = outs[1] if last else outs[0].at[pl.ds(pl.multiple_of(i * n, n), n)]
                return [pltpu.make_async_copy(source, target, sems.at[slot, 0])]
            if last:
                return [
                    pltpu.make_async_copy(
                        source.at[o * r : (o + 1) * r], outs[0].at[o, f : f + r], sems.at[slot, o]
                    )
                    for o in range(ranks)
                ]
            count = n // f
            return [
                pltpu.make_async_copy(
                    source.at[k * f : (k + 1) * f], outs[0].at[i * count + k, :f], sems.at[slot, k]
                )
                for k in range(count)
            ]

        @pl.when(i >= 2)
        def _():
            wait_all(copies_of(i - 2, slot, False))

        @pl.when(i < steps)
        def _():
            acc[slot] = t_dot(a_ref[...], dd_ref[...]).astype(BF)
            start_all(copies_of(i, slot, False))

        @pl.when(i == steps)
        def _():
            acc[slot] = t_dot(m_ref[...], da_ref[...]).astype(BF)
            copies = copies_of(i, slot, True)
            start_all(copies)
            wait_all(copies_of(i - 1, (steps - 1) % 2, False))
            wait_all(copies)

    if direct:
        out_shapes = [shaped((ranks, f + r, D), BF)]
    else:
        out_shapes = [shaped((FF, D), BF), shaped((D, D), BF)]
    return call(
        kernel,
        (steps + 1,),
        [
            pl.BlockSpec((t, n), lambda i: (0, jnp.minimum(i, steps - 1))),
            whole((t, D)),
            whole((t, D)),
            whole((t, D)),
        ],
        [ANY] * len(out_shapes),
        out_shapes,
        us=11,
        scratch=[pltpu.VMEM((2, n, D), BF), pltpu.SemaphoreType.DMA((2, 16))],
        after=after,
    )(active, d_down, mixed, d_att)


STRIP = 384
STRIPS = FF // 2 // STRIP


def grad_up(where, nl, d_upper, direct, after=()):
    t = nl.shape[0]

    def kernel(where_ref, nl_ref, du_ref, *refs):
        outs, (acc, sems) = refs[:-2], refs[-2:]
        h = pl.program_id(0)
        acc[h] = t_dot(nl_ref[...], du_ref[...]).astype(BF)

        def copies_of(h):
            if not direct:
                return [pltpu.make_async_copy(acc.at[h], outs[0].at[h], sems.at[h, 0])]
            me, replica = where_ref[0], where_ref[1]
            rows = D // RANKS
            copies = []
            for j in range(RANKS):
                owner_rows = pl.ds(pl.multiple_of((me ^ j) * rows, rows), rows)
                for strip in range(STRIPS):
                    target = outs[j & 1].at[
                        h ^ replica, (j >> 1) & 1, j >> 2, strip * rows : (strip + 1) * rows
                    ]
                    source = acc.at[h, owner_rows, strip * STRIP : (strip + 1) * STRIP]
                    copies.append(pltpu.make_async_copy(source, target, sems.at[h, len(copies)]))
            return copies

        start_all(copies_of(h))

        @pl.when(h == 1)
        def _():
            wait_all(copies_of(0))
            wait_all(copies_of(1))

    if direct:
        out_shapes = [shaped((2, 2, 4, STRIPS * D // RANKS, STRIP), BF)] * 2
    else:
        out_shapes = [shaped((2, D, FF // 2), BF)]
    return call(
        kernel,
        (2,),
        [whole((t, D)), pl.BlockSpec((t, FF // 2), lambda h, *_: (0, h))],
        [ANY] * len(out_shapes),
        out_shapes,
        us=11,
        scratch=[
            pltpu.VMEM((2, D, FF // 2), BF),
            pltpu.SemaphoreType.DMA((2, RANKS * STRIPS)),
        ],
        prefetch=1,
        after=after,
    )(where, nl, d_upper)


def swap(x, mask):
    return lax.ppermute(x, "fsdp", [(i, i ^ mask) for i in range(RANKS)])


def swap_replica(x):
    return lax.ppermute(x, "replica", [(0, 1), (1, 0)])


def added(*terms):
    total = terms[0].astype(F32)
    for term in terms[1:]:
        total = total + term.astype(F32)
    return total


def gather_qkv(where, own):
    rows, half = own.shape
    columns = 2 * half
    z = jnp.stack([own] + [swap(own, m) for m in (4, 8, 12)])
    zy = jnp.stack([z, swap(z, 2)])
    x = swap_replica(zy)
    pieces = (zy, x, swap(zy, 1), swap(x, 1))

    def kernel(where_ref, p0, p1, p2, p3, out_ref, sems):
        me, other = where_ref[0], where_ref[1]
        copies = []
        for index, piece in enumerate((p0, p1, p2, p3)):
            start = pl.multiple_of((other ^ (index % 2)) * half, 128)
            for y in range(2):
                for k in range(4):
                    owner = me ^ (4 * k + 2 * y + index // 2)
                    target = out_ref.at[
                        pl.ds(pl.multiple_of(owner * rows, rows), rows), pl.ds(start, half)
                    ]
                    copies.append(
                        pltpu.make_async_copy(piece.at[y, k], target, sems.at[len(copies)])
                    )
        start_all(copies)
        wait_all(copies)

    return call(
        kernel,
        (1,),
        [ANY] * 4,
        pl.BlockSpec((RANKS * rows, columns), lambda *_: (0, 0)),
        shaped((RANKS * rows, columns), BF),
        us=4,
        scratch=[pltpu.SemaphoreType.DMA((32,))],
        prefetch=1,
    )(where, *pieces)


def ordered(own, other, replica):
    first = jnp.where(replica == 0, own, other)
    second = jnp.where(replica == 0, other, own)
    return first, second


class Chain:
    def __init__(self, keep, send, lines=None, grow=False, two_steps=False):
        self.columns = keep.shape[-1]
        flat = lambda x: x.reshape(-1, self.columns)
        halves = [(swap_replica,)] if keep.ndim == 5 else []
        over = lambda m: lambda x: swap(x, m)
        along_z = [(over(8),), (over(4),)] if two_steps else [(over(4), over(8), over(12))]
        fsdp = [(over(1),)] + halves + [(over(2),)] + along_z
        self.moves = fsdp + [(swap_replica,)]
        self.owner_rows = keep.shape[-2]
        self.stay, self.away = flat(keep), [flat(send)]
        self.lines = None if lines is None else flat(lines)
        self.ride = [False] * len(self.moves)
        if lines is not None:
            self.ride = [not grow] + [True] * (len(fsdp) - 1) + [not halves]
        self.grow = grow

    def send(self):
        moves = self.moves.pop(0)
        self.received = [move(x) for move, x in zip(moves, self.away)]
        self.beside = []
        self.arriving = self.ride.pop(0)
        if self.arriving and len(self.received[0]) == len(self.stay):
            self.beside = [moves[0](self.lines)]


def add_all(chains, after=(), passing=()):
    operands, shapes, plans = [], [], []
    for c in chains:
        n = c.stay.shape[0]
        parts = len(c.moves[0]) + 1 if n > c.owner_rows else 1
        part = n // parts
        lines = c.lines.shape[0] if c.arriving or c.ride[0] else 0
        held = lines if c.arriving else 0
        grown = held * (2 if c.grow else 1)
        rides = (grown or lines) if c.ride[0] else 0
        ins = [c.stay] + c.received + (c.beside + [c.lines] if lines else [])
        outs = [shaped((part, c.columns), BF)]
        sends = parts - 1 if parts > 1 else int(rides > 0)
        outs += [shaped((part + rides, c.columns), BF)] * sends
        if held:
            outs.append(shaped((grown, c.columns), BF))
        plans.append((len(ins), len(outs), n, part, parts, sends, held, rides, len(c.received), len(c.beside), c.grow))
        operands += ins
        shapes += outs

    passed, inputs = len(passing), len(operands)

    def kernel(*refs):
        sources, targets = refs[: len(operands)], refs[len(operands) + passed :]
        for n_in, n_out, n, part, parts, sends, held, rides, arrivals, beside, grow in plans:
            ins, sources = sources[:n_in], sources[n_in:]
            outs, targets = targets[:n_out], targets[n_out:]
            received = ins[1 : 1 + arrivals]
            for p in range(parts):
                rows = slice(p * part, (p + 1) * part)
                total = ins[0][rows, :].astype(F32)
                for r in received:
                    total = total + r[rows, :].astype(F32)
                total = total.astype(BF)
                outs[p][:part, :] = total
                if parts == 1 and sends:
                    outs[1][:part, :] = total
            if held:
                mine = ins[-1][...]
                if beside:
                    others = [ins[1 + arrivals][...]]
                else:
                    others = [r[n : n + held, :] for r in received]
                if grow:
                    lines = jnp.concatenate([mine, others[0]], axis=0)
                else:
                    total = mine.astype(F32)
                    for other in others:
                        total = total + other.astype(F32)
                    lines = total.astype(BF)
                outs[-1][...] = lines
            elif rides:
                lines = ins[-1][...]
            if rides:
                for out in outs[1 : 1 + sends]:
                    out[part:, :] = lines

    results = list(
        call(
            kernel,
            (1,),
            [whole(x.shape) for x in operands] + [ANY] * passed,
            [whole(x.shape) for x in shapes] + [ANY] * passed,
            shapes + [shaped(x.shape, x.dtype) for x in passing],
            us=2,
            after=after,
            aliases={inputs + i: len(shapes) + i for i in range(passed)},
        )(*operands, *passing)
    )
    for c, plan in zip(chains, plans):
        n_out, sends, held = plan[1], plan[5], plan[6]
        mine, results = results[:n_out], results[n_out:]
        c.stay = mine[0]
        c.away = mine[1 : 1 + sends] if sends else [mine[0]]
        if held:
            c.lines = mine[-1]
    return results


SMALL = ("bias_qv", "bias_out", "gain_one", "shift_one", "bias_up", "bias_down", "gain_two", "shift_two")
SMALL_SIZES = (2 * D, D, D, D, FF, D, D, D)
PAD = 256


def body(
    ranks,
    replicas,
    tokens,
    lengths,
    w_qkv,
    bias_qv,
    w_out,
    bias_out,
    gain_one,
    shift_one,
    w_up,
    bias_up,
    w_down,
    bias_down,
    gain_two,
    shift_two,
    cotangent,
):
    direct = ranks == RANKS and replicas == 2
    me = lax.axis_index("fsdp")
    replica = lax.axis_index("replica")
    where = jnp.stack([me, replica]).astype(jnp.int32)
    gather = lambda w: lax.all_gather(w, "fsdp", axis=0, tiled=True)

    small = (bias_qv, bias_out, gain_one, shift_one, bias_up, bias_down, gain_two, shift_two)
    if direct:
        packed, own = pack_weights(where, w_qkv, small, w_out, w_up, w_down)
        w_first = gather_qkv(where, own)
        weights = (gather(packed).reshape(ranks, -1, D),)
    else:
        w_first = gather(w_qkv)
        weights = (gather(w_out), gather(w_up), gather(w_down))
    vectors = {}
    if direct:
        beside = w_first[:, 3 * D :].reshape(ranks, -1, PAD)
    for k, (name, value) in enumerate(zip(SMALL, small)):
        got = beside[:, k, : value.shape[0]].reshape(-1) if direct else gather(value)
        vectors[name] = got.astype(F32)

    bias = vectors["bias_qv"].reshape(2, GROUPS, GW).transpose(1, 0, 2)
    kept = attend_forward(lengths, tokens, w_first, bias)
    mixed = kept[4]
    vec = jnp.stack(
        [
            vectors[n]
            for n in ("bias_out", "gain_one", "shift_one", "bias_down", "gain_two", "shift_two")
        ]
    )
    (layer_out, nl, active, d_down, d_upper, d_first, d_att, sums, sums_up, pooled) = middle(
        lengths, tokens, mixed, weights, vec, vectors["bias_up"][None], cotangent
    )

    terms_down = grad_down_out(active, d_down, mixed, d_att, ranks, direct)
    terms_up = grad_up(where, nl, d_upper, direct, after=(terms_down[0],))
    scatter = lambda x: lax.psum_scatter(x, "fsdp", scatter_dimension=0, tiled=True)

    def small_lines(sums_a, sums_b):
        both = jnp.concatenate([sums_a, sums_b], axis=1)
        return jnp.concatenate([both, sums[3:], sums_up.reshape(-1, D), sums[:3]])

    attend_back = functools.partial(attend_backward, where, d_att, tokens, weights)
    if direct:
        chain_u = Chain(*terms_up, two_steps=True)
        chain_u.send()
        add_all([chain_u])
        shard_down = scatter(terms_down[0].reshape(-1, D))
        shard_other = swap_replica(shard_down)
        chain_u.send()
        dp_a, sums_a, *terms_a = attend_back((0, 1), kept, True, 2, after=(chain_u.away[0],))
        chain_a = Chain(*terms_a, pooled.astype(BF), grow=True, two_steps=True)
        (chain_a.away[0],) = add_all([chain_u], after=(sums_a,), passing=(chain_a.away[0],))
        chain_u.send()
        chain_a.send()
        add_all([chain_a])
        chain_a.send()
        dp_b, sums_b, *terms_b = attend_back((2,), kept, True, 1, after=(chain_a.away[0],))
        small = small_lines(sums_a, sums_b)
        small = jnp.pad(small, ((0, -small.shape[0] % 16), (0, 0))).astype(BF)
        chain_b = Chain(*terms_b, small)
        chain_b.send()
        add_all([chain_u, chain_a], after=(sums_b,))
        chain_u.send()
        chain_a.send()
        input_grad = input_gradient(
            d_first, (dp_a, dp_b), w_first, after=(chain_a.away[0],)
        )
        add_all([chain_u, chain_a, chain_b], after=(input_grad,))
        chain_u.send()
        chain_a.send()
        chain_b.send()
        while chain_u.moves or chain_a.moves or chain_b.moves:
            moving = [c for c in (chain_u, chain_a, chain_b) if c.moves]
            last = all(len(c.moves) == 1 for c in moving)
            add_all(moving, after=(shard_other,) if last else ())
            for c in moving:
                c.send()
        halves_u = ordered(chain_u.stay, chain_u.received[0][: chain_u.owner_rows], replica)
        halves_u = [
            h.reshape(STRIPS, -1, STRIP).transpose(1, 0, 2).reshape(-1, STRIPS * STRIP)
            for h in halves_u
        ]
        both = added(shard_down, shard_other)
        grad_w_down, grad_w_out = both[: FF // ranks], both[FF // ranks :]
        lines = chain_a.lines.reshape((2,) * 4 + pooled.shape)
        relative = jnp.stack([lines, swap(lines, 1)]).transpose(4, 2, 1, 3, 0, 5, 6, 7)
        relative = relative.reshape((2, ranks) + pooled.shape)
        pooled_all = relative[jnp.arange(2) ^ replica][:, me ^ jnp.arange(ranks)]
        pooled_all = pooled_all.reshape((2 * ranks * pooled.shape[0],) + pooled.shape[1:]).astype(F32)
        h0, h1 = ordered(chain_a.stay, chain_a.received[0], replica)
        span = 3 * GW // 2
        halves_a = [
            jnp.concatenate([h[:, i * span : (i + 1) * span] for h in (h0, h1)], axis=1).astype(F32)
            for i in range(2)
        ]
        sum_b = added(chain_b.stay, chain_b.received[0][: chain_b.owner_rows])
        lines = added(chain_b.lines, chain_b.received[0][chain_b.owner_rows :])
        parts = halves_a + [sum_b]
    else:
        dp_a, sums_a, term_a = attend_back((0, 1), kept, False, 1)
        dp_b, sums_b, term_b = attend_back((2,), kept, False, 1)
        input_grad = input_gradient(d_first, (dp_a, dp_b), w_first)
        pooled_all = lax.all_gather(pooled, ("replica", "fsdp"), axis=0, tiled=True)
        reduce = lambda x: lax.psum(scatter(x), "replica").astype(F32)
        grad_w_down, grad_w_out = reduce(terms_down[0]), reduce(terms_down[1])
        halves_u = [reduce(terms_up[0][h]) for h in range(2)]
        sum_a, sum_b = reduce(term_a), reduce(term_b)
        lines = lax.psum(small_lines(sums_a, sums_b), ("replica", "fsdp"))
        parts = [sum_a[:, :D], sum_a[:, D:], sum_b]
    grad_w_up = jnp.concatenate(halves_u, axis=1).astype(F32)
    grad_w_qkv = jnp.concatenate(
        [p[:, i * GW : (i + 1) * GW] for i in range(3) for p in parts], axis=1
    )
    by_owner, start = [], 0
    for size in SMALL_SIZES:
        by_owner.append(lines[start // D : (start + size) // D].reshape(ranks, -1))
        start += size
    mine = lax.dynamic_index_in_dim(jnp.concatenate(by_owner, axis=1), me, keepdims=False)
    small_grads, start = {}, 0
    for name, size in zip(SMALL, SMALL_SIZES):
        small_grads[name] = mine[start : start + size // ranks]
        start += size // ranks
    return (
        layer_out,
        input_grad,
        pooled_all,
        grad_w_qkv,
        small_grads["bias_qv"],
        grad_w_out,
        small_grads["bias_out"],
        small_grads["gain_one"],
        small_grads["shift_one"],
        grad_w_up,
        small_grads["bias_up"],
        grad_w_down,
        small_grads["bias_down"],
        small_grads["gain_two"],
        small_grads["shift_two"],
    )


def solution(mesh):
    rows = P(("replica", "fsdp"), None)
    matrix = P("fsdp", None)
    vector = P("fsdp")
    return jax.shard_map(
        functools.partial(body, mesh.shape["fsdp"], mesh.shape["replica"]),
        mesh=mesh,
        in_specs=(
            rows,
            rows,
            matrix,
            vector,
            matrix,
            vector,
            vector,
            vector,
            matrix,
            vector,
            matrix,
            vector,
            vector,
            vector,
            rows,
        ),
        out_specs=(
            rows,
            rows,
            P(),
            matrix,
            vector,
            matrix,
            vector,
            vector,
            vector,
            matrix,
            vector,
            matrix,
            vector,
            vector,
            vector,
        ),
        check_vma=False,
    )
```
